256 devices in a mesh: xfer: 32 (over x, y, core), head: 8 (over z).
Axes of the slice: x: 4, y: 4, z: 8, core: 2. Of those that a mesh axis runs over, the one named last changes fastest.
Arguments:
- kv_pool: bfloat16 [8192, 64, 576], P(('xfer', 'head')), may hold values from -8 to 8
- lengths: int32 [256], replicated, may hold values from 2 to 15936, as said below
- start_device: int32 [256], replicated, may hold values from 0 to 255, as said below
- page_table: int32 [256, 256], replicated, may hold values from 0 to 31, as said below
- queries: bfloat16 [512, 128, 192], P('xfer', 'head'), may hold values from -100 to 100
- new_latent: bfloat16 [512, 576], P('xfer'), may hold values from -100 to 100
- key_up: bfloat16 [128, 128, 512], P('head'), may hold values from -0.25 to 0.25
- value_up: bfloat16 [128, 512, 128], P('head'), may hold values from -0.25 to 0.25
- out_proj: bfloat16 [16384, 7168], P('head', 'xfer'), may hold values from -0.046875 to 0.046875
Outputs:
- attn_out: bfloat16 [512, 7168], P('head', 'xfer')
The draws below stay inside these ranges and needn't reach their ends.
Inputs may be any that keep to these rules, and one draw needn't show every extreme that they name: `lengths`: request r belongs to decode owner xfer index r // 8. The pages of one owner's requests number 256 // 2 to 256, exactly 256 for some owner, so one owner has at most one page on any device. Page j of request r lies on device (start_device[r] + j) mod 256. `page_table`: entries past a request's pages are 0; two pages on one device never share a slot.
All inputs are finite; a program needn't handle non-finite values.
Results may differ from the reference program's by a relative error of at most 0.0058.
Values may be sent and summed in bfloat16 or wider, within the bound.
A program may use at most 128 MiB of HBM per device.

```python
import jax
import jax.numpy as jnp
from jax import lax

D_MODEL = 7168
HEADS = 128
NOPE = 128
LAT_RANK = 512
VDIM = 128
PAGE = 64
STEPS = 2
R_DEV = 8
QDIM = 192
LAT = 576
REQUESTS = 256
ROWS = 512
MAXP = 256
POOL = 8192
N_XFER = 32
DEVICES = 256


def layout(key):
    key_total = jax.random.fold_in(key, 11)
    key_force = jax.random.fold_in(key, 12)
    key_split = jax.random.fold_in(key, 13)
    key_trim = jax.random.fold_in(key, 14)
    key_base = jax.random.fold_in(key, 15)
    key_shuffle = jax.random.fold_in(key, 16)
    key_longest = jax.random.fold_in(key, 17)
    totals = jax.random.randint(key_total, (N_XFER,), DEVICES // 2, DEVICES + 1)
    forced = jax.random.randint(key_force, (), 0, N_XFER)
    totals = jnp.where(jnp.arange(N_XFER) == forced, DEVICES, totals).astype(jnp.int32)
    positions = jnp.arange(1, DEVICES, dtype=jnp.int32)
    jitter = jax.random.randint(key_split, (N_XFER, DEVICES - 1), 0, 1 << 20)
    ranked = jnp.where(positions[None, :] < totals[:, None], jitter * DEVICES + positions[None, :], -1 - positions[None, :])
    cut_points, _ = lax.top_k(ranked, R_DEV - 1)
    cut_points = jnp.sort(cut_points % DEVICES, axis=1)
    boundary = jnp.concatenate([jnp.zeros((N_XFER, 1), jnp.int32), cut_points, totals[:, None]], axis=1)
    page_counts = boundary[:, 1:] - boundary[:, :-1]
    longest_slot = jax.random.randint(key_longest, (), 0, R_DEV)
    request_slot = jnp.arange(R_DEV, dtype=jnp.int32)
    special = jnp.where(request_slot == longest_slot, DEVICES - R_DEV + 1, 1).astype(jnp.int32)
    owner_rows = jnp.arange(N_XFER, dtype=jnp.int32)
    page_counts = jnp.where(owner_rows[:, None] == forced, special[None, :], page_counts).astype(jnp.int32)
    offsets = jnp.cumsum(page_counts, axis=1) - page_counts
    base_device = jax.random.randint(key_base, (N_XFER, 1), 0, DEVICES)
    start_dev = ((base_device + offsets) % DEVICES).reshape(REQUESTS).astype(jnp.int32)
    flat_counts = page_counts.reshape(REQUESTS)
    trimmed = jax.random.randint(key_trim, (REQUESTS,), 0, PAGE - 1)
    longest_request = forced * R_DEV + longest_slot
    trimmed = jnp.where(jnp.arange(REQUESTS, dtype=jnp.int32) == longest_request, 0, trimmed)
    length_all = (flat_counts * PAGE - trimmed).astype(jnp.int32)
    subkeys = jax.random.split(key_shuffle, DEVICES)
    shuffle = jax.vmap(lambda subkey: jax.random.permutation(subkey, N_XFER))(subkeys).astype(jnp.int32)
    owner_of = jnp.arange(REQUESTS, dtype=jnp.int32) // R_DEV
    column = jnp.arange(MAXP, dtype=jnp.int32)
    device_of = (start_dev[:, None] + column[None, :]) % DEVICES
    page_slots = shuffle[device_of, owner_of[:, None]]
    page_slots = jnp.where(column[None, :] < flat_counts[:, None], page_slots, 0).astype(jnp.int32)
    return (length_all, start_dev, page_slots)


def draw_lengths(key, part):
    return layout(key)[0]


def draw_start_device(key, part):
    return layout(key)[1]


def draw_page_table(key, part):
    return layout(key)[2]


def draw_kv_pool(key, part):
    key_pool = jax.random.fold_in(key, 201)
    pool = jnp.clip(jax.random.normal(key_pool, (POOL, PAGE, LAT), jnp.float32), -6.0, 6.0)
    return pool.astype(jnp.bfloat16)


def drawn(key):
    key_fresh = jax.random.fold_in(key, 101)
    key_query = jax.random.fold_in(key, 102)
    key_pull = jax.random.fold_in(key, 103)
    fresh_rows = jax.random.normal(key_fresh, (ROWS, LAT), jnp.float32)
    base_query = jax.random.normal(key_query, (ROWS, HEADS, QDIM), jnp.float32)
    strengths = jax.random.uniform(key_pull, (ROWS, HEADS), jnp.float32, 0.5, 2.0)
    rope_rows = fresh_rows[:, LAT_RANK:]
    query_rope = base_query[:, :, NOPE:] + strengths[:, :, None] * rope_rows[:, None, :]
    full_query = jnp.concatenate([base_query[:, :, :NOPE], query_rope], axis=-1)
    return (full_query, fresh_rows)


def draw_queries(key, part):
    return drawn(key)[0].astype(jnp.bfloat16)


def draw_new_latent(key, part):
    return drawn(key)[1].astype(jnp.bfloat16)


def block_levels(own_key, shape, shards, smallest, top_value):
    factor_of, own = 1.0, jax.random.fold_in(own_key, 6)
    for position, shards_of in shards:
        draws = jnp.exp(jax.random.uniform(jax.random.fold_in(own, position), (shards_of,), jnp.float32, smallest / len(shards), top_value / len(shards)))
        factor_of = factor_of * jnp.repeat(draws, shape[position] // shards_of).reshape([-1 if axis == position else 1 for axis in range(len(shape))])
    return factor_of


def centred(rng, shape, deviation, bound, cuts=(), held_as=jnp.bfloat16):
    entries = jax.random.normal(rng, shape, jnp.float32) * deviation
    if len(cuts) > 0:
        entries = block_levels(rng, shape, cuts, -0.22, 0.18) * entries
    return jnp.clip(entries, min=-bound, max=bound).astype(held_as)


def setup_inputs(seed: int = 0) -> dict:
    streams_of = jax.random.split(jax.random.key(seed), 10)
    return {
        "kv_pool": draw_kv_pool(jax.random.fold_in(streams_of[9], 71), 0),
        "lengths": draw_lengths(jax.random.fold_in(streams_of[9], 71), 0),
        "start_device": draw_start_device(jax.random.fold_in(streams_of[9], 71), 0),
        "page_table": draw_page_table(jax.random.fold_in(streams_of[9], 71), 0),
        "queries": draw_queries(jax.random.fold_in(streams_of[9], 71), 0),
        "new_latent": draw_new_latent(jax.random.fold_in(streams_of[9], 71), 0),
        "key_up": centred(streams_of[6], (HEADS, NOPE, LAT_RANK), LAT_RANK ** -0.5, 0.25, ((0, 8),)),
        "value_up": centred(streams_of[7], (HEADS, LAT_RANK, VDIM), LAT_RANK ** -0.5, 0.25, ((0, 8),)),
        "out_proj": centred(streams_of[8], (HEADS * VDIM, D_MODEL), (HEADS * VDIM) ** -0.5, 0.046875, ((0, 8), (1, 32))),
    }


def reference(kv_pool, lengths, start_device, page_table, queries, new_latent, key_up, value_up, out_proj):
    score_scale = QDIM ** -0.5
    page_index = jnp.arange(MAXP, dtype=jnp.int32)
    absorbed = jnp.einsum("rhn,hnc->rhc", queries[:, :, :NOPE].astype(jnp.float32), key_up.astype(jnp.float32)).astype(jnp.bfloat16)
    qfull = jnp.concatenate([absorbed, queries[:, :, NOPE:]], axis=-1)
    qfull = qfull.reshape(REQUESTS, STEPS, HEADS, LAT)
    fresh_rows = new_latent.reshape(REQUESTS, STEPS, LAT)
    step_index = jnp.arange(STEPS, dtype=jnp.int32)
    causal = step_index[:, None] >= step_index[None, :]

    def per_request(inputs):
        length, first, slot_row, query_rows, fresh = inputs
        device_of = (first + page_index) % DEVICES
        pool_index = (device_of * N_XFER + slot_row).astype(jnp.int32)
        key_rows = kv_pool[pool_index].reshape(MAXP * PAGE, LAT).astype(jnp.float32)
        visible = jnp.arange(MAXP * PAGE, dtype=jnp.int32) < length
        query_f = query_rows.astype(jnp.float32)
        fresh_f = fresh.astype(jnp.float32)
        cached = jnp.einsum("thc,kc->thk", query_f, key_rows) * score_scale
        cached = jnp.where(visible[None, None, :], cached, -jnp.inf)
        recent = jnp.einsum("thc,kc->thk", query_f, fresh_f) * score_scale
        recent = jnp.where(causal[:, None, :], recent, -jnp.inf)
        row_top = jnp.maximum(jnp.max(cached, axis=-1), jnp.max(recent, axis=-1))
        cached_w = jnp.exp(cached - row_top[..., None])
        recent_w = jnp.exp(recent - row_top[..., None])
        total = jnp.sum(cached_w, axis=-1) + jnp.sum(recent_w, axis=-1)
        summed = jnp.einsum("thk,kc->thc", cached_w.astype(jnp.bfloat16).astype(jnp.float32), key_rows[:, :LAT_RANK])
        summed = summed + jnp.einsum("thk,kc->thc", recent_w.astype(jnp.bfloat16).astype(jnp.float32), fresh_f[:, :LAT_RANK])
        return (summed / total[..., None]).astype(jnp.bfloat16)

    latent_out = lax.map(per_request, (lengths, start_device, page_table, qfull, fresh_rows))
    latent_out = latent_out.reshape(ROWS, HEADS, LAT_RANK)
    head_out = jnp.einsum("rhc,hcv->rhv", latent_out.astype(jnp.float32), value_up.astype(jnp.float32)).astype(jnp.bfloat16)
    head_out = head_out.reshape(ROWS, HEADS * VDIM)
    return jnp.dot(head_out, out_proj, preferred_element_type=jnp.float32).astype(jnp.bfloat16)
```

```python
import functools

import jax
import jax.numpy as jnp
from jax import lax
from jax.experimental import pallas as pl
from jax.experimental.pallas import tpu as pltpu
from jax.sharding import PartitionSpec as P

MESH = pl.DeviceIdType.MESH
STEPS = 2
LOW = -1e30
BLOCK = 256
MIB = 1024 * 1024


def pick_kernel(chosen, pool, out, sems):
    def begin(o, c):
        pltpu.make_async_copy(pool.at[chosen[o]], out.at[o], sems.at[o]).start()
        return c

    def end(o, c):
        pltpu.make_async_copy(pool.at[chosen[o]], out.at[o], sems.at[o]).wait()
        return c

    lax.fori_loop(0, out.shape[0], begin, 0)
    lax.fori_loop(0, out.shape[0], end, 0)


def pick_pages(chosen, pool):
    n = chosen.shape[0]
    return pl.pallas_call(
        pick_kernel,
        grid_spec=pltpu.PrefetchScalarGridSpec(
            num_scalar_prefetch=1,
            grid=(),
            in_specs=[pl.BlockSpec(memory_space=pl.ANY)],
            out_specs=pl.BlockSpec(memory_space=pl.ANY),
            scratch_shapes=[pltpu.SemaphoreType.DMA((n,))],
        ),
        out_shape=jax.ShapeDtypeStruct((n, *pool.shape[1:]), pool.dtype),
    )(chosen, pool)


def attend_kernel(scale, page, lengths, starts, place, q, keys, acc, stats, m_s, l_s):
    member = place[0]
    requests = lengths.shape[0]
    rows = q.shape[1] // requests
    many = q.shape[0] * rows
    latent = q.shape[2]
    rank = acc.shape[2]
    lane = lax.broadcasted_iota(jnp.int32, (1, BLOCK), 1)
    odd = lax.broadcasted_iota(jnp.int32, (many, 128), 1) % 2
    per_block = BLOCK // page
    blocks = keys.shape[0] // BLOCK
    for r in range(requests):
        length, start = lengths[r], starts[r]
        pages = (length + page - 1) // page
        skip = (member - start) & 7
        slot = ((start + skip) & 255) >> 3
        count = jnp.maximum(pages - skip + 7, 0) >> 3
        first = slot // per_block
        n = jnp.minimum((slot % per_block + count + per_block - 1) // per_block, blocks)
        n = jnp.where(count > 0, n, 0)
        part = slice(r * rows, (r + 1) * rows)
        acc[:, part, :] = jnp.zeros((q.shape[0], rows, rank), jnp.float32)
        m_s[...] = jnp.full(m_s.shape, LOW, jnp.float32)
        l_s[...] = jnp.zeros(l_s.shape, jnp.float32)

        def step(i, c):
            b = (first + i) & (blocks - 1)
            k = keys[pl.ds(pl.multiple_of(b * BLOCK, BLOCK), BLOCK), :]
            mine = q[:, part, :].reshape(many, latent)
            s = (
                lax.dot_general(
                    mine, k, (((1,), (1,)), ((), ())), preferred_element_type=jnp.float32
                )
                * scale
            )
            at = ((b * per_block + lane // page) * 8 + member - start) & 255
            s = jnp.where(at * page + lane % page < length, s, LOW)
            m_old = m_s[:, :1]
            m_new = jnp.maximum(m_old, jnp.max(s, axis=1, keepdims=True))
            keep = jnp.exp(m_old - m_new)
            w = jnp.exp(s - m_new)
            l_s[...] = l_s[...] * keep + jnp.sum(w, axis=1, keepdims=True)
            m_s[...] = jnp.broadcast_to(m_new, m_s.shape)
            more = jnp.dot(
                w.astype(jnp.bfloat16), k[:, :rank], preferred_element_type=jnp.float32
            )
            old = acc[:, part, :].reshape(many, rank)
            acc[:, part, :] = (old * keep + more).reshape(q.shape[0], rows, rank)
            return c

        lax.fori_loop(0, n, step, 0)
        both = jnp.where(odd == 0, m_s[...], l_s[...])
        stats[:, part, :] = both.reshape(q.shape[0], rows, 128)


def attend(lengths, starts, place, q, keys, page, rank, scale):
    smem = pl.BlockSpec(memory_space=pltpu.SMEM)
    vmem = pl.BlockSpec(memory_space=pltpu.VMEM)
    many = q.shape[0] * q.shape[1] // lengths.shape[0]
    return pl.pallas_call(
        functools.partial(attend_kernel, scale, page),
        in_specs=[smem, smem, smem, vmem, vmem],
        out_specs=[vmem, vmem],
        out_shape=[
            jax.ShapeDtypeStruct((*q.shape[:2], rank), jnp.float32),
            jax.ShapeDtypeStruct((*q.shape[:2], 128), jnp.float32),
        ],
        scratch_shapes=[pltpu.VMEM((many, 128), jnp.float32)] * 2,
        compiler_params=pltpu.CompilerParams(vmem_limit_bytes=40 * MIB),
    )(lengths, starts, place, q, keys)


def combine(m_a, l_a, acc_a, m_b, l_b, acc_b):
    m = jnp.maximum(m_a, m_b)
    f_a, f_b = jnp.exp(m_a - m), jnp.exp(m_b - m)
    return m, l_a * f_a + l_b * f_b, acc_a * f_a + acc_b * f_b


def finish_kernel(
    scale, acc, stats, q_own, fresh, value_up, out_proj, out,
    sent, sent_st, got, got_st, own, own_st, held, share, parts, z_send, z_recv, x_send, x_recv, o_send, o_recv,
):
    z = lax.axis_index("head")
    xfer = lax.axis_index("xfer")
    x, y, core = xfer // 8, (xfer // 2) % 4, xfer % 2
    groups = 8
    rank = acc.shape[2]
    half_rows = acc.shape[1]

    def near(dx, dy, flip):
        c = 1 - core if flip else core
        return ((lax.rem(x + dx, 4) * 4 + lax.rem(y + dy, 4)) * 2 + c, z)

    def along(k):
        return (xfer, lax.rem(z + k, groups))

    barrier = pltpu.get_barrier_semaphore()
    peers = [along(k) for k in range(1, 8)]
    peers += [near(k, 0, False) for k in range(1, 4)] + [near(0, k, False) for k in range(1, 4)]
    peers += [near(0, 0, True)]
    for peer in peers:
        pl.semaphore_signal(barrier, inc=1, device_id=peer, device_id_type=MESH)
    pl.semaphore_wait(barrier, len(peers))

    def z_copies(way, half, hop):
        to = along(1 if way == 0 else 7)
        return [
            pltpu.make_async_remote_copy(
                src_ref=src.at[way, half, hop],
                dst_ref=dst.at[way, half, hop],
                send_sem=z_send.at[way, half, hop, i],
                recv_sem=z_recv.at[way, half, hop, i],
                device_id=to,
                device_id_type=MESH,
            )
            for i, (src, dst) in enumerate(((sent, got), (sent_st, got_st)))
        ]

    def index_of(way, half, distance):
        d = lax.rem(z + distance if way == 0 else z + groups - distance, groups)
        return d * 2 + half

    odd = lax.broadcasted_iota(jnp.int32, (half_rows, 128), 1) % 2

    def arrived(way, half, hop):
        for c in z_copies(way, half, hop):
            c.wait_recv()
        st = jnp.tile(got_st[way, half, hop], (half_rows // 8, 1)).T
        return st[:, 0:1], st[:, 1:2], got[way, half, hop].astype(jnp.float32)

    started = []

    def send_on(way, half, hop):
        at = index_of(way, half, 4 - hop)
        mine = stats[at]
        if hop == (0 if way == half else 1):
            sent[way, half, hop] = acc[at].astype(jnp.bfloat16)
            sent_st[way, half, hop] = mine.T[0:8]
        else:
            m, l, total = combine(*arrived(way, half, hop - 1), mine[:, 0:1], mine[:, 1:2], acc[at])
            sent[way, half, hop] = total.astype(jnp.bfloat16)
            sent_st[way, half, hop] = jnp.where(odd == 0, m, l).T[0:8]
        for c in z_copies(way, half, hop):
            c.start()
            started.append(c)

    def take_fresh(half):
        rows = slice(half * half_rows, (half + 1) * half_rows)
        s = (
            lax.dot_general(
                q_own[rows, :], fresh[...], (((1,), (1,)), ((), ())), preferred_element_type=jnp.float32
            )
            * scale
        )
        row = lax.broadcasted_iota(jnp.int32, s.shape, 0) // 8
        col = lax.broadcasted_iota(jnp.int32, s.shape, 1)
        s = jnp.where((row // STEPS == col // STEPS) & (col <= row), s, LOW)
        m = jnp.max(s, axis=1, keepdims=True)
        w = jnp.exp(s - m)
        l = jnp.sum(w, axis=1, keepdims=True)
        more = jnp.dot(w.astype(jnp.bfloat16), fresh[:, :rank], preferred_element_type=jnp.float32)
        at = z * 2 + half
        mine = stats[at]
        m, l, total = combine(m, l, more, mine[:, 0:1], mine[:, 1:2], acc[at])
        own[half] = total
        own_st[half] = jnp.where(odd == 0, m, l)

    send_on(0, 0, 0)
    send_on(1, 1, 0)
    send_on(0, 1, 1)
    send_on(1, 0, 1)
    take_fresh(0)
    take_fresh(1)
    for hop in (1, 2, 3):
        send_on(0, 0, hop)
        send_on(1, 1, hop)
        if hop < 3:
            send_on(0, 1, hop + 1)
            send_on(1, 0, hop + 1)

    def spread(half, kind, a, b, block, to):
        return pltpu.make_async_remote_copy(
            src_ref=held.at[half, block],
            dst_ref=held.at[half, block],
            send_sem=x_send.at[half, kind, a, b],
            recv_sem=x_recv.at[half, kind, a, b],
            device_id=to,
            device_id_type=MESH,
        )

    def block_of(half, a, b):
        dx, dy = (a, b) if half == 0 else (b, a)
        return (lax.rem(x + 4 - dx, 4) * 4 + lax.rem(y + 4 - dy, 4)) * 2

    def to_first(half, k):
        return near(k, 0, False) if half == 0 else near(0, k, False)

    def to_second(half, k):
        return near(0, k, False) if half == 0 else near(k, 0, False)

    def start(copy):
        copy.start()
        started.append(copy)

    def pass_second(half, a):
        for k in range(1, 4):
            start(spread(half, 1, a, k, block_of(half, a, 0) + core, to_second(half, k)))

    def pass_core(half, a, b):
        start(spread(half, 2, a, b, block_of(half, a, b) + core, near(0, 0, True)))

    for half in (1, 0):
        m, l, total = own_st[half][:, 0:1], own_st[half][:, 1:2], own[half]
        for way in (0, 1):
            m, l, total = combine(m, l, total, *arrived(way, half, 3))
        latent = (total / l).astype(jnp.bfloat16)
        heads = half_rows // fresh.shape[0]
        for h in range(heads):
            full = jnp.dot(latent, value_up[half * heads + h], preferred_element_type=jnp.float32)
            picked = full.reshape(fresh.shape[0], heads, -1)[:, h, :]
            width = picked.shape[1]
            held[half, xfer, :, h * width : (h + 1) * width] = picked.astype(jnp.bfloat16)
        for k in range(1, 4):
            start(spread(half, 0, 0, k, xfer, to_first(half, k)))
        pass_second(half, 0)
        pass_core(half, 0, 0)
    for a in range(1, 4):
        for half in (1, 0):
            spread(half, 0, 0, a, xfer, near(0, 0, True)).wait_recv()
            pass_second(half, a)
            pass_core(half, a, 0)
    for a in range(4):
        for b in range(1, 4):
            for half in (1, 0):
                spread(half, 1, a, b, xfer, near(0, 0, True)).wait_recv()
                pass_core(half, a, b)
    for half in (1, 0):
        for a in range(4):
            for b in range(4):
                spread(half, 2, a, b, xfer, near(0, 0, True)).wait_recv()

    rows = out.shape[0]
    depth = held.shape[3]
    total = None
    for half in (0, 1):
        left = held[half].reshape(-1, depth)
        right = out_proj[half * depth : (half + 1) * depth, :]
        piece = jnp.dot(left, right, preferred_element_type=jnp.float32)
        total = piece if total is None else total + piece
    parts[...] = total.reshape(parts.shape)

    def final(k):
        return pltpu.make_async_remote_copy(
            src_ref=share.at[0, k],
            dst_ref=share.at[1, k],
            send_sem=o_send.at[k],
            recv_sem=o_recv.at[k],
            device_id=along(k),
            device_id_type=MESH,
        )

    for k in (4, 3, 5, 2, 6, 1, 7):
        share[0, k] = parts[lax.rem(z + k, groups)].astype(jnp.bfloat16)
        start(final(k))
    done = parts[z]
    for k in (1, 7, 2, 6, 3, 5, 4):
        final(k).wait_recv()
        done += share[1, k].astype(jnp.float32)
    out[...] = done.astype(jnp.bfloat16)
    for c in started:
        c.wait_send()


def finish(acc, stats, q_own, fresh, value_up, out_proj, owners, groups, scale):
    vmem = pl.BlockSpec(memory_space=pltpu.VMEM)
    rows = fresh.shape[0]
    half_rows, rank = acc.shape[1:]
    depth, width = out_proj.shape
    piece = owners * rows // groups
    dma = pltpu.SemaphoreType.DMA
    return pl.pallas_call(
        functools.partial(finish_kernel, scale),
        in_specs=[vmem] * 6,
        out_specs=vmem,
        out_shape=jax.ShapeDtypeStruct((piece, width), jnp.bfloat16),
        scratch_shapes=[
            pltpu.VMEM((2, 2, 4, half_rows, rank), jnp.bfloat16),
            pltpu.VMEM((2, 2, 4, 8, 128), jnp.float32),
            pltpu.VMEM((2, 2, 4, half_rows, rank), jnp.bfloat16),
            pltpu.VMEM((2, 2, 4, 8, 128), jnp.float32),
            pltpu.VMEM((2, half_rows, rank), jnp.float32),
            pltpu.VMEM((2, half_rows, 128), jnp.float32),
            pltpu.VMEM((2, owners, rows, depth // 2), jnp.bfloat16),
            pltpu.VMEM((2, groups, piece, width), jnp.bfloat16),
            pltpu.VMEM((groups, piece, width), jnp.float32),
            dma((2, 2, 4, 2)),
            dma((2, 2, 4, 2)),
            dma((2, 3, 4, 4)),
            dma((2, 3, 4, 4)),
            dma((groups,)),
            dma((groups,)),
        ],
        compiler_params=pltpu.CompilerParams(
            collective_id=1, has_side_effects=True, vmem_limit_bytes=48 * MIB
        ),
    )(acc, stats, q_own, fresh, value_up, out_proj)


def body(
    kv_pool, lengths, start_device, page_table, queries, new_latent, key_up, value_up, out_proj
):
    owners = lax.axis_size("xfer")
    groups = lax.axis_size("head")
    devices = owners * groups
    owner_idx = lax.axis_index("xfer")
    member = lax.axis_index("head")
    local_device = owner_idx * groups + member
    page_len = kv_pool.shape[1]
    latent = kv_pool.shape[2]
    lat_rank = value_up.shape[1]
    nope = key_up.shape[1]
    per_owner = lengths.shape[0] // owners
    table_width = page_table.shape[1]
    row_count, heads = queries.shape[:2]
    score_scale = queries.shape[2] ** (-0.5)
    page_counts = (lengths + page_len - 1) // page_len
    column = jnp.arange(table_width, dtype=jnp.int32)
    located = ((start_device[:, None] + column[None, :]) % devices == local_device) & (
        column[None, :] < page_counts[:, None]
    )
    chosen = (
        jnp.sum(jnp.where(located, page_table, 0), axis=1).reshape(owners, per_owner).sum(axis=1)
    )
    outgoing = pick_pages(chosen, kv_pool)
    arrived = lax.all_to_all(outgoing, "xfer", split_axis=0, concat_axis=0, tiled=True)
    first_req = owner_idx * per_owner
    my_lengths = lax.dynamic_slice_in_dim(lengths, first_req, per_owner, 0)
    my_starts = lax.dynamic_slice_in_dim(start_device, first_req, per_owner, 0)
    absorbed = jnp.einsum(
        "rhn,hnc->rhc", queries[:, :, :nope], key_up, preferred_element_type=jnp.float32
    ).astype(jnp.bfloat16)
    qfull = jnp.concatenate([absorbed, queries[:, :, nope:]], axis=-1)
    qfull = qfull.reshape(row_count, 2, heads // 2, latent).transpose(1, 0, 2, 3)
    q_own = qfull.reshape(row_count * heads, latent)
    every = lax.all_gather(q_own, "head", axis=0, tiled=True)
    every = every.reshape(groups * 2, row_count * heads // 2, latent)
    acc, stats = attend(
        my_lengths, my_starts, member.reshape(1), every, arrived.reshape(-1, latent),
        page_len, lat_rank, score_scale,
    )
    return finish(acc, stats, q_own, new_latent, value_up, out_proj, owners, groups, score_scale)


def solution(mesh):
    in_specs = (
        P(("xfer", "head"), None, None),
        P(),
        P(),
        P(),
        P("xfer", "head", None),
        P("xfer", None),
        P("head", None, None),
        P("head", None, None),
        P("head", "xfer"),
    )
    out_specs = P("head", "xfer")
    return jax.shard_map(body, mesh=mesh, in_specs=in_specs, out_specs=out_specs, check_vma=False)
```

```python
import functools

import jax
import jax.numpy as jnp
from jax import lax
from jax.experimental import pallas as pl
from jax.experimental.pallas import tpu as pltpu
from jax.sharding import PartitionSpec as P

MESH = pl.DeviceIdType.MESH
STEPS = 2
LOW = -1e30
BLOCK = 256
MIB = 1024 * 1024


def pick_kernel(chosen, pool, out, sems):
    def begin(o, c):
        pltpu.make_async_copy(pool.at[chosen[o]], out.at[o], sems.at[o]).start()
        return c

    def end(o, c):
        pltpu.make_async_copy(pool.at[chosen[o]], out.at[o], sems.at[o]).wait()
        return c

    lax.fori_loop(0, out.shape[0], begin, 0)
    lax.fori_loop(0, out.shape[0], end, 0)


def pick_pages(chosen, pool):
    n = chosen.shape[0]
    return pl.pallas_call(
        pick_kernel,
        grid_spec=pltpu.PrefetchScalarGridSpec(
            num_scalar_prefetch=1,
            grid=(),
            in_specs=[pl.BlockSpec(memory_space=pl.ANY)],
            out_specs=pl.BlockSpec(memory_space=pltpu.VMEM),
            scratch_shapes=[pltpu.SemaphoreType.DMA((n,))],
        ),
        out_shape=jax.ShapeDtypeStruct((n, *pool.shape[1:]), pool.dtype),
        compiler_params=pltpu.CompilerParams(vmem_limit_bytes=16 * MIB),
    )(chosen, pool)


def attend_kernel(scale, page, lengths, starts, place, q, keys, acc, stats, m_s, l_s):
    member = place[0]
    requests = lengths.shape[0]
    rows = q.shape[1] // requests
    many = q.shape[0] * rows
    latent = q.shape[2]
    rank = acc.shape[2]
    lane = lax.broadcasted_iota(jnp.int32, (1, BLOCK), 1)
    odd = lax.broadcasted_iota(jnp.int32, (many, 128), 1) % 2
    per_block = BLOCK // page
    blocks = keys.shape[0] // BLOCK
    for r in range(requests):
        length, start = lengths[r], starts[r]
        pages = (length + page - 1) // page
        skip = (member - start) & 7
        slot = ((start + skip) & 255) >> 3
        count = jnp.maximum(pages - skip + 7, 0) >> 3
        first = slot // per_block
        n = jnp.minimum((slot % per_block + count + per_block - 1) // per_block, blocks)
        n = jnp.where(count > 0, n, 0)
        part = slice(r * rows, (r + 1) * rows)
        acc[:, part, :] = jnp.zeros((q.shape[0], rows, rank), jnp.float32)
        m_s[...] = jnp.full(m_s.shape, LOW, jnp.float32)
        l_s[...] = jnp.zeros(l_s.shape, jnp.float32)

        def step(i, c):
            b = (first + i) & (blocks - 1)
            k = keys[pl.ds(pl.multiple_of(b * BLOCK, BLOCK), BLOCK), :]
            mine = q[:, part, :].reshape(many, latent)
            s = (
                lax.dot_general(
                    mine, k, (((1,), (1,)), ((), ())), preferred_element_type=jnp.float32
                )
                * scale
            )
            at = ((b * per_block + lane // page) * 8 + member - start) & 255
            s = jnp.where(at * page + lane % page < length, s, LOW)
            m_old = m_s[:, :1]
            m_new = jnp.maximum(m_old, jnp.max(s, axis=1, keepdims=True))
            keep = jnp.exp(m_old - m_new)
            w = jnp.exp(s - m_new)
            l_s[...] = l_s[...] * keep + jnp.sum(w, axis=1, keepdims=True)
            m_s[...] = jnp.broadcast_to(m_new, m_s.shape)
            more = jnp.dot(
                w.astype(jnp.bfloat16), k[:, :rank], preferred_element_type=jnp.float32
            )
            old = acc[:, part, :].reshape(many, rank)
            acc[:, part, :] = (old * keep + more).reshape(q.shape[0], rows, rank)
            return c

        lax.fori_loop(0, n, step, 0)
        both = jnp.where(odd == 0, m_s[...], l_s[...])
        stats[:, part, :] = both.reshape(q.shape[0], rows, 128)


def attend(lengths, starts, place, q, keys, page, rank, scale):
    smem = pl.BlockSpec(memory_space=pltpu.SMEM)
    vmem = pl.BlockSpec(memory_space=pltpu.VMEM)
    many = q.shape[0] * q.shape[1] // lengths.shape[0]
    return pl.pallas_call(
        functools.partial(attend_kernel, scale, page),
        in_specs=[smem, smem, smem, vmem, vmem],
        out_specs=[vmem, vmem],
        out_shape=[
            jax.ShapeDtypeStruct((*q.shape[:2], rank), jnp.float32),
            jax.ShapeDtypeStruct((*q.shape[:2], 128), jnp.float32),
        ],
        scratch_shapes=[pltpu.VMEM((many, 128), jnp.float32)] * 2,
        compiler_params=pltpu.CompilerParams(vmem_limit_bytes=40 * MIB),
    )(lengths, starts, place, q, keys)


def combine(m_a, l_a, acc_a, m_b, l_b, acc_b):
    m = jnp.maximum(m_a, m_b)
    f_a, f_b = jnp.exp(m_a - m), jnp.exp(m_b - m)
    return m, l_a * f_a + l_b * f_b, acc_a * f_a + acc_b * f_b


def finish_kernel(
    scale, acc, stats, q_own, fresh, value_up, out_proj, out,
    sent, sent_st, got, got_st, own, own_st, held, share, parts, z_send, z_recv, x_send, x_recv, o_send, o_recv,
):
    z = lax.axis_index("head")
    xfer = lax.axis_index("xfer")
    x, y, core = xfer // 8, (xfer // 2) % 4, xfer % 2
    groups = 8
    rank = acc.shape[2]
    half_rows = acc.shape[1]

    def near(dx, dy, flip):
        c = 1 - core if flip else core
        return ((lax.rem(x + dx, 4) * 4 + lax.rem(y + dy, 4)) * 2 + c, z)

    def along(k):
        return (xfer, lax.rem(z + k, groups))

    barrier = pltpu.get_barrier_semaphore()
    peers = [along(k) for k in range(1, 8)]
    peers += [near(k, 0, False) for k in range(1, 4)] + [near(0, k, False) for k in range(1, 4)]
    peers += [near(0, 0, True)]
    for peer in peers:
        pl.semaphore_signal(barrier, inc=1, device_id=peer, device_id_type=MESH)
    pl.semaphore_wait(barrier, len(peers))

    def z_copies(way, half, hop):
        to = along(1 if way == 0 else 7)
        return [
            pltpu.make_async_remote_copy(
                src_ref=src.at[way, half, hop],
                dst_ref=dst.at[way, half, hop],
                send_sem=z_send.at[way, half, hop, i],
                recv_sem=z_recv.at[way, half, hop, i],
                device_id=to,
                device_id_type=MESH,
            )
            for i, (src, dst) in enumerate(((sent, got), (sent_st, got_st)))
        ]

    def index_of(way, half, distance):
        d = lax.rem(z + distance if way == 0 else z + groups - distance, groups)
        return d * 2 + half

    odd = lax.broadcasted_iota(jnp.int32, (half_rows, 128), 1) % 2

    def arrived(way, half, hop):
        for c in z_copies(way, half, hop):
            c.wait_recv()
        st = jnp.tile(got_st[way, half, hop], (half_rows // 8, 1)).T
        return st[:, 0:1], st[:, 1:2], got[way, half, hop].astype(jnp.float32)

    started = []

    def send_on(way, half, hop):
        at = index_of(way, half, 4 - hop)
        mine = stats[at]
        if hop == (0 if way == half else 1):
            sent[way, half, hop] = acc[at].astype(jnp.bfloat16)
            sent_st[way, half, hop] = mine.T[0:8]
        else:
            m, l, total = combine(*arrived(way, half, hop - 1), mine[:, 0:1], mine[:, 1:2], acc[at])
            sent[way, half, hop] = total.astype(jnp.bfloat16)
            sent_st[way, half, hop] = jnp.where(odd == 0, m, l).T[0:8]
        for c in z_copies(way, half, hop):
            c.start()
            started.append(c)

    def take_fresh(half):
        rows = slice(half * half_rows, (half + 1) * half_rows)
        s = (
            lax.dot_general(
                q_own[rows, :], fresh[...], (((1,), (1,)), ((), ())), preferred_element_type=jnp.float32
            )
            * scale
        )
        row = lax.broadcasted_iota(jnp.int32, s.shape, 0) // 8
        col = lax.broadcasted_iota(jnp.int32, s.shape, 1)
        s = jnp.where((row // STEPS == col // STEPS) & (col <= row), s, LOW)
        m = jnp.max(s, axis=1, keepdims=True)
        w = jnp.exp(s - m)
        l = jnp.sum(w, axis=1, keepdims=True)
        more = jnp.dot(w.astype(jnp.bfloat16), fresh[:, :rank], preferred_element_type=jnp.float32)
        at = z * 2 + half
        mine = stats[at]
        m, l, total = combine(m, l, more, mine[:, 0:1], mine[:, 1:2], acc[at])
        own[half] = total
        own_st[half] = jnp.where(odd == 0, m, l)

    send_on(0, 0, 0)
    send_on(1, 1, 0)
    send_on(0, 1, 1)
    send_on(1, 0, 1)
    take_fresh(0)
    take_fresh(1)
    for hop in (1, 2, 3):
        send_on(0, 0, hop)
        send_on(1, 1, hop)
        if hop < 3:
            send_on(0, 1, hop + 1)
            send_on(1, 0, hop + 1)

    def spread(half, kind, a, b, block, to):
        return pltpu.make_async_remote_copy(
            src_ref=held.at[half, block],
            dst_ref=held.at[half, block],
            send_sem=x_send.at[half, kind, a, b],
            recv_sem=x_recv.at[half, kind, a, b],
            device_id=to,
            device_id_type=MESH,
        )

    def block_of(half, a, b):
        dx, dy = (a, b) if half == 0 else (b, a)
        return (lax.rem(x + 4 - dx, 4) * 4 + lax.rem(y + 4 - dy, 4)) * 2

    def to_first(half, k):
        return near(k, 0, False) if half == 0 else near(0, k, False)

    def to_second(half, k):
        return near(0, k, False) if half == 0 else near(k, 0, False)

    def start(copy):
        copy.start()
        started.append(copy)

    def pass_second(half, a):
        for k in range(1, 4):
            start(spread(half, 1, a, k, block_of(half, a, 0) + core, to_second(half, k)))

    def pass_core(half, a, b):
        start(spread(half, 2, a, b, block_of(half, a, b) + core, near(0, 0, True)))

    for half in (1, 0):
        m, l, total = own_st[half][:, 0:1], own_st[half][:, 1:2], own[half]
        for way in (0, 1):
            m, l, total = combine(m, l, total, *arrived(way, half, 3))
        latent = (total / l).astype(jnp.bfloat16)
        heads = half_rows // fresh.shape[0]
        for h in range(heads):
            full = jnp.dot(latent, value_up[half * heads + h], preferred_element_type=jnp.float32)
            picked = full.reshape(fresh.shape[0], heads, -1)[:, h, :]
            width = picked.shape[1]
            held[half, xfer, :, h * width : (h + 1) * width] = picked.astype(jnp.bfloat16)
        for k in range(1, 4):
            start(spread(half, 0, 0, k, xfer, to_first(half, k)))
        pass_second(half, 0)
        pass_core(half, 0, 0)
    for a in range(1, 4):
        for half in (1, 0):
            spread(half, 0, 0, a, xfer, near(0, 0, True)).wait_recv()
            pass_second(half, a)
            pass_core(half, a, 0)
    for a in range(4):
        for b in range(1, 4):
            for half in (1, 0):
                spread(half, 1, a, b, xfer, near(0, 0, True)).wait_recv()
                pass_core(half, a, b)
    for half in (1, 0):
        for a in range(4):
            for b in range(4):
                spread(half, 2, a, b, xfer, near(0, 0, True)).wait_recv()

    rows = out.shape[0]
    depth = held.shape[3]
    total = None
    for half in (0, 1):
        left = held[half].reshape(-1, depth)
        right = out_proj[half * depth : (half + 1) * depth, :]
        piece = jnp.dot(left, right, preferred_element_type=jnp.float32)
        total = piece if total is None else total + piece
    parts[...] = total.reshape(parts.shape)

    def final(k):
        return pltpu.make_async_remote_copy(
            src_ref=share.at[0, k],
            dst_ref=share.at[1, k],
            send_sem=o_send.at[k],
            recv_sem=o_recv.at[k],
            device_id=along(k),
            device_id_type=MESH,
        )

    for k in (4, 3, 5, 2, 6, 1, 7):
        share[0, k] = parts[lax.rem(z + k, groups)].astype(jnp.bfloat16)
        start(final(k))
    done = parts[z]
    for k in (1, 7, 2, 6, 3, 5, 4):
        final(k).wait_recv()
        done += share[1, k].astype(jnp.float32)
    out[...] = done.astype(jnp.bfloat16)
    for c in started:
        c.wait_send()


def finish(acc, stats, q_own, fresh, value_up, out_proj, owners, groups, scale):
    vmem = pl.BlockSpec(memory_space=pltpu.VMEM)
    rows = fresh.shape[0]
    half_rows, rank = acc.shape[1:]
    depth, width = out_proj.shape
    piece = owners * rows // groups
    dma = pltpu.SemaphoreType.DMA
    return pl.pallas_call(
        functools.partial(finish_kernel, scale),
        in_specs=[vmem] * 6,
        out_specs=vmem,
        out_shape=jax.ShapeDtypeStruct((piece, width), jnp.bfloat16),
        scratch_shapes=[
            pltpu.VMEM((2, 2, 4, half_rows, rank), jnp.bfloat16),
            pltpu.VMEM((2, 2, 4, 8, 128), jnp.float32),
            pltpu.VMEM((2, 2, 4, half_rows, rank), jnp.bfloat16),
            pltpu.VMEM((2, 2, 4, 8, 128), jnp.float32),
            pltpu.VMEM((2, half_rows, rank), jnp.float32),
            pltpu.VMEM((2, half_rows, 128), jnp.float32),
            pltpu.VMEM((2, owners, rows, depth // 2), jnp.bfloat16),
            pltpu.VMEM((2, groups, piece, width), jnp.bfloat16),
            pltpu.VMEM((groups, piece, width), jnp.float32),
            dma((2, 2, 4, 2)),
            dma((2, 2, 4, 2)),
            dma((2, 3, 4, 4)),
            dma((2, 3, 4, 4)),
            dma((groups,)),
            dma((groups,)),
        ],
        compiler_params=pltpu.CompilerParams(
            collective_id=1, has_side_effects=True, vmem_limit_bytes=48 * MIB
        ),
    )(acc, stats, q_own, fresh, value_up, out_proj)


def body(
    kv_pool, lengths, start_device, page_table, queries, new_latent, key_up, value_up, out_proj
):
    owners = lax.axis_size("xfer")
    groups = lax.axis_size("head")
    devices = owners * groups
    owner_idx = lax.axis_index("xfer")
    member = lax.axis_index("head")
    local_device = owner_idx * groups + member
    page_len = kv_pool.shape[1]
    latent = kv_pool.shape[2]
    lat_rank = value_up.shape[1]
    nope = key_up.shape[1]
    per_owner = lengths.shape[0] // owners
    table_width = page_table.shape[1]
    row_count, heads = queries.shape[:2]
    score_scale = queries.shape[2] ** (-0.5)
    page_counts = (lengths + page_len - 1) // page_len
    column = jnp.arange(table_width, dtype=jnp.int32)
    located = ((start_device[:, None] + column[None, :]) % devices == local_device) & (
        column[None, :] < page_counts[:, None]
    )
    chosen = (
        jnp.sum(jnp.where(located, page_table, 0), axis=1).reshape(owners, per_owner).sum(axis=1)
    )
    outgoing = pick_pages(chosen, kv_pool)
    arrived = lax.all_to_all(outgoing, "xfer", split_axis=0, concat_axis=0, tiled=True)
    first_req = owner_idx * per_owner
    my_lengths = lax.dynamic_slice_in_dim(lengths, first_req, per_owner, 0)
    my_starts = lax.dynamic_slice_in_dim(start_device, first_req, per_owner, 0)
    absorbed = jnp.einsum(
        "rhn,hnc->rhc", queries[:, :, :nope], key_up, preferred_element_type=jnp.float32
    ).astype(jnp.bfloat16)
    qfull = jnp.concatenate([absorbed, queries[:, :, nope:]], axis=-1)
    qfull = qfull.reshape(row_count, 2, heads // 2, latent).transpose(1, 0, 2, 3)
    q_own = qfull.reshape(row_count * heads, latent)
    every = lax.all_gather(q_own, "head", axis=0, tiled=True)
    every = every.reshape(groups * 2, row_count * heads // 2, latent)
    acc, stats = attend(
        my_lengths, my_starts, member.reshape(1), every, arrived.reshape(-1, latent),
        page_len, lat_rank, score_scale,
    )
    return finish(acc, stats, q_own, new_latent, value_up, out_proj, owners, groups, score_scale)


def solution(mesh):
    in_specs = (
        P(("xfer", "head"), None, None),
        P(),
        P(),
        P(),
        P("xfer", "head", None),
        P("xfer", None),
        P("head", None, None),
        P("head", None, None),
        P("head", "xfer"),
    )
    out_specs = P("head", "xfer")
    return jax.shard_map(body, mesh=mesh, in_specs=in_specs, out_specs=out_specs, check_vma=False)
```

```python
import functools

import jax
import jax.numpy as jnp
from jax import lax
from jax.experimental import pallas as pl
from jax.experimental.pallas import tpu as pltpu
from jax.sharding import PartitionSpec as P

MESH = pl.DeviceIdType.MESH
STEPS = 2
LOW = -1e30
BLOCK = 256
MIB = 1024 * 1024


FAR = ((2, 2), (2, 1), (1, 2), (2, 3), (3, 2), (2, 0), (0, 2), (1, 1), (3, 3), (1, 3), (3, 1), (1, 0), (3, 0), (0, 1), (0, 3))
OFFSETS = tuple((*d, 0) for d in FAR) + tuple((*d, 1) for d in FAR) + ((0, 0, 1),)


def prepare_kernel(chosen, pool, queries, key_up, pages, q_own, sems, nope_s, wide_s):
    def copy(o):
        return pltpu.make_async_copy(pool.at[chosen[o]], pages.at[o], sems.at[o])

    def begin(o, c):
        copy(o).start()
        return c

    def end(o, c):
        copy(o).wait()
        return c

    lax.fori_loop(0, pages.shape[0], begin, 0)
    rows, heads, width = queries.shape
    nope, rank = key_up.shape[1:]
    half = heads // 2
    flat = queries[...].reshape(rows * heads, width).astype(jnp.float32)
    nope_s[...] = flat[:, :nope]
    rope = flat[:, nope:].reshape(rows, 2, half, width - nope)
    for h in range(heads):
        mine = nope_s[pl.ds(h, rows, stride=heads), :].astype(jnp.bfloat16)
        full = jnp.dot(mine, key_up[h], preferred_element_type=jnp.float32)
        at = pl.ds((h // half) * rows * half + h % half, rows, stride=half)
        for c in range(rank // 128):
            wide_s[c, at, :] = full[:, c * 128 : (c + 1) * 128]
    for c in range(rank // 128):
        q_own[:, c * 128 : (c + 1) * 128] = wide_s[c].astype(jnp.bfloat16)
    for i in range(2):
        part = rope[:, i].reshape(rows * half, width - nope)
        q_own[i * rows * half : (i + 1) * rows * half, rank:] = part.astype(jnp.bfloat16)
    lax.fori_loop(0, pages.shape[0], end, 0)


def prepare(chosen, pool, queries, key_up):
    n = chosen.shape[0]
    rows, heads, width = queries.shape
    nope, rank = key_up.shape[1:]
    vmem = pl.BlockSpec(memory_space=pltpu.VMEM)
    return pl.pallas_call(
        prepare_kernel,
        in_specs=[pl.BlockSpec(memory_space=pltpu.SMEM), pl.BlockSpec(memory_space=pl.ANY), vmem, vmem],
        out_specs=[vmem, vmem],
        out_shape=[
            jax.ShapeDtypeStruct((n, *pool.shape[1:]), pool.dtype),
            jax.ShapeDtypeStruct((rows * heads, rank + width - nope), queries.dtype),
        ],
        scratch_shapes=[
            pltpu.SemaphoreType.DMA((n,)),
            pltpu.VMEM((rows * heads, nope), jnp.float32),
            pltpu.VMEM((rank // 128, rows * heads, 128), jnp.float32),
        ],
        compiler_params=pltpu.CompilerParams(vmem_limit_bytes=56 * MIB),
    )(chosen, pool, queries, key_up)


def exchange_kernel(pages, q_own, keys, q_all, p_send, p_recv, z_send, z_recv, own_sem):
    z = lax.axis_index("head")
    xfer = lax.axis_index("xfer")
    x, y, core = xfer // 8, (xfer // 2) % 4, xfer % 2
    groups = q_all.shape[0]

    def at(offset):
        dx, dy, dc = offset
        return (lax.rem(x + dx, 4) * 4 + lax.rem(y + dy, 4)) * 2 + lax.rem(core + dc, 2)

    right, left = (xfer, lax.rem(z + 1, groups)), (xfer, lax.rem(z + groups - 1, groups))
    barrier = pltpu.get_barrier_semaphore()
    peers = [right, left] + [(at(offset), z) for offset in OFFSETS]
    for peer in peers:
        pl.semaphore_signal(barrier, inc=1, device_id=peer, device_id_type=MESH)
    pl.semaphore_wait(barrier, len(peers))

    def hop(way, j):
        block = lax.rem(z + groups - (j - 1), groups) if way == 0 else lax.rem(z + j - 1, groups)
        src, dst = (q_own if j == 1 else q_all.at[block]), q_all.at[block]
        if j == groups // 2:
            src, dst = src.at[way], dst.at[way]
        return pltpu.make_async_remote_copy(
            src_ref=src,
            dst_ref=dst,
            send_sem=z_send.at[way, j],
            recv_sem=z_recv.at[way, j],
            device_id=right if way == 0 else left,
            device_id_type=MESH,
        )

    def page(i, offset):
        to = at(offset)
        return pltpu.make_async_remote_copy(
            src_ref=pages.at[to],
            dst_ref=keys.at[xfer],
            send_sem=p_send.at[i],
            recv_sem=p_recv.at[i],
            device_id=(to, z),
            device_id_type=MESH,
        )

    mine = [
        pltpu.make_async_copy(q_own, q_all.at[z], own_sem.at[0]),
        pltpu.make_async_copy(pages.at[xfer], keys.at[xfer], own_sem.at[1]),
    ]
    hops = [hop(way, j) for j in range(1, groups // 2 + 1) for way in (0, 1)]
    copies = [page(i, offset) for i, offset in enumerate(OFFSETS)]
    for c in hops[:2] + copies + mine:
        c.start()
    for j in range(1, groups // 2):
        for way in (0, 1):
            hops[(j - 1) * 2 + way].wait_recv()
            hops[j * 2 + way].start()
    for c in hops[-2:]:
        c.wait_recv()
    for c in copies:
        c.wait_recv()
    for c in mine:
        c.wait()
    for c in hops + copies:
        c.wait_send()


def exchange(pages, q_own, groups):
    vmem = pl.BlockSpec(memory_space=pltpu.VMEM)
    dma = pltpu.SemaphoreType.DMA
    n = pages.shape[0]
    return pl.pallas_call(
        exchange_kernel,
        in_specs=[vmem, vmem],
        out_specs=[vmem, vmem],
        out_shape=[
            jax.ShapeDtypeStruct(pages.shape, pages.dtype),
            jax.ShapeDtypeStruct((groups, *q_own.shape), q_own.dtype),
        ],
        scratch_shapes=[dma((n,)), dma((n,)), dma((2, 8)), dma((2, 8)), dma((2,))],
        compiler_params=pltpu.CompilerParams(
            collective_id=0, has_side_effects=True, vmem_limit_bytes=40 * MIB
        ),
    )(pages, q_own)


def attend_kernel(scale, page, lengths, starts, place, q, keys, acc, stats, m_s, l_s):
    member = place[0]
    requests = lengths.shape[0]
    rows = q.shape[1] // requests
    many = q.shape[0] * rows
    latent = q.shape[2]
    rank = acc.shape[2]
    lane = lax.broadcasted_iota(jnp.int32, (1, BLOCK), 1)
    odd = lax.broadcasted_iota(jnp.int32, (many, 128), 1) % 2
    per_block = BLOCK // page
    blocks = keys.shape[0] // BLOCK
    for r in range(requests):
        length, start = lengths[r], starts[r]
        pages = (length + page - 1) // page
        skip = (member - start) & 7
        slot = ((start + skip) & 255) >> 3
        count = jnp.maximum(pages - skip + 7, 0) >> 3
        first = slot // per_block
        n = jnp.minimum((slot % per_block + count + per_block - 1) // per_block, blocks)
        n = jnp.where(count > 0, n, 0)
        part = slice(r * rows, (r + 1) * rows)
        acc[:, part, :] = jnp.zeros((q.shape[0], rows, rank), jnp.float32)
        m_s[...] = jnp.full(m_s.shape, LOW, jnp.float32)
        l_s[...] = jnp.zeros(l_s.shape, jnp.float32)

        def step(i, c):
            b = (first + i) & (blocks - 1)
            k = keys[pl.ds(pl.multiple_of(b * BLOCK, BLOCK), BLOCK), :]
            mine = q[:, part, :].reshape(many, latent)
            s = (
                lax.dot_general(
                    mine, k, (((1,), (1,)), ((), ())), preferred_element_type=jnp.float32
                )
                * scale
            )
            at = ((b * per_block + lane // page) * 8 + member - start) & 255
            s = jnp.where(at * page + lane % page < length, s, LOW)
            m_old = m_s[:, :1]
            m_new = jnp.maximum(m_old, jnp.max(s, axis=1, keepdims=True))
            keep = jnp.exp(m_old - m_new)
            w = jnp.exp(s - m_new)
            l_s[...] = l_s[...] * keep + jnp.sum(w, axis=1, keepdims=True)
            m_s[...] = jnp.broadcast_to(m_new, m_s.shape)
            more = jnp.dot(
                w.astype(jnp.bfloat16), k[:, :rank], preferred_element_type=jnp.float32
            )
            old = acc[:, part, :].reshape(many, rank)
            acc[:, part, :] = (old * keep + more).reshape(q.shape[0], rows, rank)
            return c

        lax.fori_loop(0, n, step, 0)
        both = jnp.where(odd == 0, m_s[...], l_s[...])
        stats[:, part, :] = both.reshape(q.shape[0], rows, 128)


def attend(lengths, starts, place, q, keys, page, rank, scale):
    smem = pl.BlockSpec(memory_space=pltpu.SMEM)
    vmem = pl.BlockSpec(memory_space=pltpu.VMEM)
    many = q.shape[0] * q.shape[1] // lengths.shape[0]
    return pl.pallas_call(
        functools.partial(attend_kernel, scale, page),
        in_specs=[smem, smem, smem, vmem, vmem],
        out_specs=[vmem, vmem],
        out_shape=[
            jax.ShapeDtypeStruct((*q.shape[:2], rank), jnp.float32),
            jax.ShapeDtypeStruct((*q.shape[:2], 128), jnp.float32),
        ],
        scratch_shapes=[pltpu.VMEM((many, 128), jnp.float32)] * 2,
        compiler_params=pltpu.CompilerParams(vmem_limit_bytes=40 * MIB),
    )(lengths, starts, place, q, keys)


def combine(m_a, l_a, acc_a, m_b, l_b, acc_b):
    m = jnp.maximum(m_a, m_b)
    f_a, f_b = jnp.exp(m_a - m), jnp.exp(m_b - m)
    return m, l_a * f_a + l_b * f_b, acc_a * f_a + acc_b * f_b


def finish_kernel(
    scale, acc, stats, q_own, fresh, value_up, out_proj, out,
    sent, sent_st, got, got_st, own, own_st, held, share, parts, z_send, z_recv, x_send, x_recv, o_send, o_recv,
):
    z = lax.axis_index("head")
    xfer = lax.axis_index("xfer")
    x, y, core = xfer // 8, (xfer // 2) % 4, xfer % 2
    groups = 8
    rank = acc.shape[2]
    half_rows = acc.shape[1]

    def near(dx, dy, flip):
        c = 1 - core if flip else core
        return ((lax.rem(x + dx, 4) * 4 + lax.rem(y + dy, 4)) * 2 + c, z)

    def along(k):
        return (xfer, lax.rem(z + k, groups))

    barrier = pltpu.get_barrier_semaphore()
    peers = [along(k) for k in range(1, 8)]
    peers += [near(k, 0, False) for k in range(1, 4)] + [near(0, k, False) for k in range(1, 4)]
    peers += [near(0, 0, True)]
    for peer in peers:
        pl.semaphore_signal(barrier, inc=1, device_id=peer, device_id_type=MESH)
    pl.semaphore_wait(barrier, len(peers))

    def z_copies(way, half, hop):
        to = along(1 if way == 0 else 7)
        return [
            pltpu.make_async_remote_copy(
                src_ref=src.at[way, half, hop],
                dst_ref=dst.at[way, half, hop],
                send_sem=z_send.at[way, half, hop, i],
                recv_sem=z_recv.at[way, half, hop, i],
                device_id=to,
                device_id_type=MESH,
            )
            for i, (src, dst) in enumerate(((sent, got), (sent_st, got_st)))
        ]

    def index_of(way, half, distance):
        d = lax.rem(z + distance if way == 0 else z + groups - distance, groups)
        return d * 2 + half

    odd = lax.broadcasted_iota(jnp.int32, (half_rows, 128), 1) % 2

    def arrived(way, half, hop):
        for c in z_copies(way, half, hop):
            c.wait_recv()
        st = jnp.tile(got_st[way, half, hop], (half_rows // 8, 1)).T
        return st[:, 0:1], st[:, 1:2], got[way, half, hop].astype(jnp.float32)

    started = []

    def send_on(way, half, hop):
        at = index_of(way, half, 4 - hop)
        mine = stats[at]
        if hop == (0 if way == half else 1):
            sent[way, half, hop] = acc[at].astype(jnp.bfloat16)
            sent_st[way, half, hop] = mine.T[0:8]
        else:
            m, l, total = combine(*arrived(way, half, hop - 1), mine[:, 0:1], mine[:, 1:2], acc[at])
            sent[way, half, hop] = total.astype(jnp.bfloat16)
            sent_st[way, half, hop] = jnp.where(odd == 0, m, l).T[0:8]
        for c in z_copies(way, half, hop):
            c.start()
            started.append(c)

    def take_fresh(half):
        rows = slice(half * half_rows, (half + 1) * half_rows)
        s = (
            lax.dot_general(
                q_own[rows, :], fresh[...], (((1,), (1,)), ((), ())), preferred_element_type=jnp.float32
            )
            * scale
        )
        row = lax.broadcasted_iota(jnp.int32, s.shape, 0) // 8
        col = lax.broadcasted_iota(jnp.int32, s.shape, 1)
        s = jnp.where((row // STEPS == col // STEPS) & (col <= row), s, LOW)
        m = jnp.max(s, axis=1, keepdims=True)
        w = jnp.exp(s - m)
        l = jnp.sum(w, axis=1, keepdims=True)
        more = jnp.dot(w.astype(jnp.bfloat16), fresh[:, :rank], preferred_element_type=jnp.float32)
        at = z * 2 + half
        mine = stats[at]
        m, l, total = combine(m, l, more, mine[:, 0:1], mine[:, 1:2], acc[at])
        own[half] = total
        own_st[half] = jnp.where(odd == 0, m, l)

    send_on(0, 0, 0)
    send_on(1, 1, 0)
    send_on(0, 1, 1)
    send_on(1, 0, 1)
    take_fresh(0)
    take_fresh(1)
    for hop in (1, 2, 3):
        send_on(0, 0, hop)
        send_on(1, 1, hop)
        if hop < 3:
            send_on(0, 1, hop + 1)
            send_on(1, 0, hop + 1)

    def spread(half, kind, a, b, block, to):
        return pltpu.make_async_remote_copy(
            src_ref=held.at[half, block],
            dst_ref=held.at[half, block],
            send_sem=x_send.at[half, kind, a, b],
            recv_sem=x_recv.at[half, kind, a, b],
            device_id=to,
            device_id_type=MESH,
        )

    def block_of(half, a, b):
        dx, dy = (a, b) if half == 0 else (b, a)
        return (lax.rem(x + 4 - dx, 4) * 4 + lax.rem(y + 4 - dy, 4)) * 2

    def to_first(half, k):
        return near(k, 0, False) if half == 0 else near(0, k, False)

    def to_second(half, k):
        return near(0, k, False) if half == 0 else near(k, 0, False)

    def start(copy):
        copy.start()
        started.append(copy)

    def pass_second(half, a):
        for k in range(1, 4):
            start(spread(half, 1, a, k, block_of(half, a, 0) + core, to_second(half, k)))

    def pass_core(half, a, b):
        start(spread(half, 2, a, b, block_of(half, a, b) + core, near(0, 0, True)))

    for half in (1, 0):
        m, l, total = own_st[half][:, 0:1], own_st[half][:, 1:2], own[half]
        for way in (0, 1):
            m, l, total = combine(m, l, total, *arrived(way, half, 3))
        latent = (total / l).astype(jnp.bfloat16)
        heads = half_rows // fresh.shape[0]
        for h in range(heads):
            full = jnp.dot(latent, value_up[half * heads + h], preferred_element_type=jnp.float32)
            picked = full.reshape(fresh.shape[0], heads, -1)[:, h, :]
            width = picked.shape[1]
            held[half, xfer, :, h * width : (h + 1) * width] = picked.astype(jnp.bfloat16)
        for k in range(1, 4):
            start(spread(half, 0, 0, k, xfer, to_first(half, k)))
        pass_second(half, 0)
        pass_core(half, 0, 0)
    for a in range(1, 4):
        for half in (1, 0):
            spread(half, 0, 0, a, xfer, near(0, 0, True)).wait_recv()
            pass_second(half, a)
            pass_core(half, a, 0)
    for a in range(4):
        for b in range(1, 4):
            for half in (1, 0):
                spread(half, 1, a, b, xfer, near(0, 0, True)).wait_recv()
                pass_core(half, a, b)
    for half in (1, 0):
        for a in range(4):
            for b in range(4):
                spread(half, 2, a, b, xfer, near(0, 0, True)).wait_recv()

    rows = out.shape[0]
    depth = held.shape[3]
    total = None
    for half in (0, 1):
        left = held[half].reshape(-1, depth)
        right = out_proj[half * depth : (half + 1) * depth, :]
        piece = jnp.dot(left, right, preferred_element_type=jnp.float32)
        total = piece if total is None else total + piece
    parts[...] = total.reshape(parts.shape)

    def final(k):
        return pltpu.make_async_remote_copy(
            src_ref=share.at[0, k],
            dst_ref=share.at[1, k],
            send_sem=o_send.at[k],
            recv_sem=o_recv.at[k],
            device_id=along(k),
            device_id_type=MESH,
        )

    for k in (4, 3, 5, 2, 6, 1, 7):
        share[0, k] = parts[lax.rem(z + k, groups)].astype(jnp.bfloat16)
        start(final(k))
    done = parts[z]
    for k in (1, 7, 2, 6, 3, 5, 4):
        final(k).wait_recv()
        done += share[1, k].astype(jnp.float32)
    out[...] = done.astype(jnp.bfloat16)
    for c in started:
        c.wait_send()


def finish(acc, stats, q_own, fresh, value_up, out_proj, owners, groups, scale):
    vmem = pl.BlockSpec(memory_space=pltpu.VMEM)
    rows = fresh.shape[0]
    half_rows, rank = acc.shape[1:]
    depth, width = out_proj.shape
    piece = owners * rows // groups
    dma = pltpu.SemaphoreType.DMA
    return pl.pallas_call(
        functools.partial(finish_kernel, scale),
        in_specs=[vmem] * 6,
        out_specs=vmem,
        out_shape=jax.ShapeDtypeStruct((piece, width), jnp.bfloat16),
        scratch_shapes=[
            pltpu.VMEM((2, 2, 4, half_rows, rank), jnp.bfloat16),
            pltpu.VMEM((2, 2, 4, 8, 128), jnp.float32),
            pltpu.VMEM((2, 2, 4, half_rows, rank), jnp.bfloat16),
            pltpu.VMEM((2, 2, 4, 8, 128), jnp.float32),
            pltpu.VMEM((2, half_rows, rank), jnp.float32),
            pltpu.VMEM((2, half_rows, 128), jnp.float32),
            pltpu.VMEM((2, owners, rows, depth // 2), jnp.bfloat16),
            pltpu.VMEM((2, groups, piece, width), jnp.bfloat16),
            pltpu.VMEM((groups, piece, width), jnp.float32),
            dma((2, 2, 4, 2)),
            dma((2, 2, 4, 2)),
            dma((2, 3, 4, 4)),
            dma((2, 3, 4, 4)),
            dma((groups,)),
            dma((groups,)),
        ],
        compiler_params=pltpu.CompilerParams(
            collective_id=1, has_side_effects=True, vmem_limit_bytes=48 * MIB
        ),
    )(acc, stats, q_own, fresh, value_up, out_proj)


def body(
    kv_pool, lengths, start_device, page_table, queries, new_latent, key_up, value_up, out_proj
):
    owners = lax.axis_size("xfer")
    groups = lax.axis_size("head")
    devices = owners * groups
    owner_idx = lax.axis_index("xfer")
    member = lax.axis_index("head")
    local_device = owner_idx * groups + member
    page_len = kv_pool.shape[1]
    latent = kv_pool.shape[2]
    lat_rank = value_up.shape[1]
    per_owner = lengths.shape[0] // owners
    table_width = page_table.shape[1]
    row_count, heads = queries.shape[:2]
    score_scale = queries.shape[2] ** (-0.5)
    page_counts = (lengths + page_len - 1) // page_len
    column = jnp.arange(table_width, dtype=jnp.int32)
    located = ((start_device[:, None] + column[None, :]) % devices == local_device) & (
        column[None, :] < page_counts[:, None]
    )
    chosen = (
        jnp.sum(jnp.where(located, page_table, 0), axis=1).reshape(owners, per_owner).sum(axis=1)
    )
    first_req = owner_idx * per_owner
    my_lengths = lax.dynamic_slice_in_dim(lengths, first_req, per_owner, 0)
    my_starts = lax.dynamic_slice_in_dim(start_device, first_req, per_owner, 0)
    pages, q_own = prepare(chosen, kv_pool, queries, key_up)
    arrived, every = exchange(pages, q_own.reshape(2, row_count * heads // 2, latent), groups)
    every = every.reshape(groups * 2, row_count * heads // 2, latent)
    acc, stats = attend(
        my_lengths, my_starts, member.reshape(1), every, arrived.reshape(-1, latent),
        page_len, lat_rank, score_scale,
    )
    return finish(acc, stats, q_own, new_latent, value_up, out_proj, owners, groups, score_scale)


def solution(mesh):
    in_specs = (
        P(("xfer", "head"), None, None),
        P(),
        P(),
        P(),
        P("xfer", "head", None),
        P("xfer", None),
        P("head", None, None),
        P("head", None, None),
        P("head", "xfer"),
    )
    out_specs = P("head", "xfer")
    return jax.shard_map(body, mesh=mesh, in_specs=in_specs, out_specs=out_specs, check_vma=False)
```

```python
import functools

import jax
import jax.numpy as jnp
from jax import lax
from jax.experimental import pallas as pl
from jax.experimental.pallas import tpu as pltpu
from jax.sharding import PartitionSpec as P

MESH = pl.DeviceIdType.MESH
STEPS = 2
LOW = -1e30
BLOCK = 256
MIB = 1024 * 1024


FAR = ((2, 2), (2, 1), (1, 2), (2, 3), (3, 2), (2, 0), (0, 2), (1, 1), (3, 3), (1, 3), (3, 1), (1, 0), (3, 0), (0, 1), (0, 3))
OFFSETS = tuple((*d, 0) for d in FAR) + tuple((*d, 1) for d in FAR) + ((0, 0, 1),)


def prepare_kernel(chosen, pool, queries, key_up, pages, q_own, sems, nope_s, wide_s):
    def copy(o):
        return pltpu.make_async_copy(pool.at[chosen[o]], pages.at[o], sems.at[o])

    def begin(o, c):
        copy(o).start()
        return c

    def end(o, c):
        copy(o).wait()
        return c

    lax.fori_loop(0, pages.shape[0], begin, 0)
    rows, heads, width = queries.shape
    nope, rank = key_up.shape[1:]
    half = heads // 2
    flat = queries[...].reshape(rows * heads, width).astype(jnp.float32)
    nope_s[...] = flat[:, :nope]
    rope = flat[:, nope:].reshape(rows, 2, half, width - nope)
    for h in range(heads):
        mine = nope_s[pl.ds(h, rows, stride=heads), :].astype(jnp.bfloat16)
        full = jnp.dot(mine, key_up[h], preferred_element_type=jnp.float32)
        at = pl.ds((h // half) * rows * half + h % half, rows, stride=half)
        for c in range(rank // 128):
            wide_s[c, at, :] = full[:, c * 128 : (c + 1) * 128]
    for c in range(rank // 128):
        q_own[:, c * 128 : (c + 1) * 128] = wide_s[c].astype(jnp.bfloat16)
    for i in range(2):
        part = rope[:, i].reshape(rows * half, width - nope)
        q_own[i * rows * half : (i + 1) * rows * half, rank:] = part.astype(jnp.bfloat16)
    lax.fori_loop(0, pages.shape[0], end, 0)


def prepare(chosen, pool, queries, key_up):
    n = chosen.shape[0]
    rows, heads, width = queries.shape
    nope, rank = key_up.shape[1:]
    vmem = pl.BlockSpec(memory_space=pltpu.VMEM)
    return pl.pallas_call(
        prepare_kernel,
        in_specs=[pl.BlockSpec(memory_space=pltpu.SMEM), pl.BlockSpec(memory_space=pl.ANY), vmem, vmem],
        out_specs=[vmem, vmem],
        out_shape=[
            jax.ShapeDtypeStruct((n, *pool.shape[1:]), pool.dtype),
            jax.ShapeDtypeStruct((rows * heads, rank + width - nope), queries.dtype),
        ],
        scratch_shapes=[
            pltpu.SemaphoreType.DMA((n,)),
            pltpu.VMEM((rows * heads, nope), jnp.float32),
            pltpu.VMEM((rank // 128, rows * heads, 128), jnp.float32),
        ],
        compiler_params=pltpu.CompilerParams(vmem_limit_bytes=56 * MIB),
    )(chosen, pool, queries, key_up)


def exchange_kernel(pages, q_own, keys, q_all, q_s, page_s, p_send, p_recv, z_send, z_recv, own_sem):
    z = lax.axis_index("head")
    xfer = lax.axis_index("xfer")
    x, y, core = xfer // 8, (xfer // 2) % 4, xfer % 2
    groups = q_all.shape[0]

    def at(offset):
        dx, dy, dc = offset
        return (lax.rem(x + dx, 4) * 4 + lax.rem(y + dy, 4)) * 2 + lax.rem(core + dc, 2)

    mine = [
        pltpu.make_async_copy(q_own, q_s, own_sem.at[0]),
        pltpu.make_async_copy(pages.at[xfer], page_s, own_sem.at[1]),
    ]
    for c in mine:
        c.start()
    right, left = (xfer, lax.rem(z + 1, groups)), (xfer, lax.rem(z + groups - 1, groups))
    barrier = pltpu.get_barrier_semaphore()
    peers = [right, left] + [(at(offset), z) for offset in OFFSETS]
    for peer in peers:
        pl.semaphore_signal(barrier, inc=1, device_id=peer, device_id_type=MESH)
    pl.semaphore_wait(barrier, len(peers))

    def hop(way, j):
        block = lax.rem(z + groups - (j - 1), groups) if way == 0 else lax.rem(z + j - 1, groups)
        src, dst = (q_s if j == 1 else q_all.at[block]), q_all.at[block]
        if j == groups // 2:
            src, dst = src.at[way], dst.at[way]
        return pltpu.make_async_remote_copy(
            src_ref=src,
            dst_ref=dst,
            send_sem=z_send.at[way, j],
            recv_sem=z_recv.at[way, j],
            device_id=right if way == 0 else left,
            device_id_type=MESH,
        )

    def page(i, offset):
        to = at(offset)
        return pltpu.make_async_remote_copy(
            src_ref=pages.at[to],
            dst_ref=keys.at[xfer],
            send_sem=p_send.at[i],
            recv_sem=p_recv.at[i],
            device_id=(to, z),
            device_id_type=MESH,
        )

    hops = [hop(way, j) for j in range(1, groups // 2 + 1) for way in (0, 1)]
    copies = [page(i, offset) for i, offset in enumerate(OFFSETS)]
    for c in mine:
        c.wait()
    for c in hops[:2] + copies:
        c.start()
    mine = [
        pltpu.make_async_copy(q_s, q_all.at[z], own_sem.at[2]),
        pltpu.make_async_copy(page_s, keys.at[xfer], own_sem.at[3]),
    ]
    for c in mine:
        c.start()
    for j in range(1, groups // 2):
        for way in (0, 1):
            hops[(j - 1) * 2 + way].wait_recv()
            hops[j * 2 + way].start()
    for c in hops[-2:]:
        c.wait_recv()
    for c in copies:
        c.wait_recv()
    for c in mine:
        c.wait()
    for c in hops + copies:
        c.wait_send()


def exchange(pages, q_own, groups):
    hbm = pl.BlockSpec(memory_space=pl.ANY)
    dma = pltpu.SemaphoreType.DMA
    n = pages.shape[0]
    return pl.pallas_call(
        exchange_kernel,
        in_specs=[hbm, hbm],
        out_specs=[hbm, hbm],
        out_shape=[
            jax.ShapeDtypeStruct(pages.shape, pages.dtype),
            jax.ShapeDtypeStruct((groups, *q_own.shape), q_own.dtype),
        ],
        scratch_shapes=[
            pltpu.VMEM(q_own.shape, q_own.dtype),
            pltpu.VMEM(pages.shape[1:], pages.dtype),
            dma((n,)),
            dma((n,)),
            dma((2, 8)),
            dma((2, 8)),
            dma((4,)),
        ],
        compiler_params=pltpu.CompilerParams(
            collective_id=0, has_side_effects=True, vmem_limit_bytes=56 * MIB
        ),
    )(pages, q_own)


def attend_kernel(scale, lengths, starts, place, q, keys, acc, stats, q_s, k_s, acc_s, st_s, m_s, l_s, k_sem, q_sem, o_sem):
    member = place[0]
    requests = lengths.shape[0]
    slots, page, latent = keys.shape
    rows = q.shape[1] // requests
    many = q.shape[0] * rows
    rank = acc.shape[2]
    width = BLOCK // page
    loads = [
        pltpu.make_async_copy(keys, k_s.at[pl.ds(0, slots)], k_sem.at[0]),
        pltpu.make_async_copy(keys.at[pl.ds(0, width)], k_s.at[pl.ds(slots, width)], k_sem.at[1]),
    ]
    q_loads = [
        pltpu.make_async_copy(q.at[:, pl.ds(r * rows, rows)], q_s.at[r], q_sem.at[r]) for r in range(requests)
    ]
    for c in loads + q_loads:
        c.start()
    lane = lax.broadcasted_iota(jnp.int32, (1, BLOCK), 1)
    odd = lax.broadcasted_iota(jnp.int32, (many, 128), 1) % 2
    for c in loads:
        c.wait()
    stores = []
    for r in range(requests):
        length, start = lengths[r], starts[r]
        pages = (length + page - 1) // page
        skip = (member - start) & 7
        slot = ((start + skip) & 255) >> 3
        count = jnp.maximum(pages - skip + 7, 0) >> 3
        q_loads[r].wait()

        def window(i):
            first = (slot + i * width) & (slots - 1)
            k = k_s[pl.ds(first, width)].reshape(BLOCK, latent)
            s = lax.dot_general(
                q_s[r].reshape(many, latent), k, (((1,), (1,)), ((), ())), preferred_element_type=jnp.float32
            )
            nth = i * width + lane // page
            seen = (nth < count) & ((skip + nth * 8) * page + lane % page < length)
            return jnp.where(seen, s * scale, LOW), seen, k[:, :rank]

        def weigh(w, v):
            return jnp.dot(w.astype(jnp.bfloat16), v, preferred_element_type=jnp.float32)

        s, seen, v = window(0)
        m = jnp.max(s, axis=1, keepdims=True)
        w = jnp.where(seen, jnp.exp(s - m), 0.0)
        m_s[...] = jnp.broadcast_to(m, m_s.shape)
        l_s[...] = jnp.broadcast_to(jnp.sum(w, axis=1, keepdims=True), l_s.shape)
        acc_s[r] = weigh(w, v).reshape(acc_s.shape[1:])

        def step(i, c):
            s, _, v = window(i)
            m_old = m_s[:, :1]
            m_new = jnp.maximum(m_old, jnp.max(s, axis=1, keepdims=True))
            keep = jnp.exp(m_old - m_new)
            w = jnp.exp(s - m_new)
            l_s[...] = l_s[...] * keep + jnp.sum(w, axis=1, keepdims=True)
            m_s[...] = jnp.broadcast_to(m_new, m_s.shape)
            old = acc_s[r].reshape(many, rank)
            acc_s[r] = (old * keep + weigh(w, v)).reshape(acc_s.shape[1:])
            return c

        lax.fori_loop(1, (count + width - 1) // width, step, 0)
        st_s[r] = jnp.where(odd == 0, m_s[...], l_s[...]).reshape(st_s.shape[1:])
        part = pl.ds(r * rows, rows)
        stores += [
            pltpu.make_async_copy(acc_s.at[r], acc.at[:, part], o_sem.at[0, r]),
            pltpu.make_async_copy(st_s.at[r], stats.at[:, part], o_sem.at[1, r]),
        ]
        for c in stores[-2:]:
            c.start()
    for c in stores:
        c.wait()


def attend(lengths, starts, place, q, keys, rank, scale):
    smem = pl.BlockSpec(memory_space=pltpu.SMEM)
    hbm = pl.BlockSpec(memory_space=pl.ANY)
    requests = lengths.shape[0]
    chunks, rows = q.shape[0], q.shape[1] // requests
    many = chunks * rows
    slots, page, latent = keys.shape
    dma = pltpu.SemaphoreType.DMA
    return pl.pallas_call(
        functools.partial(attend_kernel, scale),
        in_specs=[smem, smem, smem, hbm, hbm],
        out_specs=[hbm, hbm],
        out_shape=[
            jax.ShapeDtypeStruct((*q.shape[:2], rank), jnp.float32),
            jax.ShapeDtypeStruct((*q.shape[:2], 128), jnp.float32),
        ],
        scratch_shapes=[
            pltpu.VMEM((requests, chunks, rows, latent), q.dtype),
            pltpu.VMEM((slots + BLOCK // page, page, latent), keys.dtype),
            pltpu.VMEM((requests, chunks, rows, rank), jnp.float32),
            pltpu.VMEM((requests, chunks, rows, 128), jnp.float32),
            pltpu.VMEM((many, 128), jnp.float32),
            pltpu.VMEM((many, 128), jnp.float32),
            dma((2,)),
            dma((requests,)),
            dma((2, requests)),
        ],
        compiler_params=pltpu.CompilerParams(vmem_limit_bytes=56 * MIB),
    )(lengths, starts, place, q, keys)


def combine(m_a, l_a, acc_a, m_b, l_b, acc_b):
    m = jnp.maximum(m_a, m_b)
    f_a, f_b = jnp.exp(m_a - m), jnp.exp(m_b - m)
    return m, l_a * f_a + l_b * f_b, acc_a * f_a + acc_b * f_b


def finish_kernel(
    scale, acc_h, stats_h, q_own_h, fresh_h, value_up_h, out_proj_h, out,
    acc, stats, q_own, fresh, value_up, out_proj, acc_sem, in_sem, sent, sent_st, got, got_st, own, own_st, held, share, parts, z_send, z_recv, x_send, x_recv, o_send, o_recv,
):
    z = lax.axis_index("head")
    xfer = lax.axis_index("xfer")
    x, y, core = xfer // 8, (xfer // 2) % 4, xfer % 2
    groups = 8
    rank = acc.shape[2]
    half_rows = acc.shape[1]
    loads = [
        pltpu.make_async_copy(src, dst, in_sem.at[i])
        for i, (src, dst) in enumerate(
            ((stats_h, stats), (q_own_h, q_own), (fresh_h, fresh), (value_up_h, value_up), (out_proj_h, out_proj))
        )
    ]

    def load_acc(at):
        return pltpu.make_async_copy(acc_h.at[at], acc.at[at], acc_sem.at[at])

    loads[0].start()
    for distance in (4, 3, 5, 0, 2, 6, 1, 7):
        for half in (0, 1):
            load_acc(lax.rem(z + distance, groups) * 2 + half).start()
    for c in loads[1:]:
        c.start()

    def near(dx, dy, flip):
        c = 1 - core if flip else core
        return ((lax.rem(x + dx, 4) * 4 + lax.rem(y + dy, 4)) * 2 + c, z)

    def along(k):
        return (xfer, lax.rem(z + k, groups))

    barrier = pltpu.get_barrier_semaphore()
    peers = [along(k) for k in range(1, 8)]
    peers += [near(k, 0, False) for k in range(1, 4)] + [near(0, k, False) for k in range(1, 4)]
    peers += [near(0, 0, True)]
    for peer in peers:
        pl.semaphore_signal(barrier, inc=1, device_id=peer, device_id_type=MESH)
    pl.semaphore_wait(barrier, len(peers))

    def z_copies(way, half, hop):
        to = along(1 if way == 0 else 7)
        return [
            pltpu.make_async_remote_copy(
                src_ref=src.at[way, half, hop],
                dst_ref=dst.at[way, half, hop],
                send_sem=z_send.at[way, half, hop, i],
                recv_sem=z_recv.at[way, half, hop, i],
                device_id=to,
                device_id_type=MESH,
            )
            for i, (src, dst) in enumerate(((sent, got), (sent_st, got_st)))
        ]

    def index_of(way, half, distance):
        d = lax.rem(z + distance if way == 0 else z + groups - distance, groups)
        return d * 2 + half

    odd = lax.broadcasted_iota(jnp.int32, (half_rows, 128), 1) % 2

    def arrived(way, half, hop):
        for c in z_copies(way, half, hop):
            c.wait_recv()
        st = jnp.tile(got_st[way, half, hop], (half_rows // 8, 1)).T
        return st[:, 0:1], st[:, 1:2], got[way, half, hop].astype(jnp.float32)

    started = []

    def send_on(way, half, hop):
        at = index_of(way, half, 4 - hop)
        mine = stats[at]
        load_acc(at).wait()
        if hop == (0 if way == half else 1):
            sent[way, half, hop] = acc[at].astype(jnp.bfloat16)
            sent_st[way, half, hop] = mine.T[0:8]
        else:
            m, l, total = combine(*arrived(way, half, hop - 1), mine[:, 0:1], mine[:, 1:2], acc[at])
            sent[way, half, hop] = total.astype(jnp.bfloat16)
            sent_st[way, half, hop] = jnp.where(odd == 0, m, l).T[0:8]
        for c in z_copies(way, half, hop):
            c.start()
            started.append(c)

    def take_fresh(half):
        rows = slice(half * half_rows, (half + 1) * half_rows)
        s = (
            lax.dot_general(
                q_own[rows, :], fresh[...], (((1,), (1,)), ((), ())), preferred_element_type=jnp.float32
            )
            * scale
        )
        row = lax.broadcasted_iota(jnp.int32, s.shape, 0) // 8
        col = lax.broadcasted_iota(jnp.int32, s.shape, 1)
        s = jnp.where((row // STEPS == col // STEPS) & (col <= row), s, LOW)
        m = jnp.max(s, axis=1, keepdims=True)
        w = jnp.exp(s - m)
        l = jnp.sum(w, axis=1, keepdims=True)
        more = jnp.dot(w.astype(jnp.bfloat16), fresh[:, :rank], preferred_element_type=jnp.float32)
        at = z * 2 + half
        mine = stats[at]
        load_acc(at).wait()
        m, l, total = combine(m, l, more, mine[:, 0:1], mine[:, 1:2], acc[at])
        own[half] = total
        own_st[half] = jnp.where(odd == 0, m, l)

    loads[0].wait()
    send_on(0, 0, 0)
    send_on(1, 1, 0)
    send_on(0, 1, 1)
    send_on(1, 0, 1)
    loads[1].wait()
    loads[2].wait()
    take_fresh(0)
    take_fresh(1)
    for hop in (1, 2, 3):
        send_on(0, 0, hop)
        send_on(1, 1, hop)
        if hop < 3:
            send_on(0, 1, hop + 1)
            send_on(1, 0, hop + 1)

    def spread(half, kind, a, b, block, to):
        return pltpu.make_async_remote_copy(
            src_ref=held.at[half, block],
            dst_ref=held.at[half, block],
            send_sem=x_send.at[half, kind, a, b],
            recv_sem=x_recv.at[half, kind, a, b],
            device_id=to,
            device_id_type=MESH,
        )

    def block_of(half, a, b):
        dx, dy = (a, b) if half == 0 else (b, a)
        return (lax.rem(x + 4 - dx, 4) * 4 + lax.rem(y + 4 - dy, 4)) * 2

    def to_first(half, k):
        return near(k, 0, False) if half == 0 else near(0, k, False)

    def to_second(half, k):
        return near(0, k, False) if half == 0 else near(k, 0, False)

    def start(copy):
        copy.start()
        started.append(copy)

    def pass_second(half, a):
        for k in range(1, 4):
            start(spread(half, 1, a, k, block_of(half, a, 0) + core, to_second(half, k)))

    def pass_core(half, a, b):
        start(spread(half, 2, a, b, block_of(half, a, b) + core, near(0, 0, True)))

    loads[3].wait()
    for half in (1, 0):
        m, l, total = own_st[half][:, 0:1], own_st[half][:, 1:2], own[half]
        for way in (0, 1):
            m, l, total = combine(m, l, total, *arrived(way, half, 3))
        latent = (total / l).astype(jnp.bfloat16)
        heads = half_rows // fresh.shape[0]
        for h in range(heads):
            full = jnp.dot(latent, value_up[half * heads + h], preferred_element_type=jnp.float32)
            picked = full.reshape(fresh.shape[0], heads, -1)[:, h, :]
            width = picked.shape[1]
            held[half, xfer, :, h * width : (h + 1) * width] = picked.astype(jnp.bfloat16)
        for k in range(1, 4):
            start(spread(half, 0, 0, k, xfer, to_first(half, k)))
        pass_second(half, 0)
        pass_core(half, 0, 0)
    for a in range(1, 4):
        for half in (1, 0):
            spread(half, 0, 0, a, xfer, near(0, 0, True)).wait_recv()
            pass_second(half, a)
            pass_core(half, a, 0)
    for a in range(4):
        for b in range(1, 4):
            for half in (1, 0):
                spread(half, 1, a, b, xfer, near(0, 0, True)).wait_recv()
                pass_core(half, a, b)
    for half in (1, 0):
        for a in range(4):
            for b in range(4):
                spread(half, 2, a, b, xfer, near(0, 0, True)).wait_recv()

    loads[4].wait()
    depth = held.shape[3]
    total = None
    for half in (0, 1):
        left = held[half].reshape(-1, depth)
        right = out_proj[:, half * depth : (half + 1) * depth]
        piece = lax.dot_general(left, right, (((1,), (1,)), ((), ())), preferred_element_type=jnp.float32)
        total = piece if total is None else total + piece
    parts[...] = total.reshape(parts.shape)

    def final(k):
        return pltpu.make_async_remote_copy(
            src_ref=share.at[0, k],
            dst_ref=share.at[1, k],
            send_sem=o_send.at[k],
            recv_sem=o_recv.at[k],
            device_id=along(k),
            device_id_type=MESH,
        )

    for k in (4, 3, 5, 2, 6, 1, 7):
        share[0, k] = parts[lax.rem(z + k, groups)].astype(jnp.bfloat16)
        start(final(k))
    done = parts[z]
    for k in (1, 7, 2, 6, 3, 5, 4):
        final(k).wait_recv()
        done += share[1, k].astype(jnp.float32)
    out[...] = done.astype(jnp.bfloat16)
    for c in started:
        c.wait_send()


def finish(acc, stats, q_own, fresh, value_up, out_proj, owners, groups, scale):
    vmem = pl.BlockSpec(memory_space=pltpu.VMEM)
    operands = (acc, stats, q_own, fresh, value_up, out_proj)
    rows = fresh.shape[0]
    half_rows, rank = acc.shape[1:]
    width, depth = out_proj.shape
    piece = owners * rows // groups
    dma = pltpu.SemaphoreType.DMA
    return pl.pallas_call(
        functools.partial(finish_kernel, scale),
        in_specs=[pl.BlockSpec(memory_space=pl.ANY)] * 6,
        out_specs=vmem,
        out_shape=jax.ShapeDtypeStruct((piece, width), jnp.bfloat16),
        scratch_shapes=[
            *(pltpu.VMEM(a.shape, a.dtype) for a in operands),
            dma((2 * groups,)),
            dma((5,)),
            pltpu.VMEM((2, 2, 4, half_rows, rank), jnp.bfloat16),
            pltpu.VMEM((2, 2, 4, 8, 128), jnp.float32),
            pltpu.VMEM((2, 2, 4, half_rows, rank), jnp.bfloat16),
            pltpu.VMEM((2, 2, 4, 8, 128), jnp.float32),
            pltpu.VMEM((2, half_rows, rank), jnp.float32),
            pltpu.VMEM((2, half_rows, 128), jnp.float32),
            pltpu.VMEM((2, owners, rows, depth // 2), jnp.bfloat16),
            pltpu.VMEM((2, groups, piece, width), jnp.bfloat16),
            pltpu.VMEM((groups, piece, width), jnp.float32),
            dma((2, 2, 4, 2)),
            dma((2, 2, 4, 2)),
            dma((2, 3, 4, 4)),
            dma((2, 3, 4, 4)),
            dma((groups,)),
            dma((groups,)),
        ],
        compiler_params=pltpu.CompilerParams(
            collective_id=1, has_side_effects=True, vmem_limit_bytes=56 * MIB
        ),
    )(*operands)


def body(
    kv_pool, lengths, start_device, page_table, queries, new_latent, key_up, value_up, out_proj
):
    owners = lax.axis_size("xfer")
    groups = lax.axis_size("head")
    devices = owners * groups
    owner_idx = lax.axis_index("xfer")
    member = lax.axis_index("head")
    local_device = owner_idx * groups + member
    page_len = kv_pool.shape[1]
    latent = kv_pool.shape[2]
    lat_rank = value_up.shape[1]
    per_owner = lengths.shape[0] // owners
    table_width = page_table.shape[1]
    row_count, heads = queries.shape[:2]
    score_scale = queries.shape[2] ** (-0.5)
    page_counts = (lengths + page_len - 1) // page_len
    column = jnp.arange(table_width, dtype=jnp.int32)
    located = ((start_device[:, None] + column[None, :]) % devices == local_device) & (
        column[None, :] < page_counts[:, None]
    )
    chosen = (
        jnp.sum(jnp.where(located, page_table, 0), axis=1).reshape(owners, per_owner).sum(axis=1)
    )
    first_req = owner_idx * per_owner
    my_lengths = lax.dynamic_slice_in_dim(lengths, first_req, per_owner, 0)
    my_starts = lax.dynamic_slice_in_dim(start_device, first_req, per_owner, 0)
    pages, q_own = prepare(chosen, kv_pool, queries, key_up)
    arrived, every = exchange(pages, q_own.reshape(2, row_count * heads // 2, latent), groups)
    every = every.reshape(groups * 2, row_count * heads // 2, latent)
    acc, stats = attend(
        my_lengths, my_starts, member.reshape(1), every, arrived,
        lat_rank, score_scale,
    )
    return finish(acc, stats, q_own, new_latent, value_up, out_proj.T, owners, groups, score_scale)


def solution(mesh):
    in_specs = (
        P(("xfer", "head"), None, None),
        P(),
        P(),
        P(),
        P("xfer", "head", None),
        P("xfer", None),
        P("head", None, None),
        P("head", None, None),
        P("head", "xfer"),
    )
    out_specs = P("head", "xfer")
    return jax.shard_map(body, mesh=mesh, in_specs=in_specs, out_specs=out_specs, check_vma=False)
```

```python
import functools

import jax
import jax.numpy as jnp
from jax import lax
from jax.experimental import pallas as pl
from jax.experimental.pallas import tpu as pltpu
from jax.sharding import PartitionSpec as P

MESH = pl.DeviceIdType.MESH
STEPS = 2
LOW = -1e30
BLOCK = 256
MIB = 1024 * 1024


FAR = ((2, 2), (2, 1), (1, 2), (2, 3), (3, 2), (2, 0), (0, 2), (1, 1), (3, 3), (1, 3), (3, 1), (1, 0), (3, 0), (0, 1), (0, 3))
OFFSETS = tuple((*d, 0) for d in FAR) + tuple((*d, 1) for d in FAR) + ((0, 0, 1),)


def prepare_kernel(groups, lengths, starts, table, pool, queries, key_up, pages, q_own, sems, nope_s, wide_s):
    me = lax.axis_index("xfer") * groups + lax.axis_index("head")
    per_owner = lengths.shape[0] // pages.shape[0]
    page = pages.shape[1]

    def begin(o, c):
        slot = 0
        for i in range(per_owner):
            r = o * per_owner + i
            j = (me - starts[r]) & (table.shape[1] - 1)
            slot = jnp.where(j * page < lengths[r], table[r, j], slot)
        pltpu.make_async_copy(pool.at[slot], pages.at[o], sems.at[o]).start()
        return c

    def end(o, c):
        pltpu.make_async_copy(pool.at[0], pages.at[o], sems.at[o]).wait()
        return c

    lax.fori_loop(0, pages.shape[0], begin, 0)
    rows, heads, width = queries.shape
    nope, rank = key_up.shape[1:]
    half = heads // 2
    flat = queries[...].reshape(rows * heads, width).astype(jnp.float32)
    nope_s[...] = flat[:, :nope]
    rope = flat[:, nope:].reshape(rows, 2, half, width - nope)
    for h in range(heads):
        mine = nope_s[pl.ds(h, rows, stride=heads), :].astype(jnp.bfloat16)
        full = jnp.dot(mine, key_up[h], preferred_element_type=jnp.float32)
        at = pl.ds((h // half) * rows * half + h % half, rows, stride=half)
        for c in range(rank // 128):
            wide_s[c, at, :] = full[:, c * 128 : (c + 1) * 128]
    for c in range(rank // 128):
        q_own[:, c * 128 : (c + 1) * 128] = wide_s[c].astype(jnp.bfloat16)
    for i in range(2):
        part = rope[:, i].reshape(rows * half, width - nope)
        q_own[i * rows * half : (i + 1) * rows * half, rank:] = part.astype(jnp.bfloat16)
    lax.fori_loop(0, pages.shape[0], end, 0)


def prepare(lengths, starts, table, pool, queries, key_up, n, groups):
    rows, heads, width = queries.shape
    nope, rank = key_up.shape[1:]
    vmem = pl.BlockSpec(memory_space=pltpu.VMEM)
    smem = pl.BlockSpec(memory_space=pltpu.SMEM)
    return pl.pallas_call(
        functools.partial(prepare_kernel, groups),
        in_specs=[smem, smem, smem, pl.BlockSpec(memory_space=pl.ANY), vmem, vmem],
        out_specs=[vmem, vmem],
        out_shape=[
            jax.ShapeDtypeStruct((n, *pool.shape[1:]), pool.dtype),
            jax.ShapeDtypeStruct((rows * heads, rank + width - nope), queries.dtype),
        ],
        scratch_shapes=[
            pltpu.SemaphoreType.DMA((n,)),
            pltpu.VMEM((rows * heads, nope), jnp.float32),
            pltpu.VMEM((rank // 128, rows * heads, 128), jnp.float32),
        ],
        compiler_params=pltpu.CompilerParams(vmem_limit_bytes=56 * MIB),
    )(lengths, starts, table, pool, queries, key_up)


def exchange_kernel(pages, q_own, keys, q_all, q_s, page_s, p_send, p_recv, z_send, z_recv, own_sem):
    z = lax.axis_index("head")
    xfer = lax.axis_index("xfer")
    x, y, core = xfer // 8, (xfer // 2) % 4, xfer % 2
    groups = q_all.shape[0]

    def at(offset):
        dx, dy, dc = offset
        return (lax.rem(x + dx, 4) * 4 + lax.rem(y + dy, 4)) * 2 + lax.rem(core + dc, 2)

    mine = [
        pltpu.make_async_copy(q_own, q_s, own_sem.at[0]),
        pltpu.make_async_copy(pages.at[xfer], page_s, own_sem.at[1]),
    ]
    for c in mine:
        c.start()
    right, left = (xfer, lax.rem(z + 1, groups)), (xfer, lax.rem(z + groups - 1, groups))
    barrier = pltpu.get_barrier_semaphore()
    peers = [right, left] + [(at(offset), z) for offset in OFFSETS]
    for peer in peers:
        pl.semaphore_signal(barrier, inc=1, device_id=peer, device_id_type=MESH)
    pl.semaphore_wait(barrier, len(peers))

    def hop(way, j):
        block = lax.rem(z + groups - (j - 1), groups) if way == 0 else lax.rem(z + j - 1, groups)
        src, dst = (q_s if j == 1 else q_all.at[block]), q_all.at[block]
        if j == groups // 2:
            src, dst = src.at[way], dst.at[way]
        return pltpu.make_async_remote_copy(
            src_ref=src,
            dst_ref=dst,
            send_sem=z_send.at[way, j],
            recv_sem=z_recv.at[way, j],
            device_id=right if way == 0 else left,
            device_id_type=MESH,
        )

    def page(i, offset):
        to = at(offset)
        return pltpu.make_async_remote_copy(
            src_ref=pages.at[to],
            dst_ref=keys.at[xfer],
            send_sem=p_send.at[i],
            recv_sem=p_recv.at[i],
            device_id=(to, z),
            device_id_type=MESH,
        )

    hops = [hop(way, j) for j in range(1, groups // 2 + 1) for way in (0, 1)]
    copies = [page(i, offset) for i, offset in enumerate(OFFSETS)]
    for c in mine:
        c.wait()
    for c in hops[:2] + copies:
        c.start()
    mine = [
        pltpu.make_async_copy(q_s, q_all.at[z], own_sem.at[2]),
        pltpu.make_async_copy(page_s, keys.at[xfer], own_sem.at[3]),
    ]
    for c in mine:
        c.start()
    for j in range(1, groups // 2):
        for way in (0, 1):
            hops[(j - 1) * 2 + way].wait_recv()
            hops[j * 2 + way].start()
    for c in hops[-2:]:
        c.wait_recv()
    for c in copies:
        c.wait_recv()
    for c in mine:
        c.wait()
    for c in hops + copies:
        c.wait_send()


def exchange(pages, q_own, groups):
    hbm = pl.BlockSpec(memory_space=pl.ANY)
    dma = pltpu.SemaphoreType.DMA
    n = pages.shape[0]
    return pl.pallas_call(
        exchange_kernel,
        in_specs=[hbm, hbm],
        out_specs=[hbm, hbm],
        out_shape=[
            jax.ShapeDtypeStruct(pages.shape, pages.dtype),
            jax.ShapeDtypeStruct((groups, *q_own.shape), q_own.dtype),
        ],
        scratch_shapes=[
            pltpu.VMEM(q_own.shape, q_own.dtype),
            pltpu.VMEM(pages.shape[1:], pages.dtype),
            dma((n,)),
            dma((n,)),
            dma((2, 8)),
            dma((2, 8)),
            dma((4,)),
        ],
        compiler_params=pltpu.CompilerParams(
            collective_id=0, has_side_effects=True, vmem_limit_bytes=56 * MIB
        ),
    )(pages, q_own)


def attend_kernel(scale, requests, lengths, starts, q, keys, acc, stats, q_s, k_s, acc_s, st_s, m_s, l_s, k_sem, q_sem, o_sem):
    member = lax.axis_index("head")
    base = lax.axis_index("xfer") * requests
    slots, page, latent = keys.shape
    rows = q.shape[1] // requests
    many = q.shape[0] * rows
    rank = acc.shape[2]
    width = BLOCK // page
    loads = [
        pltpu.make_async_copy(keys, k_s.at[pl.ds(0, slots)], k_sem.at[0]),
        pltpu.make_async_copy(keys.at[pl.ds(0, width)], k_s.at[pl.ds(slots, width)], k_sem.at[1]),
    ]
    q_loads = [
        pltpu.make_async_copy(q.at[:, pl.ds(r * rows, rows)], q_s.at[r], q_sem.at[r]) for r in range(requests)
    ]
    for c in loads + q_loads:
        c.start()
    lane = lax.broadcasted_iota(jnp.int32, (1, BLOCK), 1)
    odd = lax.broadcasted_iota(jnp.int32, (many, 128), 1) % 2
    for c in loads:
        c.wait()
    stores = []
    for r in range(requests):
        length, start = lengths[base + r], starts[base + r]
        pages = (length + page - 1) // page
        skip = (member - start) & 7
        slot = ((start + skip) & 255) >> 3
        count = jnp.maximum(pages - skip + 7, 0) >> 3
        q_loads[r].wait()

        def window(i):
            first = (slot + i * width) & (slots - 1)
            k = k_s[pl.ds(first, width)].reshape(BLOCK, latent)
            s = lax.dot_general(
                q_s[r].reshape(many, latent), k, (((1,), (1,)), ((), ())), preferred_element_type=jnp.float32
            )
            nth = i * width + lane // page
            seen = (nth < count) & ((skip + nth * 8) * page + lane % page < length)
            return jnp.where(seen, s * scale, LOW), seen, k[:, :rank]

        def weigh(w, v):
            return jnp.dot(w.astype(jnp.bfloat16), v, preferred_element_type=jnp.float32)

        s, seen, v = window(0)
        m = jnp.max(s, axis=1, keepdims=True)
        w = jnp.where(seen, jnp.exp(s - m), 0.0)
        m_s[...] = jnp.broadcast_to(m, m_s.shape)
        l_s[...] = jnp.broadcast_to(jnp.sum(w, axis=1, keepdims=True), l_s.shape)
        acc_s[r] = weigh(w, v).reshape(acc_s.shape[1:])

        def step(i, c):
            s, _, v = window(i)
            m_old = m_s[:, :1]
            m_new = jnp.maximum(m_old, jnp.max(s, axis=1, keepdims=True))
            keep = jnp.exp(m_old - m_new)
            w = jnp.exp(s - m_new)
            l_s[...] = l_s[...] * keep + jnp.sum(w, axis=1, keepdims=True)
            m_s[...] = jnp.broadcast_to(m_new, m_s.shape)
            old = acc_s[r].reshape(many, rank)
            acc_s[r] = (old * keep + weigh(w, v)).reshape(acc_s.shape[1:])
            return c

        lax.fori_loop(1, (count + width - 1) // width, step, 0)
        st_s[r] = jnp.where(odd == 0, m_s[...], l_s[...]).reshape(st_s.shape[1:])
        part = pl.ds(r * rows, rows)
        stores += [
            pltpu.make_async_copy(acc_s.at[r], acc.at[:, part], o_sem.at[0, r]),
            pltpu.make_async_copy(st_s.at[r], stats.at[:, part], o_sem.at[1, r]),
        ]
        for c in stores[-2:]:
            c.start()
    for c in stores:
        c.wait()


def attend(lengths, starts, q, keys, requests, rank, scale):
    smem = pl.BlockSpec(memory_space=pltpu.SMEM)
    hbm = pl.BlockSpec(memory_space=pl.ANY)
    chunks, rows = q.shape[0], q.shape[1] // requests
    many = chunks * rows
    slots, page, latent = keys.shape
    dma = pltpu.SemaphoreType.DMA
    return pl.pallas_call(
        functools.partial(attend_kernel, scale, requests),
        in_specs=[smem, smem, hbm, hbm],
        out_specs=[hbm, hbm],
        out_shape=[
            jax.ShapeDtypeStruct((*q.shape[:2], rank), jnp.float32),
            jax.ShapeDtypeStruct((*q.shape[:2], 128), jnp.float32),
        ],
        scratch_shapes=[
            pltpu.VMEM((requests, chunks, rows, latent), q.dtype),
            pltpu.VMEM((slots + BLOCK // page, page, latent), keys.dtype),
            pltpu.VMEM((requests, chunks, rows, rank), jnp.float32),
            pltpu.VMEM((requests, chunks, rows, 128), jnp.float32),
            pltpu.VMEM((many, 128), jnp.float32),
            pltpu.VMEM((many, 128), jnp.float32),
            dma((2,)),
            dma((requests,)),
            dma((2, requests)),
        ],
        compiler_params=pltpu.CompilerParams(vmem_limit_bytes=56 * MIB),
    )(lengths, starts, q, keys)


def combine(m_a, l_a, acc_a, m_b, l_b, acc_b):
    m = jnp.maximum(m_a, m_b)
    f_a, f_b = jnp.exp(m_a - m), jnp.exp(m_b - m)
    return m, l_a * f_a + l_b * f_b, acc_a * f_a + acc_b * f_b


def finish_kernel(
    scale, acc_h, stats_h, q_own_h, fresh_h, value_up_h, out_proj_h, out,
    acc, stats, q_own, fresh, value_up, out_proj, acc_sem, in_sem, sent, sent_st, got, got_st, own, own_st, lat_s, held, share, parts, z_send, z_recv, x_send, x_recv, o_send, o_recv,
):
    z = lax.axis_index("head")
    xfer = lax.axis_index("xfer")
    x, y, core = xfer // 8, (xfer // 2) % 4, xfer % 2
    groups = 8
    rank = acc.shape[2]
    half_rows = acc.shape[1]
    loads = [
        pltpu.make_async_copy(src, dst, in_sem.at[i])
        for i, (src, dst) in enumerate(
            ((stats_h, stats), (q_own_h, q_own), (fresh_h, fresh), (value_up_h, value_up), (out_proj_h, out_proj))
        )
    ]

    def load_acc(at):
        return pltpu.make_async_copy(acc_h.at[at], acc.at[at], acc_sem.at[at])

    loads[0].start()
    for half in (0, 1):
        for i in range(groups):
            load_acc(2 * i + half).start()
    for c in loads[1:]:
        c.start()

    def near(dx, dy, flip):
        c = 1 - core if flip else core
        return ((lax.rem(x + dx, 4) * 4 + lax.rem(y + dy, 4)) * 2 + c, z)

    def along(k):
        return (xfer, lax.rem(z + k, groups))

    barrier = pltpu.get_barrier_semaphore()
    peers = [along(k) for k in range(1, 8)]
    peers += [near(k, 0, False) for k in range(1, 4)] + [near(0, k, False) for k in range(1, 4)]
    peers += [near(0, 0, True)]
    for peer in peers:
        pl.semaphore_signal(barrier, inc=1, device_id=peer, device_id_type=MESH)
    pl.semaphore_wait(barrier, len(peers))

    rows = half_rows // 2

    def z_copies(way, piece, hop):
        to = along(1 if way == 0 else 7)
        return [
            pltpu.make_async_remote_copy(
                src_ref=src.at[way, piece, hop],
                dst_ref=dst.at[way, piece, hop],
                send_sem=z_send.at[way, piece, hop, i],
                recv_sem=z_recv.at[way, piece, hop, i],
                device_id=to,
                device_id_type=MESH,
            )
            for i, (src, dst) in enumerate(((sent, got), (sent_st, got_st)))
        ]

    def index_of(way, piece, distance):
        d = lax.rem(z + distance if way == 0 else z + groups - distance, groups)
        return d * 2 + piece // 2

    def rows_of(piece):
        return slice(piece % 2 * rows, (piece % 2 + 1) * rows)

    odd = lax.broadcasted_iota(jnp.int32, (half_rows, 128), 1) % 2

    def as_rows(st):
        return jnp.concatenate([st, st], axis=0).T[0:8]

    def arrived(way, piece, hop):
        for c in z_copies(way, piece, hop):
            c.wait_recv()
        st = jnp.tile(got_st[way, piece, hop], (half_rows // 8, 1)).T[0:rows]
        return st[:, 0:1], st[:, 1:2], got[way, piece, hop].astype(jnp.float32)

    started = []

    def send_on(way, piece, hop):
        at = index_of(way, piece, 4 - hop)
        part = rows_of(piece)
        mine = stats[at, part]
        if hop == (0 if way == piece % 2 else 1):
            sent[way, piece, hop] = acc[at, part].astype(jnp.bfloat16)
            sent_st[way, piece, hop] = as_rows(mine)
        else:
            m, l, total = combine(*arrived(way, piece, hop - 1), mine[:, 0:1], mine[:, 1:2], acc[at, part])
            sent[way, piece, hop] = total.astype(jnp.bfloat16)
            sent_st[way, piece, hop] = as_rows(jnp.where(odd[0:rows] == 0, m, l))
        for c in z_copies(way, piece, hop):
            c.start()
            started.append(c)

    def take_fresh(half):
        part = slice(half * half_rows, (half + 1) * half_rows)
        s = (
            lax.dot_general(
                q_own[part, :], fresh[...], (((1,), (1,)), ((), ())), preferred_element_type=jnp.float32
            )
            * scale
        )
        row = lax.broadcasted_iota(jnp.int32, s.shape, 0) // 8
        col = lax.broadcasted_iota(jnp.int32, s.shape, 1)
        s = jnp.where((row // STEPS == col // STEPS) & (col <= row), s, LOW)
        m = jnp.max(s, axis=1, keepdims=True)
        w = jnp.exp(s - m)
        l = jnp.sum(w, axis=1, keepdims=True)
        more = jnp.dot(w.astype(jnp.bfloat16), fresh[:, :rank], preferred_element_type=jnp.float32)
        at = z * 2 + half
        mine = stats[at]
        m, l, total = combine(m, l, more, mine[:, 0:1], mine[:, 1:2], acc[at])
        own[half] = total
        own_st[half] = jnp.where(odd == 0, m, l)

    def chain(half, part):
        a, b = 2 * half, 2 * half + 1
        steps = (
            ((0, a, 0), (1, b, 0), (0, b, 1), (1, a, 1)),
            ((0, a, 1), (1, b, 1)),
            ((0, b, 2), (1, a, 2)),
            ((0, a, 2), (1, b, 2)),
            ((0, b, 3), (1, a, 3)),
            ((0, a, 3), (1, b, 3)),
        )
        for step in steps[part]:
            send_on(*step)

    def spread(half, kind, a, b, block, to):
        return pltpu.make_async_remote_copy(
            src_ref=held.at[half, block],
            dst_ref=held.at[half, block],
            send_sem=x_send.at[half, kind, a, b],
            recv_sem=x_recv.at[half, kind, a, b],
            device_id=to,
            device_id_type=MESH,
        )

    def block_of(half, a, b):
        dx, dy = (a, b) if half == 0 else (b, a)
        return (lax.rem(x + 4 - dx, 4) * 4 + lax.rem(y + 4 - dy, 4)) * 2

    def to_first(half, k):
        return near(k, 0, False) if half == 0 else near(0, k, False)

    def to_second(half, k):
        return near(0, k, False) if half == 0 else near(k, 0, False)

    def start(copy):
        copy.start()
        started.append(copy)

    def pass_second(half, a):
        for k in range(1, 4):
            start(spread(half, 1, a, k, block_of(half, a, 0) + core, to_second(half, k)))

    def pass_core(half, a, b):
        start(spread(half, 2, a, b, block_of(half, a, b) + core, near(0, 0, True)))

    def values(half):
        for piece in (2 * half, 2 * half + 1):
            part = rows_of(piece)
            st = own_st[half, part]
            m, l, total = st[:, 0:1], st[:, 1:2], own[half, part]
            for way in (0, 1):
                m, l, total = combine(m, l, total, *arrived(way, piece, 3))
            lat_s[part] = (total / l).astype(jnp.bfloat16)
        latent = lat_s[...]
        heads = half_rows // fresh.shape[0]
        for h in range(heads):
            full = jnp.dot(latent, value_up[half * heads + h], preferred_element_type=jnp.float32)
            picked = full.reshape(fresh.shape[0], heads, -1)[:, h, :]
            width = picked.shape[1]
            held[half, xfer, :, h * width : (h + 1) * width] = picked.astype(jnp.bfloat16)
        for k in range(1, 4):
            start(spread(half, 0, 0, k, xfer, to_first(half, k)))
        pass_second(half, 0)
        pass_core(half, 0, 0)

    def spread_first(half):
        for a in range(1, 4):
            spread(half, 0, 0, a, xfer, near(0, 0, True)).wait_recv()
            pass_second(half, a)
            pass_core(half, a, 0)

    def spread_second(half):
        for a in range(4):
            for b in range(1, 4):
                spread(half, 1, a, b, xfer, near(0, 0, True)).wait_recv()
                pass_core(half, a, b)

    def project(half):
        for a in range(4):
            for b in range(4):
                spread(half, 2, a, b, xfer, near(0, 0, True)).wait_recv()
        depth = held.shape[3]
        left = held[half].reshape(-1, depth)
        right = out_proj[:, half * depth : (half + 1) * depth]
        piece = lax.dot_general(left, right, (((1,), (1,)), ((), ())), preferred_element_type=jnp.float32)
        return piece.reshape(parts.shape)

    loads[0].wait()
    for half in (0, 1):
        for i in range(groups):
            load_acc(2 * i + half).wait()
        if half == 0:
            chain(0, 0)
            loads[1].wait()
            loads[2].wait()
            take_fresh(0)
    for part in (1, 2, 3):
        chain(0, part)
    chain(1, 0)
    take_fresh(1)
    chain(0, 4)
    chain(0, 5)
    chain(1, 1)
    loads[3].wait()
    values(0)
    chain(1, 2)
    chain(1, 3)
    spread_first(0)
    chain(1, 4)
    spread_second(0)
    chain(1, 5)
    loads[4].wait()
    parts[...] = project(0)
    values(1)
    spread_first(1)
    spread_second(1)
    parts[...] += project(1)

    def final(k):
        return pltpu.make_async_remote_copy(
            src_ref=share.at[0, k],
            dst_ref=share.at[1, k],
            send_sem=o_send.at[k],
            recv_sem=o_recv.at[k],
            device_id=along(k),
            device_id_type=MESH,
        )

    for k in (4, 3, 5, 2, 6, 1, 7):
        share[0, k] = parts[lax.rem(z + k, groups)].astype(jnp.bfloat16)
        start(final(k))
    done = parts[z]
    for k in (1, 7, 2, 6, 3, 5, 4):
        final(k).wait_recv()
        done += share[1, k].astype(jnp.float32)
    out[...] = done.astype(jnp.bfloat16)
    for c in started:
        c.wait_send()


def finish(acc, stats, q_own, fresh, value_up, out_proj, owners, groups, scale):
    vmem = pl.BlockSpec(memory_space=pltpu.VMEM)
    operands = (acc, stats, q_own, fresh, value_up, out_proj)
    rows = fresh.shape[0]
    half_rows, rank = acc.shape[1:]
    width, depth = out_proj.shape
    piece = owners * rows // groups
    dma = pltpu.SemaphoreType.DMA
    return pl.pallas_call(
        functools.partial(finish_kernel, scale),
        in_specs=[pl.BlockSpec(memory_space=pl.ANY)] * 6,
        out_specs=vmem,
        out_shape=jax.ShapeDtypeStruct((piece, width), jnp.bfloat16),
        scratch_shapes=[
            *(pltpu.VMEM(a.shape, a.dtype) for a in operands),
            dma((2 * groups,)),
            dma((5,)),
            pltpu.VMEM((2, 4, 4, half_rows // 2, rank), jnp.bfloat16),
            pltpu.VMEM((2, 4, 4, 8, 128), jnp.float32),
            pltpu.VMEM((2, 4, 4, half_rows // 2, rank), jnp.bfloat16),
            pltpu.VMEM((2, 4, 4, 8, 128), jnp.float32),
            pltpu.VMEM((2, half_rows, rank), jnp.float32),
            pltpu.VMEM((2, half_rows, 128), jnp.float32),
            pltpu.VMEM((half_rows, rank), jnp.bfloat16),
            pltpu.VMEM((2, owners, rows, depth // 2), jnp.bfloat16),
            pltpu.VMEM((2, groups, piece, width), jnp.bfloat16),
            pltpu.VMEM((groups, piece, width), jnp.float32),
            dma((2, 4, 4, 2)),
            dma((2, 4, 4, 2)),
            dma((2, 3, 4, 4)),
            dma((2, 3, 4, 4)),
            dma((groups,)),
            dma((groups,)),
        ],
        compiler_params=pltpu.CompilerParams(
            collective_id=1, has_side_effects=True, vmem_limit_bytes=56 * MIB
        ),
    )(*operands)


def body(
    kv_pool, lengths, start_device, page_table, queries, new_latent, key_up, value_up, out_proj
):
    owners = lax.axis_size("xfer")
    groups = lax.axis_size("head")
    latent = kv_pool.shape[2]
    lat_rank = value_up.shape[1]
    row_count, heads = queries.shape[:2]
    score_scale = queries.shape[2] ** (-0.5)
    half_rows = row_count * heads // 2
    pages, q_own = prepare(lengths, start_device, page_table, kv_pool, queries, key_up, owners, groups)
    keys, every = exchange(pages, q_own.reshape(2, half_rows, latent), groups)
    every = every.reshape(groups * 2, half_rows, latent)
    acc, stats = attend(lengths, start_device, every, keys, lengths.shape[0] // owners, lat_rank, score_scale)
    return finish(acc, stats, q_own, new_latent, value_up, out_proj.T, owners, groups, score_scale)


def solution(mesh):
    in_specs = (
        P(("xfer", "head"), None, None),
        P(),
        P(),
        P(),
        P("xfer", "head", None),
        P("xfer", None),
        P("head", None, None),
        P("head", None, None),
        P("head", "xfer"),
    )
    out_specs = P("head", "xfer")
    return jax.shard_map(body, mesh=mesh, in_specs=in_specs, out_specs=out_specs, check_vma=False)
```

```python
import functools

import jax
import jax.numpy as jnp
from jax import lax
from jax.experimental import pallas as pl
from jax.experimental.pallas import tpu as pltpu
from jax.sharding import PartitionSpec as P

MESH = pl.DeviceIdType.MESH
STEPS = 2
LOW = -1e30
FIRST, NEXT = 4, 8
MIB = 1024 * 1024


FAR = ((2, 2), (2, 1), (1, 2), (2, 3), (3, 2), (2, 0), (0, 2), (1, 1), (3, 3), (1, 3), (3, 1), (1, 0), (3, 0), (0, 1), (0, 3))
OFFSETS = tuple((*d, 0) for d in FAR) + tuple((*d, 1) for d in FAR) + ((0, 0, 1),)


def prepare_kernel(which, table, pool, queries, key_up_h, pages, q_own, raw, packed, key_up, sems, out_sems, up_sem, nope_s, wide_s):
    shift = table.shape[1]
    load_up = pltpu.make_async_copy(key_up_h, key_up, up_sem.at[0])

    def fetch(o, slot):
        return pltpu.make_async_copy(pool.at[slot], raw.at[o], sems.at[o])

    def store(o):
        return pltpu.make_async_copy(packed.at[o], pages.at[o], out_sems.at[o])

    def begin(o, c):
        e = which[o]
        fetch(o, table[e // shift, e % shift]).start()
        return c

    page = pool.shape[1]

    def pack(o, c):
        fetch(o, 0).wait()
        for i in range(rank // 128):
            packed[o, i * page : (i + 1) * page, :] = raw[o, :, i * 128 : (i + 1) * 128]
        top, low = raw[o, : page // 2, rank:], raw[o, page // 2 :, rank:]
        packed[o, rank // 128 * page :, :] = jnp.concatenate([top, low], axis=1)
        store(o).start()
        return c

    def end(o, c):
        store(o).wait()
        return c

    lax.fori_loop(0, pages.shape[0], begin, 0)
    load_up.start()
    rows, heads, width = queries.shape
    nope, rank = key_up.shape[1:]
    half = heads // 2
    flat = queries[...].reshape(rows * heads, width).astype(jnp.float32)
    nope_s[...] = flat[:, :nope]
    rope = flat[:, nope:].reshape(rows, 2, half, width - nope)
    lax.fori_loop(0, pages.shape[0], pack, 0)
    load_up.wait()
    for h in range(heads):
        mine = nope_s[pl.ds(h, rows, stride=heads), :].astype(jnp.bfloat16)
        full = jnp.dot(mine, key_up[h], preferred_element_type=jnp.float32)
        at = pl.ds((h // half) * rows * half + h % half, rows, stride=half)
        for c in range(rank // 128):
            wide_s[c, at, :] = full[:, c * 128 : (c + 1) * 128]
    for c in range(rank // 128):
        q_own[:, c * 128 : (c + 1) * 128] = wide_s[c].astype(jnp.bfloat16)
    for i in range(2):
        part = rope[:, i].reshape(rows * half, width - nope)
        q_own[i * rows * half : (i + 1) * rows * half, rank:] = part.astype(jnp.bfloat16)
    lax.fori_loop(0, pages.shape[0], end, 0)


def prepare(which, table, pool, queries, key_up):
    n = which.shape[0]
    rows, heads, width = queries.shape
    nope, rank = key_up.shape[1:]
    page, latent = pool.shape[1:]
    vmem = pl.BlockSpec(memory_space=pltpu.VMEM)
    smem = pl.BlockSpec(memory_space=pltpu.SMEM)
    hbm = pl.BlockSpec(memory_space=pl.ANY)
    tall = page * latent // 128
    dma = pltpu.SemaphoreType.DMA
    return pl.pallas_call(
        prepare_kernel,
        in_specs=[smem, smem, hbm, vmem, hbm],
        out_specs=[hbm, vmem],
        out_shape=[
            jax.ShapeDtypeStruct((n, tall, 128), pool.dtype),
            jax.ShapeDtypeStruct((rows * heads, rank + width - nope), queries.dtype),
        ],
        scratch_shapes=[
            pltpu.VMEM((n, page, latent), pool.dtype),
            pltpu.VMEM((n, tall, 128), pool.dtype),
            pltpu.VMEM(key_up.shape, key_up.dtype),
            dma((n,)),
            dma((n,)),
            dma((1,)),
            pltpu.VMEM((rows * heads, nope), jnp.float32),
            pltpu.VMEM((rank // 128, rows * heads, 128), jnp.float32),
        ],
        compiler_params=pltpu.CompilerParams(vmem_limit_bytes=56 * MIB),
    )(which, table, pool, queries, key_up)


def exchange_kernel(pages, q_own, keys, q_all, q_s, page_s, p_send, p_recv, z_send, z_recv, own_sem):
    z = lax.axis_index("head")
    xfer = lax.axis_index("xfer")
    x, y, core = xfer // 8, (xfer // 2) % 4, xfer % 2
    groups = q_all.shape[0]

    def at(offset):
        dx, dy, dc = offset
        return (lax.rem(x + dx, 4) * 4 + lax.rem(y + dy, 4)) * 2 + lax.rem(core + dc, 2)

    mine = [
        pltpu.make_async_copy(q_own, q_s, own_sem.at[0]),
        pltpu.make_async_copy(pages.at[xfer], page_s, own_sem.at[1]),
    ]
    for c in mine:
        c.start()
    right, left = (xfer, lax.rem(z + 1, groups)), (xfer, lax.rem(z + groups - 1, groups))
    barrier = pltpu.get_barrier_semaphore()
    peers = [right, left] + [(at(offset), z) for offset in OFFSETS]
    for peer in peers:
        pl.semaphore_signal(barrier, inc=1, device_id=peer, device_id_type=MESH)
    pl.semaphore_wait(barrier, len(peers))

    def hop(way, j):
        block = lax.rem(z + groups - (j - 1), groups) if way == 0 else lax.rem(z + j - 1, groups)
        src, dst = (q_s if j == 1 else q_all.at[block]), q_all.at[block]
        if j == groups // 2:
            src, dst = src.at[way], dst.at[way]
        return pltpu.make_async_remote_copy(
            src_ref=src,
            dst_ref=dst,
            send_sem=z_send.at[way, j],
            recv_sem=z_recv.at[way, j],
            device_id=right if way == 0 else left,
            device_id_type=MESH,
        )

    def page(i, offset):
        to = at(offset)
        return pltpu.make_async_remote_copy(
            src_ref=pages.at[to],
            dst_ref=keys.at[xfer],
            send_sem=p_send.at[i],
            recv_sem=p_recv.at[i],
            device_id=(to, z),
            device_id_type=MESH,
        )

    hops = [hop(way, j) for j in range(1, groups // 2 + 1) for way in (0, 1)]
    copies = [page(i, offset) for i, offset in enumerate(OFFSETS)]
    for c in mine:
        c.wait()
    for c in hops[:2] + copies:
        c.start()
    mine = [
        pltpu.make_async_copy(q_s, q_all.at[z], own_sem.at[2]),
        pltpu.make_async_copy(page_s, keys.at[xfer], own_sem.at[3]),
    ]
    for c in mine:
        c.start()
    for j in range(1, groups // 2):
        for way in (0, 1):
            hops[(j - 1) * 2 + way].wait_recv()
            hops[j * 2 + way].start()
    for c in hops[-2:]:
        c.wait_recv()
    for c in copies:
        c.wait_recv()
    for c in mine:
        c.wait()
    for c in hops + copies:
        c.wait_send()


def exchange(pages, q_own, groups):
    hbm = pl.BlockSpec(memory_space=pl.ANY)
    dma = pltpu.SemaphoreType.DMA
    n = pages.shape[0]
    return pl.pallas_call(
        exchange_kernel,
        in_specs=[hbm, hbm],
        out_specs=[hbm, hbm],
        out_shape=[
            jax.ShapeDtypeStruct(pages.shape, pages.dtype),
            jax.ShapeDtypeStruct((groups, *q_own.shape), q_own.dtype),
        ],
        scratch_shapes=[
            pltpu.VMEM(q_own.shape, q_own.dtype),
            pltpu.VMEM(pages.shape[1:], pages.dtype),
            dma((n,)),
            dma((n,)),
            dma((2, 8)),
            dma((2, 8)),
            dma((4,)),
        ],
        compiler_params=pltpu.CompilerParams(
            collective_id=0, has_side_effects=True, vmem_limit_bytes=56 * MIB
        ),
    )(pages, q_own)


def attend_kernel(scale, requests, lengths, starts, q, keys, acc, stats, q_s, k_s, acc_s, st_s, m_s, l_s, k_sem, q_sem, o_sem):
    member = lax.axis_index("head")
    base = lax.axis_index("xfer") * requests
    slots = keys.shape[0]
    latent, rank = q.shape[2], acc.shape[2]
    page = keys.shape[1] * 128 // latent
    rows = q.shape[1] // requests
    many = q.shape[0] * rows
    more = k_s.shape[0] - slots
    loads = [
        pltpu.make_async_copy(keys, k_s.at[pl.ds(0, slots)], k_sem.at[0]),
        pltpu.make_async_copy(keys.at[pl.ds(0, more)], k_s.at[pl.ds(slots, more)], k_sem.at[1]),
    ]
    q_loads = [
        pltpu.make_async_copy(q.at[:, pl.ds(r * rows, rows)], q_s.at[r], q_sem.at[r]) for r in range(requests)
    ]
    for c in loads + q_loads:
        c.start()
    odd = lax.broadcasted_iota(jnp.int32, (many, 128), 1) % 2
    for c in loads:
        c.wait()
    stores = []
    for r in range(requests):
        length, start = lengths[base + r], starts[base + r]
        pages = (length + page - 1) // page
        skip = (member - start) & 7
        slot = ((start + skip) & 255) >> 3
        count = jnp.maximum(pages - skip + 7, 0) >> 3
        q_loads[r].wait()

        def window(nth, size):
            k = k_s[pl.ds((slot + nth) & (slots - 1), size)]
            columns = [k[:, i * page : (i + 1) * page].reshape(size * page, 128) for i in range(rank // 128)]
            wide = jnp.concatenate(columns, axis=1)
            folded = k[:, rank // 128 * page :]
            narrow = jnp.concatenate([folded[:, :, : latent - rank], folded[:, :, latent - rank :]], axis=1)
            mine = q_s[r].reshape(many, latent)
            s = lax.dot_general(
                mine[:, :rank], wide, (((1,), (1,)), ((), ())), preferred_element_type=jnp.float32
            )
            s += lax.dot_general(
                mine[:, rank:],
                narrow.reshape(size * page, latent - rank),
                (((1,), (1,)), ((), ())),
                preferred_element_type=jnp.float32,
            )
            lane = lax.broadcasted_iota(jnp.int32, (1, size * page), 1)
            at = nth + lane // page
            seen = (at < count) & ((skip + at * 8) * page + lane % page < length)
            return jnp.where(seen, s * scale, LOW), seen, wide

        def weigh(w, v):
            return jnp.dot(w.astype(jnp.bfloat16), v, preferred_element_type=jnp.float32)

        s, seen, v = window(0, FIRST)
        m = jnp.max(s, axis=1, keepdims=True)
        w = jnp.where(seen, jnp.exp(s - m), 0.0)
        m_s[...] = jnp.broadcast_to(m, m_s.shape)
        l_s[...] = jnp.broadcast_to(jnp.sum(w, axis=1, keepdims=True), l_s.shape)
        acc_s[r] = weigh(w, v).reshape(acc_s.shape[1:])

        def step(i, c):
            s, _, v = window(FIRST + i * NEXT, NEXT)
            m_old = m_s[:, :1]
            m_new = jnp.maximum(m_old, jnp.max(s, axis=1, keepdims=True))
            keep = jnp.exp(m_old - m_new)
            w = jnp.exp(s - m_new)
            l_s[...] = l_s[...] * keep + jnp.sum(w, axis=1, keepdims=True)
            m_s[...] = jnp.broadcast_to(m_new, m_s.shape)
            old = acc_s[r].reshape(many, rank)
            acc_s[r] = (old * keep + weigh(w, v)).reshape(acc_s.shape[1:])
            return c

        lax.fori_loop(0, (jnp.maximum(count - FIRST, 0) + NEXT - 1) // NEXT, step, 0)
        st_s[r] = jnp.where(odd == 0, m_s[...], l_s[...]).reshape(st_s.shape[1:])
        part = pl.ds(r * rows, rows)
        stores += [
            pltpu.make_async_copy(acc_s.at[r], acc.at[:, part], o_sem.at[0, r]),
            pltpu.make_async_copy(st_s.at[r], stats.at[:, part], o_sem.at[1, r]),
        ]
        for c in stores[-2:]:
            c.start()
    for c in stores:
        c.wait()


def attend(lengths, starts, q, keys, requests, rank, scale):
    smem = pl.BlockSpec(memory_space=pltpu.SMEM)
    hbm = pl.BlockSpec(memory_space=pl.ANY)
    chunks, rows = q.shape[0], q.shape[1] // requests
    many = chunks * rows
    slots, tall = keys.shape[:2]
    latent = q.shape[2]
    dma = pltpu.SemaphoreType.DMA
    return pl.pallas_call(
        functools.partial(attend_kernel, scale, requests),
        in_specs=[smem, smem, hbm, hbm],
        out_specs=[hbm, hbm],
        out_shape=[
            jax.ShapeDtypeStruct((*q.shape[:2], rank), jnp.float32),
            jax.ShapeDtypeStruct((*q.shape[:2], 128), jnp.float32),
        ],
        scratch_shapes=[
            pltpu.VMEM((requests, chunks, rows, latent), q.dtype),
            pltpu.VMEM((slots + NEXT, tall, 128), keys.dtype),
            pltpu.VMEM((requests, chunks, rows, rank), jnp.float32),
            pltpu.VMEM((requests, chunks, rows, 128), jnp.float32),
            pltpu.VMEM((many, 128), jnp.float32),
            pltpu.VMEM((many, 128), jnp.float32),
            dma((2,)),
            dma((requests,)),
            dma((2, requests)),
        ],
        compiler_params=pltpu.CompilerParams(vmem_limit_bytes=56 * MIB),
    )(lengths, starts, q, keys)


def combine(m_a, l_a, acc_a, m_b, l_b, acc_b):
    m = jnp.maximum(m_a, m_b)
    f_a, f_b = jnp.exp(m_a - m), jnp.exp(m_b - m)
    return m, l_a * f_a + l_b * f_b, acc_a * f_a + acc_b * f_b


def finish_kernel(
    scale, acc_h, stats_h, q_own_h, fresh_h, value_up_h, out_proj_h, out,
    acc, stats, q_own, fresh, value_up, out_proj, acc_sem, in_sem, sent, sent_st, got, got_st, own, own_st, held, share, parts, z_send, z_recv, x_send, x_recv, o_send, o_recv,
):
    z = lax.axis_index("head")
    xfer = lax.axis_index("xfer")
    x, y, core = xfer // 8, (xfer // 2) % 4, xfer % 2
    groups = 8
    rank = acc.shape[2]
    half_rows = acc.shape[1]
    loads = [
        pltpu.make_async_copy(src, dst, in_sem.at[i])
        for i, (src, dst) in enumerate(
            ((stats_h, stats), (q_own_h, q_own), (fresh_h, fresh), (value_up_h, value_up), (out_proj_h, out_proj))
        )
    ]

    def load_acc(at):
        return pltpu.make_async_copy(acc_h.at[at], acc.at[at], acc_sem.at[at])

    loads[0].start()
    for distance in (4, 3, 5, 0, 2, 6, 1, 7):
        for half in (0, 1):
            load_acc(lax.rem(z + distance, groups) * 2 + half).start()
    for c in loads[1:]:
        c.start()

    def near(dx, dy, flip):
        c = 1 - core if flip else core
        return ((lax.rem(x + dx, 4) * 4 + lax.rem(y + dy, 4)) * 2 + c, z)

    def along(k):
        return (xfer, lax.rem(z + k, groups))

    barrier = pltpu.get_barrier_semaphore()
    peers = [along(k) for k in range(1, 8)]
    peers += [near(k, 0, False) for k in range(1, 4)] + [near(0, k, False) for k in range(1, 4)]
    peers += [near(0, 0, True)]
    for peer in peers:
        pl.semaphore_signal(barrier, inc=1, device_id=peer, device_id_type=MESH)
    pl.semaphore_wait(barrier, len(peers))

    def z_copies(way, half, hop):
        to = along(1 if way == 0 else 7)
        return [
            pltpu.make_async_remote_copy(
                src_ref=src.at[way, half, hop],
                dst_ref=dst.at[way, half, hop],
                send_sem=z_send.at[way, half, hop, i],
                recv_sem=z_recv.at[way, half, hop, i],
                device_id=to,
                device_id_type=MESH,
            )
            for i, (src, dst) in enumerate(((sent, got), (sent_st, got_st)))
        ]

    def index_of(way, half, distance):
        d = lax.rem(z + distance if way == 0 else z + groups - distance, groups)
        return d * 2 + half

    odd = lax.broadcasted_iota(jnp.int32, (half_rows, 128), 1) % 2

    def arrived(way, half, hop):
        for c in z_copies(way, half, hop):
            c.wait_recv()
        st = jnp.tile(got_st[way, half, hop], (half_rows // 8, 1)).T
        return st[:, 0:1], st[:, 1:2], got[way, half, hop].astype(jnp.float32)

    started = []

    def send_on(way, half, hop):
        at = index_of(way, half, 4 - hop)
        mine = stats[at]
        load_acc(at).wait()
        if hop == (0 if way == half else 1):
            sent[way, half, hop] = acc[at].astype(jnp.bfloat16)
            sent_st[way, half, hop] = mine.T[0:8]
        else:
            m, l, total = combine(*arrived(way, half, hop - 1), mine[:, 0:1], mine[:, 1:2], acc[at])
            sent[way, half, hop] = total.astype(jnp.bfloat16)
            sent_st[way, half, hop] = jnp.where(odd == 0, m, l).T[0:8]
        for c in z_copies(way, half, hop):
            c.start()
            started.append(c)

    def take_fresh(half):
        rows = slice(half * half_rows, (half + 1) * half_rows)
        s = (
            lax.dot_general(
                q_own[rows, :], fresh[...], (((1,), (1,)), ((), ())), preferred_element_type=jnp.float32
            )
            * scale
        )
        row = lax.broadcasted_iota(jnp.int32, s.shape, 0) // 8
        col = lax.broadcasted_iota(jnp.int32, s.shape, 1)
        s = jnp.where((row // STEPS == col // STEPS) & (col <= row), s, LOW)
        m = jnp.max(s, axis=1, keepdims=True)
        w = jnp.exp(s - m)
        l = jnp.sum(w, axis=1, keepdims=True)
        more = jnp.dot(w.astype(jnp.bfloat16), fresh[:, :rank], preferred_element_type=jnp.float32)
        at = z * 2 + half
        mine = stats[at]
        load_acc(at).wait()
        m, l, total = combine(m, l, more, mine[:, 0:1], mine[:, 1:2], acc[at])
        own[half] = total
        own_st[half] = jnp.where(odd == 0, m, l)

    loads[0].wait()
    send_on(0, 0, 0)
    send_on(1, 1, 0)
    send_on(0, 1, 1)
    send_on(1, 0, 1)
    loads[1].wait()
    loads[2].wait()
    take_fresh(0)
    take_fresh(1)
    for hop in (1, 2, 3):
        send_on(0, 0, hop)
        send_on(1, 1, hop)
        if hop < 3:
            send_on(0, 1, hop + 1)
            send_on(1, 0, hop + 1)

    def spread(half, kind, a, b, block, to):
        return pltpu.make_async_remote_copy(
            src_ref=held.at[half, block],
            dst_ref=held.at[half, block],
            send_sem=x_send.at[half, kind, a, b],
            recv_sem=x_recv.at[half, kind, a, b],
            device_id=to,
            device_id_type=MESH,
        )

    def block_of(half, a, b):
        dx, dy = (a, b) if half == 0 else (b, a)
        return (lax.rem(x + 4 - dx, 4) * 4 + lax.rem(y + 4 - dy, 4)) * 2

    def to_first(half, k):
        return near(k, 0, False) if half == 0 else near(0, k, False)

    def to_second(half, k):
        return near(0, k, False) if half == 0 else near(k, 0, False)

    def start(copy):
        copy.start()
        started.append(copy)

    def pass_second(half, a):
        for k in range(1, 4):
            start(spread(half, 1, a, k, block_of(half, a, 0) + core, to_second(half, k)))

    def pass_core(half, a, b):
        start(spread(half, 2, a, b, block_of(half, a, b) + core, near(0, 0, True)))

    loads[3].wait()
    for half in (1, 0):
        m, l, total = own_st[half][:, 0:1], own_st[half][:, 1:2], own[half]
        for way in (0, 1):
            m, l, total = combine(m, l, total, *arrived(way, half, 3))
        latent = (total / l).astype(jnp.bfloat16)
        heads = half_rows // fresh.shape[0]
        for h in range(heads):
            full = jnp.dot(latent, value_up[half * heads + h], preferred_element_type=jnp.float32)
            picked = full.reshape(fresh.shape[0], heads, -1)[:, h, :]
            width = picked.shape[1]
            held[half, xfer, :, h * width : (h + 1) * width] = picked.astype(jnp.bfloat16)
        for k in range(1, 4):
            start(spread(half, 0, 0, k, xfer, to_first(half, k)))
        pass_second(half, 0)
        pass_core(half, 0, 0)
    for a in range(1, 4):
        for half in (1, 0):
            spread(half, 0, 0, a, xfer, near(0, 0, True)).wait_recv()
            pass_second(half, a)
            pass_core(half, a, 0)
    for a in range(4):
        for b in range(1, 4):
            for half in (1, 0):
                spread(half, 1, a, b, xfer, near(0, 0, True)).wait_recv()
                pass_core(half, a, b)
    for half in (1, 0):
        for a in range(4):
            for b in range(4):
                spread(half, 2, a, b, xfer, near(0, 0, True)).wait_recv()

    loads[4].wait()
    depth = held.shape[3]
    total = None
    for half in (0, 1):
        left = held[half].reshape(-1, depth)
        right = out_proj[:, half * depth : (half + 1) * depth]
        piece = lax.dot_general(left, right, (((1,), (1,)), ((), ())), preferred_element_type=jnp.float32)
        total = piece if total is None else total + piece
    parts[...] = total.reshape(parts.shape)

    def final(k):
        return pltpu.make_async_remote_copy(
            src_ref=share.at[0, k],
            dst_ref=share.at[1, k],
            send_sem=o_send.at[k],
            recv_sem=o_recv.at[k],
            device_id=along(k),
            device_id_type=MESH,
        )

    for k in (4, 3, 5, 2, 6, 1, 7):
        share[0, k] = parts[lax.rem(z + k, groups)].astype(jnp.bfloat16)
        start(final(k))
    done = parts[z]
    for k in (1, 7, 2, 6, 3, 5, 4):
        final(k).wait_recv()
        done += share[1, k].astype(jnp.float32)
    out[...] = done.astype(jnp.bfloat16)
    for c in started:
        c.wait_send()


def finish(acc, stats, q_own, fresh, value_up, out_proj, owners, groups, scale):
    vmem = pl.BlockSpec(memory_space=pltpu.VMEM)
    operands = (acc, stats, q_own, fresh, value_up, out_proj)
    rows = fresh.shape[0]
    half_rows, rank = acc.shape[1:]
    width, depth = out_proj.shape
    piece = owners * rows // groups
    dma = pltpu.SemaphoreType.DMA
    return pl.pallas_call(
        functools.partial(finish_kernel, scale),
        in_specs=[pl.BlockSpec(memory_space=pl.ANY)] * 6,
        out_specs=vmem,
        out_shape=jax.ShapeDtypeStruct((piece, width), jnp.bfloat16),
        scratch_shapes=[
            *(pltpu.VMEM(a.shape, a.dtype) for a in operands),
            dma((2 * groups,)),
            dma((5,)),
            pltpu.VMEM((2, 2, 4, half_rows, rank), jnp.bfloat16),
            pltpu.VMEM((2, 2, 4, 8, 128), jnp.float32),
            pltpu.VMEM((2, 2, 4, half_rows, rank), jnp.bfloat16),
            pltpu.VMEM((2, 2, 4, 8, 128), jnp.float32),
            pltpu.VMEM((2, half_rows, rank), jnp.float32),
            pltpu.VMEM((2, half_rows, 128), jnp.float32),
            pltpu.VMEM((2, owners, rows, depth // 2), jnp.bfloat16),
            pltpu.VMEM((2, groups, piece, width), jnp.bfloat16),
            pltpu.VMEM((groups, piece, width), jnp.float32),
            dma((2, 2, 4, 2)),
            dma((2, 2, 4, 2)),
            dma((2, 3, 4, 4)),
            dma((2, 3, 4, 4)),
            dma((groups,)),
            dma((groups,)),
        ],
        compiler_params=pltpu.CompilerParams(
            collective_id=1, has_side_effects=True, vmem_limit_bytes=56 * MIB
        ),
    )(*operands)


def body(
    kv_pool, lengths, start_device, page_table, queries, new_latent, key_up, value_up, out_proj
):
    owners = lax.axis_size("xfer")
    groups = lax.axis_size("head")
    latent = kv_pool.shape[2]
    lat_rank = value_up.shape[1]
    row_count, heads = queries.shape[:2]
    score_scale = queries.shape[2] ** (-0.5)
    half_rows = row_count * heads // 2
    device = lax.axis_index("xfer") * groups + lax.axis_index("head")
    nth = (device - start_device) % (owners * groups)
    flat = jnp.arange(lengths.shape[0], dtype=jnp.int32) * page_table.shape[1] + nth
    here = nth * kv_pool.shape[1] < lengths
    which = jnp.where(here, flat, 0).reshape(owners, -1).sum(axis=1)
    pages, q_own = prepare(which, page_table, kv_pool, queries, key_up)
    keys, every = exchange(pages, q_own.reshape(2, half_rows, latent), groups)
    every = every.reshape(groups * 2, half_rows, latent)
    acc, stats = attend(lengths, start_device, every, keys, lengths.shape[0] // owners, lat_rank, score_scale)
    return finish(acc, stats, q_own, new_latent, value_up, out_proj.T, owners, groups, score_scale)


def solution(mesh):
    in_specs = (
        P(("xfer", "head"), None, None),
        P(),
        P(),
        P(),
        P("xfer", "head", None),
        P("xfer", None),
        P("head", None, None),
        P("head", None, None),
        P("head", "xfer"),
    )
    out_specs = P("head", "xfer")
    return jax.shard_map(body, mesh=mesh, in_specs=in_specs, out_specs=out_specs, check_vma=False)
```

```python
import functools

import jax
import jax.numpy as jnp
from jax import lax
from jax.experimental import pallas as pl
from jax.experimental.pallas import tpu as pltpu
from jax.sharding import PartitionSpec as P

MESH = pl.DeviceIdType.MESH
STEPS = 2
LOW = -1e30
FIRST, NEXT = 4, 8
TOGETHER = 4
MIB = 1024 * 1024


FAR = ((2, 2), (2, 1), (1, 2), (2, 3), (3, 2), (2, 0), (0, 2), (1, 1), (3, 3), (1, 3), (3, 1), (1, 0), (3, 0), (0, 1), (0, 3))
OFFSETS = tuple((*d, 0) for d in FAR) + tuple((*d, 1) for d in FAR) + ((0, 0, 1),)


def prepare_kernel(chosen, pool, queries, key_up_h, pages, q_own, raw, packed, key_up, sems, out_sems, up_sem, nope_s, wide_s):
    load_up = pltpu.make_async_copy(key_up_h, key_up, up_sem.at[0])

    def fetch(o, slot):
        return pltpu.make_async_copy(pool.at[slot], raw.at[o], sems.at[o])

    def store(o):
        return pltpu.make_async_copy(packed.at[o], pages.at[o], out_sems.at[o])

    def begin(o, c):
        fetch(o, chosen[o]).start()
        return c

    page = pool.shape[1]

    def pack(o, c):
        fetch(o, 0).wait()
        for i in range(rank // 128):
            packed[o, i * page : (i + 1) * page, :] = raw[o, :, i * 128 : (i + 1) * 128]
        top, low = raw[o, : page // 2, rank:], raw[o, page // 2 :, rank:]
        packed[o, rank // 128 * page :, :] = jnp.concatenate([top, low], axis=1)
        store(o).start()
        return c

    def end(o, c):
        store(o).wait()
        return c

    lax.fori_loop(0, pages.shape[0], begin, 0)
    load_up.start()
    rows, heads, width = queries.shape
    nope, rank = key_up.shape[1:]
    half = heads // 2
    flat = queries[...].reshape(rows * heads, width).astype(jnp.float32)
    nope_s[...] = flat[:, :nope]
    rope = flat[:, nope:].reshape(rows, 2, half, width - nope)
    lax.fori_loop(0, pages.shape[0], pack, 0)
    load_up.wait()
    for h in range(heads):
        mine = nope_s[pl.ds(h, rows, stride=heads), :].astype(jnp.bfloat16)
        full = jnp.dot(mine, key_up[h], preferred_element_type=jnp.float32)
        at = pl.ds((h // half) * rows * half + h % half, rows, stride=half)
        for c in range(rank // 128):
            wide_s[c, at, :] = full[:, c * 128 : (c + 1) * 128]
    for c in range(rank // 128):
        q_own[:, c * 128 : (c + 1) * 128] = wide_s[c].astype(jnp.bfloat16)
    for i in range(2):
        part = rope[:, i].reshape(rows * half, width - nope)
        q_own[i * rows * half : (i + 1) * rows * half, rank:] = part.astype(jnp.bfloat16)
    lax.fori_loop(0, pages.shape[0], end, 0)


def prepare(chosen, pool, queries, key_up):
    n = chosen.shape[0]
    rows, heads, width = queries.shape
    nope, rank = key_up.shape[1:]
    page, latent = pool.shape[1:]
    vmem = pl.BlockSpec(memory_space=pltpu.VMEM)
    smem = pl.BlockSpec(memory_space=pltpu.SMEM)
    hbm = pl.BlockSpec(memory_space=pl.ANY)
    tall = page * latent // 128
    dma = pltpu.SemaphoreType.DMA
    return pl.pallas_call(
        prepare_kernel,
        in_specs=[smem, hbm, vmem, hbm],
        out_specs=[hbm, vmem],
        out_shape=[
            jax.ShapeDtypeStruct((n, tall, 128), pool.dtype),
            jax.ShapeDtypeStruct((rows * heads, rank + width - nope), queries.dtype),
        ],
        scratch_shapes=[
            pltpu.VMEM((n, page, latent), pool.dtype),
            pltpu.VMEM((n, tall, 128), pool.dtype),
            pltpu.VMEM(key_up.shape, key_up.dtype),
            dma((n,)),
            dma((n,)),
            dma((1,)),
            pltpu.VMEM((rows * heads, nope), jnp.float32),
            pltpu.VMEM((rank // 128, rows * heads, 128), jnp.float32),
        ],
        compiler_params=pltpu.CompilerParams(vmem_limit_bytes=56 * MIB),
    )(chosen, pool, queries, key_up)


def exchange_kernel(pages, q_own, keys, q_all, q_s, page_s, p_send, p_recv, z_send, z_recv, own_sem):
    z = lax.axis_index("head")
    xfer = lax.axis_index("xfer")
    x, y, core = xfer // 8, (xfer // 2) % 4, xfer % 2
    groups = q_all.shape[0]

    def at(offset):
        dx, dy, dc = offset
        return (lax.rem(x + dx, 4) * 4 + lax.rem(y + dy, 4)) * 2 + lax.rem(core + dc, 2)

    mine = [
        pltpu.make_async_copy(q_own, q_s, own_sem.at[0]),
        pltpu.make_async_copy(pages.at[xfer], page_s, own_sem.at[1]),
    ]
    for c in mine:
        c.start()
    right, left = (xfer, lax.rem(z + 1, groups)), (xfer, lax.rem(z + groups - 1, groups))
    barrier = pltpu.get_barrier_semaphore()
    peers = [right, left] + [(at(offset), z) for offset in OFFSETS]
    for peer in peers:
        pl.semaphore_signal(barrier, inc=1, device_id=peer, device_id_type=MESH)
    pl.semaphore_wait(barrier, len(peers))

    def hop(way, j):
        block = lax.rem(z + groups - (j - 1), groups) if way == 0 else lax.rem(z + j - 1, groups)
        src, dst = (q_s if j == 1 else q_all.at[block]), q_all.at[block]
        if j == groups // 2:
            src, dst = src.at[way], dst.at[way]
        return pltpu.make_async_remote_copy(
            src_ref=src,
            dst_ref=dst,
            send_sem=z_send.at[way, j],
            recv_sem=z_recv.at[way, j],
            device_id=right if way == 0 else left,
            device_id_type=MESH,
        )

    def page(i, offset):
        to = at(offset)
        return pltpu.make_async_remote_copy(
            src_ref=pages.at[to],
            dst_ref=keys.at[xfer],
            send_sem=p_send.at[i],
            recv_sem=p_recv.at[i],
            device_id=(to, z),
            device_id_type=MESH,
        )

    hops = [hop(way, j) for j in range(1, groups // 2 + 1) for way in (0, 1)]
    copies = [page(i, offset) for i, offset in enumerate(OFFSETS)]
    for c in mine:
        c.wait()
    for c in hops[:2] + copies:
        c.start()
    mine = [
        pltpu.make_async_copy(q_s, q_all.at[z], own_sem.at[2]),
        pltpu.make_async_copy(page_s, keys.at[xfer], own_sem.at[3]),
    ]
    for c in mine:
        c.start()
    for j in range(1, groups // 2):
        for way in (0, 1):
            hops[(j - 1) * 2 + way].wait_recv()
            hops[j * 2 + way].start()
    for c in hops[-2:]:
        c.wait_recv()
    for c in copies:
        c.wait_recv()
    for c in mine:
        c.wait()
    for c in hops + copies:
        c.wait_send()


def exchange(pages, q_own, groups):
    hbm = pl.BlockSpec(memory_space=pl.ANY)
    dma = pltpu.SemaphoreType.DMA
    n = pages.shape[0]
    return pl.pallas_call(
        exchange_kernel,
        in_specs=[hbm, hbm],
        out_specs=[hbm, hbm],
        out_shape=[
            jax.ShapeDtypeStruct(pages.shape, pages.dtype),
            jax.ShapeDtypeStruct((groups, *q_own.shape), q_own.dtype),
        ],
        scratch_shapes=[
            pltpu.VMEM(q_own.shape, q_own.dtype),
            pltpu.VMEM(pages.shape[1:], pages.dtype),
            dma((n,)),
            dma((n,)),
            dma((2, 8)),
            dma((2, 8)),
            dma((4,)),
        ],
        compiler_params=pltpu.CompilerParams(
            collective_id=0, has_side_effects=True, vmem_limit_bytes=56 * MIB
        ),
    )(pages, q_own)


def attend_kernel(scale, requests, lengths, starts, q, keys, acc, stats, q_s, k_s, acc_s, st_s, k_sem, q_sem, o_sem):
    member = lax.axis_index("head")
    base = lax.axis_index("xfer") * requests
    slots = keys.shape[0]
    latent, rank = q.shape[2], acc.shape[2]
    page = keys.shape[1] * 128 // latent
    rows = q.shape[1] // requests
    many = q.shape[0] * rows
    more = k_s.shape[0] - slots
    loads = [
        pltpu.make_async_copy(keys, k_s.at[pl.ds(0, slots)], k_sem.at[0]),
        pltpu.make_async_copy(keys.at[pl.ds(0, more)], k_s.at[pl.ds(slots, more)], k_sem.at[1]),
    ]
    q_loads = [
        pltpu.make_async_copy(q.at[:, pl.ds(r * rows, rows)], q_s.at[r], q_sem.at[r]) for r in range(requests)
    ]
    for c in loads + q_loads:
        c.start()
    odd = lax.broadcasted_iota(jnp.int32, (many, 128), 1) % 2
    def weigh(w, v):
        return jnp.dot(w.astype(jnp.bfloat16), v, preferred_element_type=jnp.float32)

    def place(r):
        length, start = lengths[base + r], starts[base + r]
        skip = (member - start) & 7
        slot = ((start + skip) & 255) >> 3
        count = jnp.maximum((length + page - 1) // page - skip + 7, 0) >> 3
        return length, skip, slot, count

    def window(r, where, nth, size):
        length, skip, slot, count = where
        k = k_s[pl.ds((slot + nth) & (slots - 1), size)]
        columns = [k[:, i * page : (i + 1) * page].reshape(size * page, 128) for i in range(rank // 128)]
        wide = jnp.concatenate(columns, axis=1)
        folded = k[:, rank // 128 * page :]
        narrow = jnp.concatenate([folded[:, :, : latent - rank], folded[:, :, latent - rank :]], axis=1)
        mine = q_s[r].reshape(many, latent)
        s = lax.dot_general(
            mine[:, :rank], wide, (((1,), (1,)), ((), ())), preferred_element_type=jnp.float32
        )
        s += lax.dot_general(
            mine[:, rank:],
            narrow.reshape(size * page, latent - rank),
            (((1,), (1,)), ((), ())),
            preferred_element_type=jnp.float32,
        )
        lane = lax.broadcasted_iota(jnp.int32, (1, size * page), 1)
        at = nth + lane // page
        seen = (at < count) & ((skip + at * 8) * page + lane % page < length)
        return jnp.where(seen, s * scale, LOW), seen, wide

    def begin(r):
        s, seen, v = window(r, place(r), 0, FIRST)
        m = jnp.max(s, axis=1, keepdims=True)
        w = jnp.where(seen, jnp.exp(s - m), 0.0)
        l = jnp.sum(w, axis=1, keepdims=True)
        st_s[r] = jnp.where(odd == 0, m, l).reshape(st_s.shape[1:])
        acc_s[r] = weigh(w, v).reshape(acc_s.shape[1:])

    def go_on(r):
        where = place(r)

        def step(i, c):
            s, _, v = window(r, where, FIRST + i * NEXT, NEXT)
            old = st_s[r].reshape(many, 128)
            m_old, l_old = old[:, 0:1], old[:, 1:2]
            m = jnp.maximum(m_old, jnp.max(s, axis=1, keepdims=True))
            keep = jnp.exp(m_old - m)
            w = jnp.exp(s - m)
            l = l_old * keep + jnp.sum(w, axis=1, keepdims=True)
            st_s[r] = jnp.where(odd == 0, m, l).reshape(st_s.shape[1:])
            old_acc = acc_s[r].reshape(many, rank)
            acc_s[r] = (old_acc * keep + weigh(w, v)).reshape(acc_s.shape[1:])
            return c

        lax.fori_loop(0, (jnp.maximum(where[3] - FIRST, 0) + NEXT - 1) // NEXT, step, 0)

    for c in loads:
        c.wait()
    stores = []
    for group in range(0, requests, TOGETHER):
        members = range(group, group + TOGETHER)
        for r in members:
            q_loads[r].wait()
        for r in members:
            begin(r)
        for r in members:
            go_on(r)
            part = pl.ds(r * rows, rows)
            stores += [
                pltpu.make_async_copy(acc_s.at[r], acc.at[:, part], o_sem.at[0, r]),
                pltpu.make_async_copy(st_s.at[r], stats.at[:, part], o_sem.at[1, r]),
            ]
            for c in stores[-2:]:
                c.start()
    for c in stores:
        c.wait()


def attend(lengths, starts, q, keys, requests, rank, scale):
    smem = pl.BlockSpec(memory_space=pltpu.SMEM)
    hbm = pl.BlockSpec(memory_space=pl.ANY)
    chunks, rows = q.shape[0], q.shape[1] // requests
    slots, tall = keys.shape[:2]
    latent = q.shape[2]
    dma = pltpu.SemaphoreType.DMA
    return pl.pallas_call(
        functools.partial(attend_kernel, scale, requests),
        in_specs=[smem, smem, hbm, hbm],
        out_specs=[hbm, hbm],
        out_shape=[
            jax.ShapeDtypeStruct((*q.shape[:2], rank), jnp.float32),
            jax.ShapeDtypeStruct((*q.shape[:2], 128), jnp.float32),
        ],
        scratch_shapes=[
            pltpu.VMEM((requests, chunks, rows, latent), q.dtype),
            pltpu.VMEM((slots + NEXT, tall, 128), keys.dtype),
            pltpu.VMEM((requests, chunks, rows, rank), jnp.float32),
            pltpu.VMEM((requests, chunks, rows, 128), jnp.float32),
            dma((2,)),
            dma((requests,)),
            dma((2, requests)),
        ],
        compiler_params=pltpu.CompilerParams(vmem_limit_bytes=56 * MIB),
    )(lengths, starts, q, keys)


def combine(m_a, l_a, acc_a, m_b, l_b, acc_b):
    m = jnp.maximum(m_a, m_b)
    f_a, f_b = jnp.exp(m_a - m), jnp.exp(m_b - m)
    return m, l_a * f_a + l_b * f_b, acc_a * f_a + acc_b * f_b


def finish_kernel(
    scale, acc_h, stats_h, q_own_h, fresh_h, value_up_h, out_proj_h, out,
    acc, stats, q_own, fresh, value_up, out_proj, acc_sem, in_sem, sent, sent_st, got, got_st, own, own_st, held, share, parts, z_send, z_recv, x_send, x_recv, o_send, o_recv,
):
    z = lax.axis_index("head")
    xfer = lax.axis_index("xfer")
    x, y, core = xfer // 8, (xfer // 2) % 4, xfer % 2
    groups = 8
    rank = acc.shape[2]
    half_rows = acc.shape[1]
    loads = [
        pltpu.make_async_copy(src, dst, in_sem.at[i])
        for i, (src, dst) in enumerate(
            ((stats_h, stats), (q_own_h, q_own), (fresh_h, fresh), (value_up_h, value_up), (out_proj_h, out_proj))
        )
    ]

    def load_acc(at):
        return pltpu.make_async_copy(acc_h.at[at], acc.at[at], acc_sem.at[at])

    loads[0].start()
    for distance in (4, 3, 5, 0, 2, 6, 1, 7):
        for half in (0, 1):
            load_acc(lax.rem(z + distance, groups) * 2 + half).start()
    for c in loads[1:]:
        c.start()

    def near(dx, dy, flip):
        c = 1 - core if flip else core
        return ((lax.rem(x + dx, 4) * 4 + lax.rem(y + dy, 4)) * 2 + c, z)

    def along(k):
        return (xfer, lax.rem(z + k, groups))

    barrier = pltpu.get_barrier_semaphore()
    peers = [along(k) for k in range(1, 8)]
    peers += [near(k, 0, False) for k in range(1, 4)] + [near(0, k, False) for k in range(1, 4)]
    peers += [near(0, 0, True)]
    for peer in peers:
        pl.semaphore_signal(barrier, inc=1, device_id=peer, device_id_type=MESH)
    pl.semaphore_wait(barrier, len(peers))

    def z_copies(way, half, hop):
        to = along(1 if way == 0 else 7)
        return [
            pltpu.make_async_remote_copy(
                src_ref=src.at[way, half, hop],
                dst_ref=dst.at[way, half, hop],
                send_sem=z_send.at[way, half, hop, i],
                recv_sem=z_recv.at[way, half, hop, i],
                device_id=to,
                device_id_type=MESH,
            )
            for i, (src, dst) in enumerate(((sent, got), (sent_st, got_st)))
        ]

    def index_of(way, half, distance):
        d = lax.rem(z + distance if way == 0 else z + groups - distance, groups)
        return d * 2 + half

    odd = lax.broadcasted_iota(jnp.int32, (half_rows, 128), 1) % 2

    def arrived(way, half, hop):
        for c in z_copies(way, half, hop):
            c.wait_recv()
        st = jnp.tile(got_st[way, half, hop], (half_rows // 8, 1)).T
        return st[:, 0:1], st[:, 1:2], got[way, half, hop].astype(jnp.float32)

    started = []

    def send_on(way, half, hop):
        at = index_of(way, half, 4 - hop)
        mine = stats[at]
        load_acc(at).wait()
        if hop == (0 if way == half else 1):
            sent[way, half, hop] = acc[at].astype(jnp.bfloat16)
            sent_st[way, half, hop] = mine.T[0:8]
        else:
            m, l, total = combine(*arrived(way, half, hop - 1), mine[:, 0:1], mine[:, 1:2], acc[at])
            sent[way, half, hop] = total.astype(jnp.bfloat16)
            sent_st[way, half, hop] = jnp.where(odd == 0, m, l).T[0:8]
        for c in z_copies(way, half, hop):
            c.start()
            started.append(c)

    def take_fresh(half):
        rows = slice(half * half_rows, (half + 1) * half_rows)
        s = (
            lax.dot_general(
                q_own[rows, :], fresh[...], (((1,), (1,)), ((), ())), preferred_element_type=jnp.float32
            )
            * scale
        )
        row = lax.broadcasted_iota(jnp.int32, s.shape, 0) // 8
        col = lax.broadcasted_iota(jnp.int32, s.shape, 1)
        s = jnp.where((row // STEPS == col // STEPS) & (col <= row), s, LOW)
        m = jnp.max(s, axis=1, keepdims=True)
        w = jnp.exp(s - m)
        l = jnp.sum(w, axis=1, keepdims=True)
        more = jnp.dot(w.astype(jnp.bfloat16), fresh[:, :rank], preferred_element_type=jnp.float32)
        at = z * 2 + half
        mine = stats[at]
        load_acc(at).wait()
        m, l, total = combine(m, l, more, mine[:, 0:1], mine[:, 1:2], acc[at])
        own[half] = total
        own_st[half] = jnp.where(odd == 0, m, l)

    loads[0].wait()
    send_on(0, 0, 0)
    send_on(1, 1, 0)
    send_on(0, 1, 1)
    send_on(1, 0, 1)
    loads[1].wait()
    loads[2].wait()
    take_fresh(0)
    take_fresh(1)
    for hop in (1, 2, 3):
        send_on(0, 0, hop)
        send_on(1, 1, hop)
        if hop < 3:
            send_on(0, 1, hop + 1)
            send_on(1, 0, hop + 1)

    def spread(half, kind, a, b, block, to):
        return pltpu.make_async_remote_copy(
            src_ref=held.at[half, block],
            dst_ref=held.at[half, block],
            send_sem=x_send.at[half, kind, a, b],
            recv_sem=x_recv.at[half, kind, a, b],
            device_id=to,
            device_id_type=MESH,
        )

    def block_of(half, a, b):
        dx, dy = (a, b) if half == 0 else (b, a)
        return (lax.rem(x + 4 - dx, 4) * 4 + lax.rem(y + 4 - dy, 4)) * 2

    def to_first(half, k):
        return near(k, 0, False) if half == 0 else near(0, k, False)

    def to_second(half, k):
        return near(0, k, False) if half == 0 else near(k, 0, False)

    def start(copy):
        copy.start()
        started.append(copy)

    def pass_second(half, a):
        for k in range(1, 4):
            start(spread(half, 1, a, k, block_of(half, a, 0) + core, to_second(half, k)))

    def pass_core(half, a, b):
        start(spread(half, 2, a, b, block_of(half, a, b) + core, near(0, 0, True)))

    loads[3].wait()
    for half in (1, 0):
        m, l, total = own_st[half][:, 0:1], own_st[half][:, 1:2], own[half]
        for way in (0, 1):
            m, l, total = combine(m, l, total, *arrived(way, half, 3))
        latent = (total / l).astype(jnp.bfloat16)
        heads = half_rows // fresh.shape[0]
        for h in range(heads):
            full = jnp.dot(latent, value_up[half * heads + h], preferred_element_type=jnp.float32)
            picked = full.reshape(fresh.shape[0], heads, -1)[:, h, :]
            width = picked.shape[1]
            held[half, xfer, :, h * width : (h + 1) * width] = picked.astype(jnp.bfloat16)
        for k in range(1, 4):
            start(spread(half, 0, 0, k, xfer, to_first(half, k)))
        pass_second(half, 0)
        pass_core(half, 0, 0)
    for a in range(1, 4):
        for half in (1, 0):
            spread(half, 0, 0, a, xfer, near(0, 0, True)).wait_recv()
            pass_second(half, a)
            pass_core(half, a, 0)
    for a in range(4):
        for b in range(1, 4):
            for half in (1, 0):
                spread(half, 1, a, b, xfer, near(0, 0, True)).wait_recv()
                pass_core(half, a, b)
    for half in (1, 0):
        for a in range(4):
            for b in range(4):
                spread(half, 2, a, b, xfer, near(0, 0, True)).wait_recv()

    loads[4].wait()
    depth = held.shape[3]
    total = None
    for half in (0, 1):
        left = held[half].reshape(-1, depth)
        right = out_proj[:, half * depth : (half + 1) * depth]
        piece = lax.dot_general(left, right, (((1,), (1,)), ((), ())), preferred_element_type=jnp.float32)
        total = piece if total is None else total + piece
    parts[...] = total.reshape(parts.shape)

    def final(k):
        return pltpu.make_async_remote_copy(
            src_ref=share.at[0, k],
            dst_ref=share.at[1, k],
            send_sem=o_send.at[k],
            recv_sem=o_recv.at[k],
            device_id=along(k),
            device_id_type=MESH,
        )

    for k in (4, 3, 5, 2, 6, 1, 7):
        share[0, k] = parts[lax.rem(z + k, groups)].astype(jnp.bfloat16)
        start(final(k))
    done = parts[z]
    for k in (1, 7, 2, 6, 3, 5, 4):
        final(k).wait_recv()
        done += share[1, k].astype(jnp.float32)
    out[...] = done.astype(jnp.bfloat16)
    for c in started:
        c.wait_send()


def finish(acc, stats, q_own, fresh, value_up, out_proj, owners, groups, scale):
    vmem = pl.BlockSpec(memory_space=pltpu.VMEM)
    operands = (acc, stats, q_own, fresh, value_up, out_proj)
    rows = fresh.shape[0]
    half_rows, rank = acc.shape[1:]
    width, depth = out_proj.shape
    piece = owners * rows // groups
    dma = pltpu.SemaphoreType.DMA
    return pl.pallas_call(
        functools.partial(finish_kernel, scale),
        in_specs=[pl.BlockSpec(memory_space=pl.ANY)] * 6,
        out_specs=vmem,
        out_shape=jax.ShapeDtypeStruct((piece, width), jnp.bfloat16),
        scratch_shapes=[
            *(pltpu.VMEM(a.shape, a.dtype) for a in operands),
            dma((2 * groups,)),
            dma((5,)),
            pltpu.VMEM((2, 2, 4, half_rows, rank), jnp.bfloat16),
            pltpu.VMEM((2, 2, 4, 8, 128), jnp.float32),
            pltpu.VMEM((2, 2, 4, half_rows, rank), jnp.bfloat16),
            pltpu.VMEM((2, 2, 4, 8, 128), jnp.float32),
            pltpu.VMEM((2, half_rows, rank), jnp.float32),
            pltpu.VMEM((2, half_rows, 128), jnp.float32),
            pltpu.VMEM((2, owners, rows, depth // 2), jnp.bfloat16),
            pltpu.VMEM((2, groups, piece, width), jnp.bfloat16),
            pltpu.VMEM((groups, piece, width), jnp.float32),
            dma((2, 2, 4, 2)),
            dma((2, 2, 4, 2)),
            dma((2, 3, 4, 4)),
            dma((2, 3, 4, 4)),
            dma((groups,)),
            dma((groups,)),
        ],
        compiler_params=pltpu.CompilerParams(
            collective_id=1, has_side_effects=True, vmem_limit_bytes=56 * MIB
        ),
    )(*operands)


def body(
    kv_pool, lengths, start_device, page_table, queries, new_latent, key_up, value_up, out_proj
):
    owners = lax.axis_size("xfer")
    groups = lax.axis_size("head")
    latent = kv_pool.shape[2]
    lat_rank = value_up.shape[1]
    row_count, heads = queries.shape[:2]
    score_scale = queries.shape[2] ** (-0.5)
    half_rows = row_count * heads // 2
    device = lax.axis_index("xfer") * groups + lax.axis_index("head")
    nth = (device - start_device) % (owners * groups)
    here = nth * kv_pool.shape[1] < lengths
    column = jnp.arange(page_table.shape[1], dtype=jnp.int32)
    picked = (column[None, :] == nth[:, None]) & here[:, None]
    chosen = jnp.where(picked, page_table, 0).reshape(owners, -1, page_table.shape[1]).sum(axis=(1, 2))
    pages, q_own = prepare(chosen, kv_pool, queries, key_up)
    keys, every = exchange(pages, q_own.reshape(2, half_rows, latent), groups)
    every = every.reshape(groups * 2, half_rows, latent)
    acc, stats = attend(lengths, start_device, every, keys, lengths.shape[0] // owners, lat_rank, score_scale)
    return finish(acc, stats, q_own, new_latent, value_up, out_proj.T, owners, groups, score_scale)


def solution(mesh):
    in_specs = (
        P(("xfer", "head"), None, None),
        P(),
        P(),
        P(),
        P("xfer", "head", None),
        P("xfer", None),
        P("head", None, None),
        P("head", None, None),
        P("head", "xfer"),
    )
    out_specs = P("head", "xfer")
    return jax.shard_map(body, mesh=mesh, in_specs=in_specs, out_specs=out_specs, check_vma=False)
```

```python
import functools

import jax
import jax.numpy as jnp
from jax import lax
from jax.experimental import pallas as pl
from jax.experimental.pallas import tpu as pltpu
from jax.sharding import PartitionSpec as P

MESH = pl.DeviceIdType.MESH
STEPS = 2
LOW = -1e30
FLOOR = -1e29
BLOCK = 512
MIB = 1024 * 1024


FAR = ((2, 2), (2, 1), (1, 2), (2, 3), (3, 2), (2, 0), (0, 2), (1, 1), (3, 3), (1, 3), (3, 1), (1, 0), (3, 0), (0, 1), (0, 3))
OFFSETS = tuple((*d, 0) for d in FAR) + tuple((*d, 1) for d in FAR) + ((0, 0, 1),)


def prepare_kernel(chosen, pool, queries, key_up_h, pages, q_own, raw, packed, key_up, sems, out_sems, up_sem, nope_s, wide_s):
    load_up = pltpu.make_async_copy(key_up_h, key_up, up_sem.at[0])

    def fetch(o, slot):
        return pltpu.make_async_copy(pool.at[slot], raw.at[o], sems.at[o])

    def store(o):
        return pltpu.make_async_copy(packed.at[o], pages.at[o], out_sems.at[o])

    def begin(o, c):
        fetch(o, chosen[o]).start()
        return c

    page = pool.shape[1]

    def pack(o, c):
        fetch(o, 0).wait()
        for i in range(rank // 128):
            packed[o, i * page : (i + 1) * page, :] = raw[o, :, i * 128 : (i + 1) * 128]
        top, low = raw[o, : page // 2, rank:], raw[o, page // 2 :, rank:]
        packed[o, rank // 128 * page :, :] = jnp.concatenate([top, low], axis=1)
        store(o).start()
        return c

    def end(o, c):
        store(o).wait()
        return c

    lax.fori_loop(0, pages.shape[0], begin, 0)
    load_up.start()
    rows, heads, width = queries.shape
    nope, rank = key_up.shape[1:]
    half = heads // 2
    flat = queries[...].reshape(rows * heads, width).astype(jnp.float32)
    nope_s[...] = flat[:, :nope]
    rope = flat[:, nope:].reshape(rows, 2, half, width - nope)
    lax.fori_loop(0, pages.shape[0], pack, 0)
    load_up.wait()
    for h in range(heads):
        mine = nope_s[pl.ds(h, rows, stride=heads), :].astype(jnp.bfloat16)
        full = jnp.dot(mine, key_up[h], preferred_element_type=jnp.float32)
        at = pl.ds((h // half) * rows * half + h % half, rows, stride=half)
        for c in range(rank // 128):
            wide_s[c, at, :] = full[:, c * 128 : (c + 1) * 128]
    for c in range(rank // 128):
        q_own[:, c * 128 : (c + 1) * 128] = wide_s[c].astype(jnp.bfloat16)
    for i in range(2):
        part = rope[:, i].reshape(rows * half, width - nope)
        q_own[i * rows * half : (i + 1) * rows * half, rank:] = part.astype(jnp.bfloat16)
    lax.fori_loop(0, pages.shape[0], end, 0)


def prepare(chosen, pool, queries, key_up):
    n = chosen.shape[0]
    rows, heads, width = queries.shape
    nope, rank = key_up.shape[1:]
    page, latent = pool.shape[1:]
    vmem = pl.BlockSpec(memory_space=pltpu.VMEM)
    smem = pl.BlockSpec(memory_space=pltpu.SMEM)
    hbm = pl.BlockSpec(memory_space=pl.ANY)
    tall = page * latent // 128
    dma = pltpu.SemaphoreType.DMA
    return pl.pallas_call(
        prepare_kernel,
        in_specs=[smem, hbm, vmem, hbm],
        out_specs=[hbm, vmem],
        out_shape=[
            jax.ShapeDtypeStruct((n, tall, 128), pool.dtype),
            jax.ShapeDtypeStruct((rows * heads, rank + width - nope), queries.dtype),
        ],
        scratch_shapes=[
            pltpu.VMEM((n, page, latent), pool.dtype),
            pltpu.VMEM((n, tall, 128), pool.dtype),
            pltpu.VMEM(key_up.shape, key_up.dtype),
            dma((n,)),
            dma((n,)),
            dma((1,)),
            pltpu.VMEM((rows * heads, nope), jnp.float32),
            pltpu.VMEM((rank // 128, rows * heads, 128), jnp.float32),
        ],
        compiler_params=pltpu.CompilerParams(vmem_limit_bytes=56 * MIB),
    )(chosen, pool, queries, key_up)


def exchange_kernel(pages, q_own, keys, q_all, q_s, page_s, p_send, p_recv, z_send, z_recv, own_sem):
    z = lax.axis_index("head")
    xfer = lax.axis_index("xfer")
    x, y, core = xfer // 8, (xfer // 2) % 4, xfer % 2
    groups = q_all.shape[0]

    def at(offset):
        dx, dy, dc = offset
        return (lax.rem(x + dx, 4) * 4 + lax.rem(y + dy, 4)) * 2 + lax.rem(core + dc, 2)

    mine = [
        pltpu.make_async_copy(q_own, q_s, own_sem.at[0]),
        pltpu.make_async_copy(pages.at[xfer], page_s, own_sem.at[1]),
    ]
    for c in mine:
        c.start()
    right, left = (xfer, lax.rem(z + 1, groups)), (xfer, lax.rem(z + groups - 1, groups))
    barrier = pltpu.get_barrier_semaphore()
    peers = [right, left] + [(at(offset), z) for offset in OFFSETS]
    for peer in peers:
        pl.semaphore_signal(barrier, inc=1, device_id=peer, device_id_type=MESH)
    pl.semaphore_wait(barrier, len(peers))

    def hop(way, j):
        block = lax.rem(z + groups - (j - 1), groups) if way == 0 else lax.rem(z + j - 1, groups)
        src, dst = (q_s if j == 1 else q_all.at[block]), q_all.at[block]
        if j == groups // 2:
            src, dst = src.at[way], dst.at[way]
        return pltpu.make_async_remote_copy(
            src_ref=src,
            dst_ref=dst,
            send_sem=z_send.at[way, j],
            recv_sem=z_recv.at[way, j],
            device_id=right if way == 0 else left,
            device_id_type=MESH,
        )

    def page(i, offset):
        to = at(offset)
        return pltpu.make_async_remote_copy(
            src_ref=pages.at[to],
            dst_ref=keys.at[xfer],
            send_sem=p_send.at[i],
            recv_sem=p_recv.at[i],
            device_id=(to, z),
            device_id_type=MESH,
        )

    hops = [hop(way, j) for j in range(1, groups // 2 + 1) for way in (0, 1)]
    copies = [page(i, offset) for i, offset in enumerate(OFFSETS)]
    for c in mine:
        c.wait()
    for c in hops[:2] + copies:
        c.start()
    mine = [
        pltpu.make_async_copy(q_s, q_all.at[z], own_sem.at[2]),
        pltpu.make_async_copy(page_s, keys.at[xfer], own_sem.at[3]),
    ]
    for c in mine:
        c.start()
    for j in range(1, groups // 2):
        for way in (0, 1):
            hops[(j - 1) * 2 + way].wait_recv()
            hops[j * 2 + way].start()
    for c in hops[-2:]:
        c.wait_recv()
    for c in copies:
        c.wait_recv()
    for c in mine:
        c.wait()
    for c in hops + copies:
        c.wait_send()


def exchange(pages, q_own, groups):
    hbm = pl.BlockSpec(memory_space=pl.ANY)
    dma = pltpu.SemaphoreType.DMA
    n = pages.shape[0]
    return pl.pallas_call(
        exchange_kernel,
        in_specs=[hbm, hbm],
        out_specs=[hbm, hbm],
        out_shape=[
            jax.ShapeDtypeStruct(pages.shape, pages.dtype),
            jax.ShapeDtypeStruct((groups, *q_own.shape), q_own.dtype),
        ],
        scratch_shapes=[
            pltpu.VMEM(q_own.shape, q_own.dtype),
            pltpu.VMEM(pages.shape[1:], pages.dtype),
            dma((n,)),
            dma((n,)),
            dma((2, 8)),
            dma((2, 8)),
            dma((4,)),
        ],
        compiler_params=pltpu.CompilerParams(
            collective_id=0, has_side_effects=True, vmem_limit_bytes=56 * MIB
        ),
    )(pages, q_own)


def combine(m_a, l_a, acc_a, m_b, l_b, acc_b):
    m = jnp.maximum(m_a, m_b)
    f_a, f_b = jnp.exp(m_a - m), jnp.exp(m_b - m)
    return m, l_a * f_a + l_b * f_b, acc_a * f_a + acc_b * f_b


def finish_kernel(
    scale, lengths, starts, keys_h, q_h, fresh_h, value_up_h, out_proj_h, out,
    packed, q, fresh, value_up, out_proj, in_sem, wide, narrow, bias, s_s, w_s, acc, stats, sent, sent_st, got, got_st, own, own_st, held, share, parts, z_send, z_recv, x_send, x_recv, o_send, o_recv,
):
    z = lax.axis_index("head")
    xfer = lax.axis_index("xfer")
    x, y, core = xfer // 8, (xfer // 2) % 4, xfer % 2
    groups = 8
    rank = acc.shape[2]
    half_rows = acc.shape[1]
    loads = [
        pltpu.make_async_copy(src, dst, in_sem.at[i])
        for i, (src, dst) in enumerate(
            ((keys_h, packed), (q_h, q), (fresh_h, fresh), (value_up_h, value_up), (out_proj_h, out_proj))
        )
    ]
    for c in loads:
        c.start()

    def near(dx, dy, flip):
        c = 1 - core if flip else core
        return ((lax.rem(x + dx, 4) * 4 + lax.rem(y + dy, 4)) * 2 + c, z)

    def along(k):
        return (xfer, lax.rem(z + k, groups))

    barrier = pltpu.get_barrier_semaphore()
    peers = [along(k) for k in range(1, 8)]
    peers += [near(k, 0, False) for k in range(1, 4)] + [near(0, k, False) for k in range(1, 4)]
    peers += [near(0, 0, True)]
    for peer in peers:
        pl.semaphore_signal(barrier, inc=1, device_id=peer, device_id_type=MESH)
    pl.semaphore_wait(barrier, len(peers))

    def z_copies(way, half, hop):
        to = along(1 if way == 0 else 7)
        return [
            pltpu.make_async_remote_copy(
                src_ref=src.at[way, half, hop],
                dst_ref=dst.at[way, half, hop],
                send_sem=z_send.at[way, half, hop, i],
                recv_sem=z_recv.at[way, half, hop, i],
                device_id=to,
                device_id_type=MESH,
            )
            for i, (src, dst) in enumerate(((sent, got), (sent_st, got_st)))
        ]

    def index_of(way, half, distance):
        d = lax.rem(z + distance if way == 0 else z + groups - distance, groups)
        return d * 2 + half

    odd = lax.broadcasted_iota(jnp.int32, (half_rows, 128), 1) % 2

    def arrived(way, half, hop):
        for c in z_copies(way, half, hop):
            c.wait_recv()
        st = jnp.tile(got_st[way, half, hop], (half_rows // 8, 1)).T
        return st[:, 0:1], st[:, 1:2], got[way, half, hop].astype(jnp.float32)

    started = []

    def send_on(way, half, hop):
        at = index_of(way, half, 4 - hop)
        mine = stats[at]
        if hop == (0 if way == half else 1):
            sent[way, half, hop] = acc[at].astype(jnp.bfloat16)
            sent_st[way, half, hop] = mine.T[0:8]
        else:
            m, l, total = combine(*arrived(way, half, hop - 1), mine[:, 0:1], mine[:, 1:2], acc[at])
            sent[way, half, hop] = total.astype(jnp.bfloat16)
            sent_st[way, half, hop] = jnp.where(odd == 0, m, l).T[0:8]
        for c in z_copies(way, half, hop):
            c.start()
            started.append(c)

    def take_fresh(half):
        s = (
            lax.dot_general(
                q[z * 2 + half], fresh[...], (((1,), (1,)), ((), ())), preferred_element_type=jnp.float32
            )
            * scale
        )
        row = lax.broadcasted_iota(jnp.int32, s.shape, 0) // 8
        col = lax.broadcasted_iota(jnp.int32, s.shape, 1)
        s = jnp.where((row // STEPS == col // STEPS) & (col <= row), s, LOW)
        m = jnp.max(s, axis=1, keepdims=True)
        w = jnp.exp(s - m)
        l = jnp.sum(w, axis=1, keepdims=True)
        more = jnp.dot(w.astype(jnp.bfloat16), fresh[:, :rank], preferred_element_type=jnp.float32)
        at = z * 2 + half
        mine = stats[at]
        m, l, total = combine(m, l, more, mine[:, 0:1], mine[:, 1:2], acc[at])
        own[half] = total
        own_st[half] = jnp.where(odd == 0, m, l)

    requests = lengths.shape[0] // 32
    page = packed.shape[1] * 128 // q.shape[2]
    keys = wide.shape[0]
    lane = lax.broadcasted_iota(jnp.int32, (1, keys), 1)

    def unpack():
        pages = packed.shape[0]
        for i in range(rank // 128):
            wide[:, i * 128 : (i + 1) * 128] = packed[:, i * page : (i + 1) * page].reshape(keys, 128)
        folded = packed[:, rank // 128 * page :]
        thin = narrow.shape[1]
        both = jnp.concatenate([folded[:, :, :thin], folded[:, :, thin:]], axis=1)
        narrow[...] = both.reshape(keys, thin)
        for r in range(requests):
            length, start = lengths[xfer * requests + r], starts[xfer * requests + r]
            at = (lane // page * groups + z - start) & (pages * groups - 1)
            seen = at * page + lane % page < length
            many = half_rows // requests
            bias[r * many : (r + 1) * many] = jnp.broadcast_to(jnp.where(seen, 0.0, LOW), (many, keys))

    def attend(distance):
        d = lax.rem(z + distance, groups)
        mine = q[pl.ds(d * 2, 2)].reshape(2 * half_rows, q.shape[2])
        top = None
        for b in range(0, keys, BLOCK):
            part = slice(b, b + BLOCK)
            s = lax.dot_general(
                mine[:, :rank], wide[part], (((1,), (1,)), ((), ())), preferred_element_type=jnp.float32
            )
            s += lax.dot_general(
                mine[:, rank:], narrow[part], (((1,), (1,)), ((), ())), preferred_element_type=jnp.float32
            )
            s = (s * scale).reshape(2, half_rows, BLOCK) + bias[:, part][None]
            s = s.reshape(2 * half_rows, BLOCK)
            s_s[:, part] = s
            most = jnp.max(s, axis=1, keepdims=True)
            top = most if top is None else jnp.maximum(top, most)
        top = jnp.maximum(top, FLOOR)
        total = None
        for b in range(0, keys, BLOCK):
            part = slice(b, b + BLOCK)
            w = jnp.exp(s_s[:, part] - top)
            w_s[:, part] = w.astype(jnp.bfloat16)
            more = jnp.sum(w, axis=1, keepdims=True)
            total = more if total is None else total + more
        summed = jnp.dot(w_s[...], wide[...], preferred_element_type=jnp.float32)
        acc[pl.ds(d * 2, 2)] = summed.reshape(2, half_rows, rank)
        both = jnp.where(lax.broadcasted_iota(jnp.int32, (2 * half_rows, 128), 1) % 2 == 0, top, total)
        stats[pl.ds(d * 2, 2)] = both.reshape(2, half_rows, 128)

    loads[0].wait()
    unpack()
    loads[1].wait()
    attend(4)
    send_on(0, 0, 0)
    send_on(1, 1, 0)
    for hop in (1, 2, 3):
        attend(4 - hop)
        if hop == 1:
            send_on(0, 1, 1)
            attend(4 + hop)
            send_on(1, 0, 1)
            send_on(0, 0, 1)
            send_on(1, 1, 1)
        else:
            send_on(0, 1, hop)
            send_on(0, 0, hop)
            attend(4 + hop)
            send_on(1, 0, hop)
            send_on(1, 1, hop)
    attend(0)
    loads[2].wait()
    take_fresh(0)
    take_fresh(1)

    def spread(half, kind, a, b, block, to):
        return pltpu.make_async_remote_copy(
            src_ref=held.at[half, block],
            dst_ref=held.at[half, block],
            send_sem=x_send.at[half, kind, a, b],
            recv_sem=x_recv.at[half, kind, a, b],
            device_id=to,
            device_id_type=MESH,
        )

    def block_of(half, a, b):
        dx, dy = (a, b) if half == 0 else (b, a)
        return (lax.rem(x + 4 - dx, 4) * 4 + lax.rem(y + 4 - dy, 4)) * 2

    def to_first(half, k):
        return near(k, 0, False) if half == 0 else near(0, k, False)

    def to_second(half, k):
        return near(0, k, False) if half == 0 else near(k, 0, False)

    def start(copy):
        copy.start()
        started.append(copy)

    def pass_second(half, a):
        for k in range(1, 4):
            start(spread(half, 1, a, k, block_of(half, a, 0) + core, to_second(half, k)))

    def pass_core(half, a, b):
        start(spread(half, 2, a, b, block_of(half, a, b) + core, near(0, 0, True)))

    loads[3].wait()
    for half in (1, 0):
        m, l, total = own_st[half][:, 0:1], own_st[half][:, 1:2], own[half]
        for way in (0, 1):
            m, l, total = combine(m, l, total, *arrived(way, half, 3))
        latent = (total / l).astype(jnp.bfloat16)
        heads = half_rows // fresh.shape[0]
        for h in range(heads):
            full = jnp.dot(latent, value_up[half * heads + h], preferred_element_type=jnp.float32)
            picked = full.reshape(fresh.shape[0], heads, -1)[:, h, :]
            width = picked.shape[1]
            held[half, xfer, :, h * width : (h + 1) * width] = picked.astype(jnp.bfloat16)
        for k in range(1, 4):
            start(spread(half, 0, 0, k, xfer, to_first(half, k)))
        pass_second(half, 0)
        pass_core(half, 0, 0)
    for a in range(1, 4):
        for half in (1, 0):
            spread(half, 0, 0, a, xfer, near(0, 0, True)).wait_recv()
            pass_second(half, a)
            pass_core(half, a, 0)
    for a in range(4):
        for b in range(1, 4):
            for half in (1, 0):
                spread(half, 1, a, b, xfer, near(0, 0, True)).wait_recv()
                pass_core(half, a, b)
    for half in (1, 0):
        for a in range(4):
            for b in range(4):
                spread(half, 2, a, b, xfer, near(0, 0, True)).wait_recv()

    loads[4].wait()
    depth = held.shape[3]
    total = None
    for half in (0, 1):
        left = held[half].reshape(-1, depth)
        right = out_proj[:, half * depth : (half + 1) * depth]
        piece = lax.dot_general(left, right, (((1,), (1,)), ((), ())), preferred_element_type=jnp.float32)
        total = piece if total is None else total + piece
    parts[...] = total.reshape(parts.shape)

    def final(k):
        return pltpu.make_async_remote_copy(
            src_ref=share.at[0, k],
            dst_ref=share.at[1, k],
            send_sem=o_send.at[k],
            recv_sem=o_recv.at[k],
            device_id=along(k),
            device_id_type=MESH,
        )

    for k in (4, 3, 5, 2, 6, 1, 7):
        share[0, k] = parts[lax.rem(z + k, groups)].astype(jnp.bfloat16)
        start(final(k))
    done = parts[z]
    for k in (1, 7, 2, 6, 3, 5, 4):
        final(k).wait_recv()
        done += share[1, k].astype(jnp.float32)
    out[...] = done.astype(jnp.bfloat16)
    for c in started:
        c.wait_send()


def finish(lengths, starts, keys, q, fresh, value_up, out_proj, owners, groups, scale):
    vmem = pl.BlockSpec(memory_space=pltpu.VMEM)
    operands = (keys, q, fresh, value_up, out_proj)
    smem = pl.BlockSpec(memory_space=pltpu.SMEM)
    rows = fresh.shape[0]
    half_rows, latent = q.shape[1:]
    rank = value_up.shape[1]
    tokens = keys.shape[0] * keys.shape[1] * 128 // latent
    width, depth = out_proj.shape
    piece = owners * rows // groups
    dma = pltpu.SemaphoreType.DMA
    return pl.pallas_call(
        functools.partial(finish_kernel, scale),
        in_specs=[smem, smem] + [pl.BlockSpec(memory_space=pl.ANY)] * 5,
        out_specs=vmem,
        out_shape=jax.ShapeDtypeStruct((piece, width), jnp.bfloat16),
        scratch_shapes=[
            *(pltpu.VMEM(a.shape, a.dtype) for a in operands),
            dma((5,)),
            pltpu.VMEM((tokens, rank), jnp.bfloat16),
            pltpu.VMEM((tokens, latent - rank), jnp.bfloat16),
            pltpu.VMEM((half_rows, tokens), jnp.float32),
            pltpu.VMEM((2 * half_rows, tokens), jnp.float32),
            pltpu.VMEM((2 * half_rows, tokens), jnp.bfloat16),
            pltpu.VMEM((2 * groups, half_rows, rank), jnp.float32),
            pltpu.VMEM((2 * groups, half_rows, 128), jnp.float32),
            pltpu.VMEM((2, 2, 4, half_rows, rank), jnp.bfloat16),
            pltpu.VMEM((2, 2, 4, 8, 128), jnp.float32),
            pltpu.VMEM((2, 2, 4, half_rows, rank), jnp.bfloat16),
            pltpu.VMEM((2, 2, 4, 8, 128), jnp.float32),
            pltpu.VMEM((2, half_rows, rank), jnp.float32),
            pltpu.VMEM((2, half_rows, 128), jnp.float32),
            pltpu.VMEM((2, owners, rows, depth // 2), jnp.bfloat16),
            pltpu.VMEM((2, groups, piece, width), jnp.bfloat16),
            pltpu.VMEM((groups, piece, width), jnp.float32),
            dma((2, 2, 4, 2)),
            dma((2, 2, 4, 2)),
            dma((2, 3, 4, 4)),
            dma((2, 3, 4, 4)),
            dma((groups,)),
            dma((groups,)),
        ],
        compiler_params=pltpu.CompilerParams(
            collective_id=1, has_side_effects=True, vmem_limit_bytes=56 * MIB
        ),
    )(lengths, starts, *operands)


def body(
    kv_pool, lengths, start_device, page_table, queries, new_latent, key_up, value_up, out_proj
):
    owners = lax.axis_size("xfer")
    groups = lax.axis_size("head")
    latent = kv_pool.shape[2]
    lat_rank = value_up.shape[1]
    row_count, heads = queries.shape[:2]
    score_scale = queries.shape[2] ** (-0.5)
    half_rows = row_count * heads // 2
    device = lax.axis_index("xfer") * groups + lax.axis_index("head")
    nth = (device - start_device) % (owners * groups)
    here = nth * kv_pool.shape[1] < lengths
    column = jnp.arange(page_table.shape[1], dtype=jnp.int32)
    picked = (column[None, :] == nth[:, None]) & here[:, None]
    chosen = jnp.where(picked, page_table, 0).reshape(owners, -1, page_table.shape[1]).sum(axis=(1, 2))
    pages, q_own = prepare(chosen, kv_pool, queries, key_up)
    keys, every = exchange(pages, q_own.reshape(2, half_rows, latent), groups)
    every = every.reshape(groups * 2, half_rows, latent)
    return finish(
        lengths, start_device, keys, every, new_latent, value_up, out_proj.T, owners, groups, score_scale
    )


def solution(mesh):
    in_specs = (
        P(("xfer", "head"), None, None),
        P(),
        P(),
        P(),
        P("xfer", "head", None),
        P("xfer", None),
        P("head", None, None),
        P("head", None, None),
        P("head", "xfer"),
    )
    out_specs = P("head", "xfer")
    return jax.shard_map(body, mesh=mesh, in_specs=in_specs, out_specs=out_specs, check_vma=False)
```

```python
import functools

import jax
import jax.numpy as jnp
from jax import lax
from jax.experimental import pallas as pl
from jax.experimental.pallas import tpu as pltpu
from jax.sharding import PartitionSpec as P

MESH = pl.DeviceIdType.MESH
STEPS = 2
LOW = -1e30
FLOOR = -1e29
BLOCK = 512
MIB = 1024 * 1024


FAR = ((2, 2), (2, 1), (1, 2), (2, 3), (3, 2), (2, 0), (0, 2), (1, 1), (3, 3), (1, 3), (3, 1), (1, 0), (3, 0), (0, 1), (0, 3))
OFFSETS = tuple((*d, 0) for d in FAR) + tuple((*d, 1) for d in FAR) + ((0, 0, 1),)


def prepare_kernel(chosen, pool, queries, key_up_h, pages, q_own, raw, packed, key_up, sems, out_sems, up_sem, nope_s, wide_s):
    load_up = pltpu.make_async_copy(key_up_h, key_up, up_sem.at[0])

    def fetch(o, slot):
        return pltpu.make_async_copy(pool.at[slot], raw.at[o], sems.at[o])

    def store(o):
        return pltpu.make_async_copy(packed.at[o], pages.at[o], out_sems.at[o])

    def begin(o, c):
        fetch(o, chosen[o]).start()
        return c

    page = pool.shape[1]

    def pack(o, c):
        fetch(o, 0).wait()
        for i in range(rank // 128):
            packed[o, i * page : (i + 1) * page, :] = raw[o, :, i * 128 : (i + 1) * 128]
        top, low = raw[o, : page // 2, rank:], raw[o, page // 2 :, rank:]
        packed[o, rank // 128 * page :, :] = jnp.concatenate([top, low], axis=1)
        store(o).start()
        return c

    def end(o, c):
        store(o).wait()
        return c

    lax.fori_loop(0, pages.shape[0], begin, 0)
    load_up.start()
    rows, heads, width = queries.shape
    nope, rank = key_up.shape[1:]
    half = heads // 2
    flat = queries[...].reshape(rows * heads, width).astype(jnp.float32)
    nope_s[...] = flat[:, :nope]
    rope = flat[:, nope:].reshape(rows, 2, half, width - nope)
    lax.fori_loop(0, pages.shape[0], pack, 0)
    load_up.wait()
    for h in range(heads):
        mine = nope_s[pl.ds(h, rows, stride=heads), :].astype(jnp.bfloat16)
        full = jnp.dot(mine, key_up[h], preferred_element_type=jnp.float32)
        at = pl.ds((h // half) * rows * half + h % half, rows, stride=half)
        for c in range(rank // 128):
            wide_s[c, at, :] = full[:, c * 128 : (c + 1) * 128]
    for c in range(rank // 128):
        q_own[:, c * 128 : (c + 1) * 128] = wide_s[c].astype(jnp.bfloat16)
    for i in range(2):
        part = rope[:, i].reshape(rows * half, width - nope)
        q_own[i * rows * half : (i + 1) * rows * half, rank:] = part.astype(jnp.bfloat16)
    lax.fori_loop(0, pages.shape[0], end, 0)


def prepare(chosen, pool, queries, key_up):
    n = chosen.shape[0]
    rows, heads, width = queries.shape
    nope, rank = key_up.shape[1:]
    page, latent = pool.shape[1:]
    vmem = pl.BlockSpec(memory_space=pltpu.VMEM)
    smem = pl.BlockSpec(memory_space=pltpu.SMEM)
    hbm = pl.BlockSpec(memory_space=pl.ANY)
    tall = page * latent // 128
    dma = pltpu.SemaphoreType.DMA
    return pl.pallas_call(
        prepare_kernel,
        in_specs=[smem, hbm, vmem, hbm],
        out_specs=[hbm, vmem],
        out_shape=[
            jax.ShapeDtypeStruct((n, tall, 128), pool.dtype),
            jax.ShapeDtypeStruct((rows * heads, rank + width - nope), queries.dtype),
        ],
        scratch_shapes=[
            pltpu.VMEM((n, page, latent), pool.dtype),
            pltpu.VMEM((n, tall, 128), pool.dtype),
            pltpu.VMEM(key_up.shape, key_up.dtype),
            dma((n,)),
            dma((n,)),
            dma((1,)),
            pltpu.VMEM((rows * heads, nope), jnp.float32),
            pltpu.VMEM((rank // 128, rows * heads, 128), jnp.float32),
        ],
        compiler_params=pltpu.CompilerParams(vmem_limit_bytes=56 * MIB),
    )(chosen, pool, queries, key_up)


def combine(m_a, l_a, acc_a, m_b, l_b, acc_b):
    m = jnp.maximum(m_a, m_b)
    f_a, f_b = jnp.exp(m_a - m), jnp.exp(m_b - m)
    return m, l_a * f_a + l_b * f_b, acc_a * f_a + acc_b * f_b


def finish_kernel(
    scale, lengths, starts, pages_h, q_own_h, fresh_h, value_up_h, out_proj_h, out,
    packed, q, fresh, value_up, out_proj, in_sem, wide, narrow, bias, s_s, w_s, acc, stats, sent, sent_st, got, got_st, own, own_st, held, share, parts, z_send, z_recv, x_send, x_recv, o_send, o_recv,
    p_send, p_recv, r_send, r_recv,
):
    z = lax.axis_index("head")
    xfer = lax.axis_index("xfer")
    x, y, core = xfer // 8, (xfer // 2) % 4, xfer % 2
    groups = 8
    rank = acc.shape[2]
    half_rows = acc.shape[1]
    loads = [
        pltpu.make_async_copy(src, dst, in_sem.at[i])
        for i, (src, dst) in enumerate(
            (
                (pages_h.at[xfer], packed.at[xfer]),
                (q_own_h, q.at[pl.ds(z * 2, 2)]),
                (fresh_h, fresh),
                (value_up_h, value_up),
                (out_proj_h, out_proj),
            )
        )
    ]
    for c in loads:
        c.start()

    def near(dx, dy, flip):
        c = 1 - core if flip else core
        return ((lax.rem(x + dx, 4) * 4 + lax.rem(y + dy, 4)) * 2 + c, z)

    def along(k):
        return (xfer, lax.rem(z + k, groups))

    def owner_at(offset, sign):
        dx, dy, dc = offset
        return (lax.rem(x + 4 + sign * dx, 4) * 4 + lax.rem(y + 4 + sign * dy, 4)) * 2 + lax.rem(core + dc, 2)

    barrier = pltpu.get_barrier_semaphore()
    peers = [along(k) for k in range(1, 8)] + [(owner_at(offset, 1), z) for offset in OFFSETS]
    for peer in peers:
        pl.semaphore_signal(barrier, inc=1, device_id=peer, device_id_type=MESH)
    pl.semaphore_wait(barrier, len(peers))

    def hop_of(way, j):
        block = lax.rem(z + groups - (j - 1), groups) if way == 0 else lax.rem(z + j - 1, groups)
        part = q.at[block * 2 + way] if j == groups // 2 else q.at[pl.ds(block * 2, 2)]
        return pltpu.make_async_remote_copy(
            src_ref=part,
            dst_ref=part,
            send_sem=r_send.at[way, j],
            recv_sem=r_recv.at[way, j],
            device_id=along(1 if way == 0 else 7),
            device_id_type=MESH,
        )

    def page_to(i, offset):
        to = owner_at(offset, 1)
        return pltpu.make_async_remote_copy(
            src_ref=pages_h.at[to],
            dst_ref=packed.at[xfer],
            send_sem=p_send.at[i],
            recv_sem=p_recv.at[i],
            device_id=(to, z),
            device_id_type=MESH,
        )

    hops = [hop_of(way, j) for j in range(1, groups // 2 + 1) for way in (0, 1)]
    page_copies = [page_to(i, offset) for i, offset in enumerate(OFFSETS)]
    loads[1].wait()
    for c in hops[:2] + page_copies:
        c.start()

    def z_copies(way, half, hop):
        to = along(1 if way == 0 else 7)
        return [
            pltpu.make_async_remote_copy(
                src_ref=src.at[way, half, hop],
                dst_ref=dst.at[way, half, hop],
                send_sem=z_send.at[way, half, hop, i],
                recv_sem=z_recv.at[way, half, hop, i],
                device_id=to,
                device_id_type=MESH,
            )
            for i, (src, dst) in enumerate(((sent, got), (sent_st, got_st)))
        ]

    def index_of(way, half, distance):
        d = lax.rem(z + distance if way == 0 else z + groups - distance, groups)
        return d * 2 + half

    odd = lax.broadcasted_iota(jnp.int32, (half_rows, 128), 1) % 2

    def arrived(way, half, hop):
        for c in z_copies(way, half, hop):
            c.wait_recv()
        st = jnp.tile(got_st[way, half, hop], (half_rows // 8, 1)).T
        return st[:, 0:1], st[:, 1:2], got[way, half, hop].astype(jnp.float32)

    started = hops + page_copies

    def send_on(way, half, hop):
        at = index_of(way, half, 4 - hop)
        mine = stats[at]
        if hop == (0 if way == half else 1):
            sent[way, half, hop] = acc[at].astype(jnp.bfloat16)
            sent_st[way, half, hop] = mine.T[0:8]
        else:
            m, l, total = combine(*arrived(way, half, hop - 1), mine[:, 0:1], mine[:, 1:2], acc[at])
            sent[way, half, hop] = total.astype(jnp.bfloat16)
            sent_st[way, half, hop] = jnp.where(odd == 0, m, l).T[0:8]
        for c in z_copies(way, half, hop):
            c.start()
            started.append(c)

    def take_fresh(half):
        s = (
            lax.dot_general(
                q[z * 2 + half], fresh[...], (((1,), (1,)), ((), ())), preferred_element_type=jnp.float32
            )
            * scale
        )
        row = lax.broadcasted_iota(jnp.int32, s.shape, 0) // 8
        col = lax.broadcasted_iota(jnp.int32, s.shape, 1)
        s = jnp.where((row // STEPS == col // STEPS) & (col <= row), s, LOW)
        m = jnp.max(s, axis=1, keepdims=True)
        w = jnp.exp(s - m)
        l = jnp.sum(w, axis=1, keepdims=True)
        more = jnp.dot(w.astype(jnp.bfloat16), fresh[:, :rank], preferred_element_type=jnp.float32)
        at = z * 2 + half
        mine = stats[at]
        m, l, total = combine(m, l, more, mine[:, 0:1], mine[:, 1:2], acc[at])
        own[half] = total
        own_st[half] = jnp.where(odd == 0, m, l)

    requests = lengths.shape[0] // 32
    page = packed.shape[1] * 128 // q.shape[2]
    keys = wide.shape[0]
    lane = lax.broadcasted_iota(jnp.int32, (1, keys), 1)

    def unpack(slot):
        to = pl.ds(pl.multiple_of(slot * page, page), page)
        for i in range(rank // 128):
            wide[to, i * 128 : (i + 1) * 128] = packed[slot, i * page : (i + 1) * page, :]
        folded = packed[slot, rank // 128 * page :, :]
        thin = narrow.shape[1]
        narrow[to] = jnp.concatenate([folded[:, :thin], folded[:, thin:]], axis=0)

    def hide():
        for r in range(requests):
            length, start = lengths[xfer * requests + r], starts[xfer * requests + r]
            at = (lane // page * groups + z - start) & (packed.shape[0] * groups - 1)
            seen = at * page + lane % page < length
            many = half_rows // requests
            bias[r * many : (r + 1) * many] = jnp.broadcast_to(jnp.where(seen, 0.0, LOW), (many, keys))

    def attend(distance):
        d = lax.rem(z + distance, groups)
        mine = q[pl.ds(d * 2, 2)].reshape(2 * half_rows, q.shape[2])
        top = None
        for b in range(0, keys, BLOCK):
            part = slice(b, b + BLOCK)
            s = lax.dot_general(
                mine[:, :rank], wide[part], (((1,), (1,)), ((), ())), preferred_element_type=jnp.float32
            )
            s += lax.dot_general(
                mine[:, rank:], narrow[part], (((1,), (1,)), ((), ())), preferred_element_type=jnp.float32
            )
            s = (s * scale).reshape(2, half_rows, BLOCK) + bias[:, part][None]
            s = s.reshape(2 * half_rows, BLOCK)
            s_s[:, part] = s
            most = jnp.max(s, axis=1, keepdims=True)
            top = most if top is None else jnp.maximum(top, most)
        top = jnp.maximum(top, FLOOR)
        total = None
        for b in range(0, keys, BLOCK):
            part = slice(b, b + BLOCK)
            w = jnp.exp(s_s[:, part] - top)
            w_s[:, part] = w.astype(jnp.bfloat16)
            more = jnp.sum(w, axis=1, keepdims=True)
            total = more if total is None else total + more
        summed = jnp.dot(w_s[...], wide[...], preferred_element_type=jnp.float32)
        acc[pl.ds(d * 2, 2)] = summed.reshape(2, half_rows, rank)
        both = jnp.where(lax.broadcasted_iota(jnp.int32, (2 * half_rows, 128), 1) % 2 == 0, top, total)
        stats[pl.ds(d * 2, 2)] = both.reshape(2, half_rows, 128)

    for j in range(1, groups // 2):
        for way in (0, 1):
            hops[(j - 1) * 2 + way].wait_recv()
            hops[j * 2 + way].start()
        if j == 1:
            hide()
    for c in hops[-2:]:
        c.wait_recv()
    loads[0].wait()
    unpack(xfer)
    for c, offset in zip(page_copies, OFFSETS):
        c.wait_recv()
        unpack(owner_at(offset, -1))
    attend(4)
    send_on(0, 0, 0)
    send_on(1, 1, 0)
    for hop in (1, 2, 3):
        attend(4 - hop)
        if hop == 1:
            send_on(0, 1, 1)
            attend(4 + hop)
            send_on(1, 0, 1)
            send_on(0, 0, 1)
            send_on(1, 1, 1)
        else:
            send_on(0, 1, hop)
            send_on(0, 0, hop)
            attend(4 + hop)
            send_on(1, 0, hop)
            send_on(1, 1, hop)
    attend(0)
    loads[2].wait()
    take_fresh(0)
    take_fresh(1)

    def spread(half, kind, a, b, block, to):
        return pltpu.make_async_remote_copy(
            src_ref=held.at[half, block],
            dst_ref=held.at[half, block],
            send_sem=x_send.at[half, kind, a, b],
            recv_sem=x_recv.at[half, kind, a, b],
            device_id=to,
            device_id_type=MESH,
        )

    def block_of(half, a, b):
        dx, dy = (a, b) if half == 0 else (b, a)
        return (lax.rem(x + 4 - dx, 4) * 4 + lax.rem(y + 4 - dy, 4)) * 2

    def to_first(half, k):
        return near(k, 0, False) if half == 0 else near(0, k, False)

    def to_second(half, k):
        return near(0, k, False) if half == 0 else near(k, 0, False)

    def start(copy):
        copy.start()
        started.append(copy)

    def pass_second(half, a):
        for k in range(1, 4):
            start(spread(half, 1, a, k, block_of(half, a, 0) + core, to_second(half, k)))

    def pass_core(half, a, b):
        start(spread(half, 2, a, b, block_of(half, a, b) + core, near(0, 0, True)))

    loads[3].wait()
    for half in (1, 0):
        m, l, total = own_st[half][:, 0:1], own_st[half][:, 1:2], own[half]
        for way in (0, 1):
            m, l, total = combine(m, l, total, *arrived(way, half, 3))
        latent = (total / l).astype(jnp.bfloat16)
        heads = half_rows // fresh.shape[0]
        for h in range(heads):
            full = jnp.dot(latent, value_up[half * heads + h], preferred_element_type=jnp.float32)
            picked = full.reshape(fresh.shape[0], heads, -1)[:, h, :]
            width = picked.shape[1]
            held[half, xfer, :, h * width : (h + 1) * width] = picked.astype(jnp.bfloat16)
        for k in range(1, 4):
            start(spread(half, 0, 0, k, xfer, to_first(half, k)))
        pass_second(half, 0)
        pass_core(half, 0, 0)
    for a in range(1, 4):
        for half in (1, 0):
            spread(half, 0, 0, a, xfer, near(0, 0, True)).wait_recv()
            pass_second(half, a)
            pass_core(half, a, 0)
    for a in range(4):
        for b in range(1, 4):
            for half in (1, 0):
                spread(half, 1, a, b, xfer, near(0, 0, True)).wait_recv()
                pass_core(half, a, b)
    for half in (1, 0):
        for a in range(4):
            for b in range(4):
                spread(half, 2, a, b, xfer, near(0, 0, True)).wait_recv()

    loads[4].wait()
    depth = held.shape[3]
    total = None
    for half in (0, 1):
        left = held[half].reshape(-1, depth)
        right = out_proj[:, half * depth : (half + 1) * depth]
        piece = lax.dot_general(left, right, (((1,), (1,)), ((), ())), preferred_element_type=jnp.float32)
        total = piece if total is None else total + piece
    parts[...] = total.reshape(parts.shape)

    def final(k):
        return pltpu.make_async_remote_copy(
            src_ref=share.at[0, k],
            dst_ref=share.at[1, k],
            send_sem=o_send.at[k],
            recv_sem=o_recv.at[k],
            device_id=along(k),
            device_id_type=MESH,
        )

    for k in (4, 3, 5, 2, 6, 1, 7):
        share[0, k] = parts[lax.rem(z + k, groups)].astype(jnp.bfloat16)
        start(final(k))
    done = parts[z]
    for k in (1, 7, 2, 6, 3, 5, 4):
        final(k).wait_recv()
        done += share[1, k].astype(jnp.float32)
    out[...] = done.astype(jnp.bfloat16)
    for c in started:
        c.wait_send()


def finish(lengths, starts, pages, q_own, fresh, value_up, out_proj, owners, groups, scale):
    vmem = pl.BlockSpec(memory_space=pltpu.VMEM)
    operands = (pages, q_own, fresh, value_up, out_proj)
    smem = pl.BlockSpec(memory_space=pltpu.SMEM)
    rows = fresh.shape[0]
    half_rows, latent = q_own.shape[1:]
    rank = value_up.shape[1]
    tokens = pages.shape[0] * pages.shape[1] * 128 // latent
    width, depth = out_proj.shape
    piece = owners * rows // groups
    dma = pltpu.SemaphoreType.DMA
    return pl.pallas_call(
        functools.partial(finish_kernel, scale),
        in_specs=[smem, smem] + [pl.BlockSpec(memory_space=pl.ANY)] * 5,
        out_specs=vmem,
        out_shape=jax.ShapeDtypeStruct((piece, width), jnp.bfloat16),
        scratch_shapes=[
            pltpu.VMEM(pages.shape, pages.dtype),
            pltpu.VMEM((2 * groups, half_rows, latent), q_own.dtype),
            *(pltpu.VMEM(a.shape, a.dtype) for a in operands[2:]),
            dma((5,)),
            pltpu.VMEM((tokens, rank), jnp.bfloat16),
            pltpu.VMEM((tokens, latent - rank), jnp.bfloat16),
            pltpu.VMEM((half_rows, tokens), jnp.float32),
            pltpu.VMEM((2 * half_rows, tokens), jnp.float32),
            pltpu.VMEM((2 * half_rows, tokens), jnp.bfloat16),
            pltpu.VMEM((2 * groups, half_rows, rank), jnp.float32),
            pltpu.VMEM((2 * groups, half_rows, 128), jnp.float32),
            pltpu.VMEM((2, 2, 4, half_rows, rank), jnp.bfloat16),
            pltpu.VMEM((2, 2, 4, 8, 128), jnp.float32),
            pltpu.VMEM((2, 2, 4, half_rows, rank), jnp.bfloat16),
            pltpu.VMEM((2, 2, 4, 8, 128), jnp.float32),
            pltpu.VMEM((2, half_rows, rank), jnp.float32),
            pltpu.VMEM((2, half_rows, 128), jnp.float32),
            pltpu.VMEM((2, owners, rows, depth // 2), jnp.bfloat16),
            pltpu.VMEM((2, groups, piece, width), jnp.bfloat16),
            pltpu.VMEM((groups, piece, width), jnp.float32),
            dma((2, 2, 4, 2)),
            dma((2, 2, 4, 2)),
            dma((2, 3, 4, 4)),
            dma((2, 3, 4, 4)),
            dma((groups,)),
            dma((groups,)),
            dma((owners,)),
            dma((owners,)),
            dma((2, 8)),
            dma((2, 8)),
        ],
        compiler_params=pltpu.CompilerParams(
            collective_id=0, has_side_effects=True, vmem_limit_bytes=56 * MIB
        ),
    )(lengths, starts, *operands)


def body(
    kv_pool, lengths, start_device, page_table, queries, new_latent, key_up, value_up, out_proj
):
    owners = lax.axis_size("xfer")
    groups = lax.axis_size("head")
    latent = kv_pool.shape[2]
    row_count, heads = queries.shape[:2]
    score_scale = queries.shape[2] ** (-0.5)
    device = lax.axis_index("xfer") * groups + lax.axis_index("head")
    nth = (device - start_device) % (owners * groups)
    here = nth * kv_pool.shape[1] < lengths
    column = jnp.arange(page_table.shape[1], dtype=jnp.int32)
    picked = (column[None, :] == nth[:, None]) & here[:, None]
    chosen = jnp.where(picked, page_table, 0).reshape(owners, -1, page_table.shape[1]).sum(axis=(1, 2))
    pages, q_own = prepare(chosen, kv_pool, queries, key_up)
    q_own = q_own.reshape(2, row_count * heads // 2, latent)
    return finish(
        lengths, start_device, pages, q_own, new_latent, value_up, out_proj.T, owners, groups, score_scale
    )


def solution(mesh):
    in_specs = (
        P(("xfer", "head"), None, None),
        P(),
        P(),
        P(),
        P("xfer", "head", None),
        P("xfer", None),
        P("head", None, None),
        P("head", None, None),
        P("head", "xfer"),
    )
    out_specs = P("head", "xfer")
    return jax.shard_map(body, mesh=mesh, in_specs=in_specs, out_specs=out_specs, check_vma=False)
```

```python
import functools

import jax
import jax.numpy as jnp
from jax import lax
from jax.experimental import pallas as pl
from jax.experimental.pallas import tpu as pltpu
from jax.sharding import PartitionSpec as P

MESH = pl.DeviceIdType.MESH
STEPS = 2
LOW = -1e30
FLOOR = -1e29
BLOCK = 512
MIB = 1024 * 1024


FAR = ((2, 2), (2, 1), (1, 2), (2, 3), (3, 2), (2, 0), (0, 2), (1, 1), (3, 3), (1, 3), (3, 1), (1, 0), (3, 0), (0, 1), (0, 3))
OFFSETS = tuple((*d, 0) for d in FAR) + tuple((*d, 1) for d in FAR) + ((0, 0, 1),)


def prepare_kernel(chosen, pool, queries, key_up_h, pages, q_own, raw, packed, key_up, sems, out_sems, up_sem, nope_s, wide_s):
    load_up = pltpu.make_async_copy(key_up_h, key_up, up_sem.at[0])

    def fetch(o, slot):
        return pltpu.make_async_copy(pool.at[slot], raw.at[o], sems.at[o])

    def store(o):
        return pltpu.make_async_copy(packed.at[o], pages.at[o], out_sems.at[o])

    def begin(o, c):
        fetch(o, chosen[o]).start()
        return c

    page = pool.shape[1]

    def pack(o, c):
        fetch(o, 0).wait()
        for i in range(rank // 128):
            packed[o, i * page : (i + 1) * page, :] = raw[o, :, i * 128 : (i + 1) * 128]
        top, low = raw[o, : page // 2, rank:], raw[o, page // 2 :, rank:]
        packed[o, rank // 128 * page :, :] = jnp.concatenate([top, low], axis=1)
        store(o).start()
        return c

    def end(o, c):
        store(o).wait()
        return c

    lax.fori_loop(0, pages.shape[0], begin, 0)
    load_up.start()
    rows, heads, width = queries.shape
    nope, rank = key_up.shape[1:]
    half = heads // 2
    flat = queries[...].reshape(rows * heads, width).astype(jnp.float32)
    nope_s[...] = flat[:, :nope]
    rope = flat[:, nope:].reshape(rows, 2, half, width - nope)
    lax.fori_loop(0, pages.shape[0], pack, 0)
    load_up.wait()
    for h in range(heads):
        mine = nope_s[pl.ds(h, rows, stride=heads), :].astype(jnp.bfloat16)
        full = jnp.dot(mine, key_up[h], preferred_element_type=jnp.float32)
        at = pl.ds((h // half) * rows * half + h % half, rows, stride=half)
        for c in range(rank // 128):
            wide_s[c, at, :] = full[:, c * 128 : (c + 1) * 128]
    for c in range(rank // 128):
        q_own[:, c * 128 : (c + 1) * 128] = wide_s[c].astype(jnp.bfloat16)
    for i in range(2):
        part = rope[:, i].reshape(rows * half, width - nope)
        q_own[i * rows * half : (i + 1) * rows * half, rank:] = part.astype(jnp.bfloat16)
    lax.fori_loop(0, pages.shape[0], end, 0)


def prepare(chosen, pool, queries, key_up):
    n = chosen.shape[0]
    rows, heads, width = queries.shape
    nope, rank = key_up.shape[1:]
    page, latent = pool.shape[1:]
    vmem = pl.BlockSpec(memory_space=pltpu.VMEM)
    smem = pl.BlockSpec(memory_space=pltpu.SMEM)
    hbm = pl.BlockSpec(memory_space=pl.ANY)
    tall = page * latent // 128
    dma = pltpu.SemaphoreType.DMA
    return pl.pallas_call(
        prepare_kernel,
        in_specs=[smem, hbm, vmem, hbm],
        out_specs=[hbm, vmem],
        out_shape=[
            jax.ShapeDtypeStruct((n, tall, 128), pool.dtype),
            jax.ShapeDtypeStruct((rows * heads, rank + width - nope), queries.dtype),
        ],
        scratch_shapes=[
            pltpu.VMEM((n, page, latent), pool.dtype),
            pltpu.VMEM((n, tall, 128), pool.dtype),
            pltpu.VMEM(key_up.shape, key_up.dtype),
            dma((n,)),
            dma((n,)),
            dma((1,)),
            pltpu.VMEM((rows * heads, nope), jnp.float32),
            pltpu.VMEM((rank // 128, rows * heads, 128), jnp.float32),
        ],
        compiler_params=pltpu.CompilerParams(vmem_limit_bytes=56 * MIB),
    )(chosen, pool, queries, key_up)


def combine(m_a, l_a, acc_a, m_b, l_b, acc_b):
    m = jnp.maximum(m_a, m_b)
    f_a, f_b = jnp.exp(m_a - m), jnp.exp(m_b - m)
    return m, l_a * f_a + l_b * f_b, acc_a * f_a + acc_b * f_b


def finish_kernel(
    scale, lengths, starts, pages_h, q_own_h, fresh_h, value_up_h, out_proj_h, out,
    pages_v, packed, q, fresh, value_up, out_proj, in_sem, wide, narrow, bias, s_s, w_s, acc, stats, sent, sent_st, got, got_st, own, own_st, held, share, parts, z_send, z_recv, x_send, x_recv, o_send, o_recv,
    p_send, p_recv, r_send, r_recv,
):
    z = lax.axis_index("head")
    xfer = lax.axis_index("xfer")
    x, y, core = xfer // 8, (xfer // 2) % 4, xfer % 2
    groups = 8
    rank = acc.shape[2]
    half_rows = acc.shape[1]
    loads = [
        pltpu.make_async_copy(src, dst, in_sem.at[i])
        for i, (src, dst) in enumerate(
            (
                (pages_h, pages_v),
                (q_own_h, q.at[pl.ds(z * 2, 2)]),
                (fresh_h, fresh),
                (value_up_h, value_up),
                (out_proj_h, out_proj),
            )
        )
    ]
    for c in loads:
        c.start()

    xs = [x] + [lax.rem(x + k, 4) for k in range(1, 4)]
    ys = [y] + [lax.rem(y + k, 4) for k in range(1, 4)]
    zs = [z] + [lax.rem(z + k, groups) for k in range(1, groups)]

    def near(dx, dy, flip):
        c = 1 - core if flip else core
        return ((xs[dx] * 4 + ys[dy]) * 2 + c, z)

    def along(k):
        return (xfer, zs[k])

    def owner_at(offset, sign):
        dx, dy, dc = offset
        return (xs[sign * dx % 4] * 4 + ys[sign * dy % 4]) * 2 + (1 - core if dc else core)

    barrier = pltpu.get_barrier_semaphore()
    peers = [along(k) for k in range(1, 8)] + [(owner_at(offset, 1), z) for offset in OFFSETS]
    for peer in peers:
        pl.semaphore_signal(barrier, inc=1, device_id=peer, device_id_type=MESH)
    pl.semaphore_wait(barrier, len(peers))

    def hop_of(way, j):
        block = zs[(1 - j) % groups] if way == 0 else zs[j - 1]
        part = q.at[block * 2 + way] if j == groups // 2 else q.at[pl.ds(block * 2, 2)]
        return pltpu.make_async_remote_copy(
            src_ref=part,
            dst_ref=part,
            send_sem=r_send.at[way, j],
            recv_sem=r_recv.at[way, j],
            device_id=along(1 if way == 0 else 7),
            device_id_type=MESH,
        )

    def page_to(i, offset):
        to = owner_at(offset, 1)
        return pltpu.make_async_remote_copy(
            src_ref=pages_v.at[to],
            dst_ref=packed.at[xfer],
            send_sem=p_send.at[i],
            recv_sem=p_recv.at[i],
            device_id=(to, z),
            device_id_type=MESH,
        )

    hops = [hop_of(way, j) for j in range(1, groups // 2 + 1) for way in (0, 1)]
    page_copies = [page_to(i, offset) for i, offset in enumerate(OFFSETS)]
    loads[1].wait()
    for c in hops[:2]:
        c.start()
    loads[0].wait()
    for c in page_copies:
        c.start()

    def z_copies(way, half, hop):
        to = along(1 if way == 0 else 7)
        return [
            pltpu.make_async_remote_copy(
                src_ref=src.at[way, half, hop],
                dst_ref=dst.at[way, half, hop],
                send_sem=z_send.at[way, half, hop, i],
                recv_sem=z_recv.at[way, half, hop, i],
                device_id=to,
                device_id_type=MESH,
            )
            for i, (src, dst) in enumerate(((sent, got), (sent_st, got_st)))
        ]

    def index_of(way, half, distance):
        d = zs[distance] if way == 0 else zs[groups - distance]
        return d * 2 + half

    odd = lax.broadcasted_iota(jnp.int32, (half_rows, 128), 1) % 2

    def arrived(way, half, hop):
        for c in z_copies(way, half, hop):
            c.wait_recv()
        st = jnp.tile(got_st[way, half, hop], (half_rows // 8, 1)).T
        return st[:, 0:1], st[:, 1:2], got[way, half, hop].astype(jnp.float32)

    started = hops + page_copies

    def send_on(way, half, hop):
        at = index_of(way, half, 4 - hop)
        mine = stats[at]
        if hop == (0 if way == half else 1):
            sent[way, half, hop] = acc[at].astype(jnp.bfloat16)
            sent_st[way, half, hop] = mine.T[0:8]
        else:
            m, l, total = combine(*arrived(way, half, hop - 1), mine[:, 0:1], mine[:, 1:2], acc[at])
            sent[way, half, hop] = total.astype(jnp.bfloat16)
            sent_st[way, half, hop] = jnp.where(odd == 0, m, l).T[0:8]
        for c in z_copies(way, half, hop):
            c.start()
            started.append(c)

    def take_fresh(half):
        s = (
            lax.dot_general(
                q[z * 2 + half], fresh[...], (((1,), (1,)), ((), ())), preferred_element_type=jnp.float32
            )
            * scale
        )
        row = lax.broadcasted_iota(jnp.int32, s.shape, 0) // 8
        col = lax.broadcasted_iota(jnp.int32, s.shape, 1)
        s = jnp.where((row // STEPS == col // STEPS) & (col <= row), s, LOW)
        m = jnp.max(s, axis=1, keepdims=True)
        w = jnp.exp(s - m)
        l = jnp.sum(w, axis=1, keepdims=True)
        more = jnp.dot(w.astype(jnp.bfloat16), fresh[:, :rank], preferred_element_type=jnp.float32)
        at = z * 2 + half
        mine = stats[at]
        m, l, total = combine(m, l, more, mine[:, 0:1], mine[:, 1:2], acc[at])
        own[half] = total
        own_st[half] = jnp.where(odd == 0, m, l)

    requests = lengths.shape[0] // 32
    page = packed.shape[1] * 128 // q.shape[2]
    keys = wide.shape[0]
    lane = lax.broadcasted_iota(jnp.int32, (1, keys), 1)

    def unpack(source, slot):
        to = pl.ds(pl.multiple_of(slot * page, page), page)
        for i in range(rank // 128):
            wide[to, i * 128 : (i + 1) * 128] = source[slot, i * page : (i + 1) * page, :]
        folded = source[slot, rank // 128 * page :, :]
        thin = narrow.shape[1]
        narrow[to] = jnp.concatenate([folded[:, :thin], folded[:, thin:]], axis=0)

    def hide():
        for r in range(requests):
            length, start = lengths[xfer * requests + r], starts[xfer * requests + r]
            at = (lane // page * groups + z - start) & (packed.shape[0] * groups - 1)
            seen = at * page + lane % page < length
            many = half_rows // requests
            bias[r * many : (r + 1) * many] = jnp.broadcast_to(jnp.where(seen, 0.0, LOW), (many, keys))

    def attend(distance):
        d = zs[distance]
        mine = q[pl.ds(d * 2, 2)].reshape(2 * half_rows, q.shape[2])
        top = None
        for b in range(0, keys, BLOCK):
            part = slice(b, b + BLOCK)
            s = lax.dot_general(
                mine[:, :rank], wide[part], (((1,), (1,)), ((), ())), preferred_element_type=jnp.float32
            )
            s += lax.dot_general(
                mine[:, rank:], narrow[part], (((1,), (1,)), ((), ())), preferred_element_type=jnp.float32
            )
            s = (s * scale).reshape(2, half_rows, BLOCK) + bias[:, part][None]
            s = s.reshape(2 * half_rows, BLOCK)
            s_s[:, part] = s
            most = jnp.max(s, axis=1, keepdims=True)
            top = most if top is None else jnp.maximum(top, most)
        top = jnp.maximum(top, FLOOR)
        total = None
        for b in range(0, keys, BLOCK):
            part = slice(b, b + BLOCK)
            w = jnp.exp(s_s[:, part] - top)
            w_s[:, part] = w.astype(jnp.bfloat16)
            more = jnp.sum(w, axis=1, keepdims=True)
            total = more if total is None else total + more
        summed = jnp.dot(w_s[...], wide[...], preferred_element_type=jnp.float32)
        acc[pl.ds(d * 2, 2)] = summed.reshape(2, half_rows, rank)
        both = jnp.where(lax.broadcasted_iota(jnp.int32, (2 * half_rows, 128), 1) % 2 == 0, top, total)
        stats[pl.ds(d * 2, 2)] = both.reshape(2, half_rows, 128)

    for j in range(1, groups // 2):
        for way in (0, 1):
            hops[(j - 1) * 2 + way].wait_recv()
            hops[j * 2 + way].start()
        if j == 1:
            hide()
    for c in hops[-2:]:
        c.wait_recv()
    unpack(pages_v, xfer)
    for c, offset in zip(page_copies, OFFSETS):
        c.wait_recv()
        unpack(packed, owner_at(offset, -1))
    attend(4)
    send_on(0, 0, 0)
    send_on(1, 1, 0)
    for hop in (1, 2, 3):
        attend(4 - hop)
        if hop == 1:
            send_on(0, 1, 1)
            attend(4 + hop)
            send_on(1, 0, 1)
            send_on(0, 0, 1)
            send_on(1, 1, 1)
        else:
            send_on(0, 1, hop)
            send_on(0, 0, hop)
            attend(4 + hop)
            send_on(1, 0, hop)
            send_on(1, 1, hop)
    attend(0)
    loads[2].wait()
    take_fresh(0)
    take_fresh(1)

    def spread(half, kind, a, b, block, to):
        return pltpu.make_async_remote_copy(
            src_ref=held.at[half, block],
            dst_ref=held.at[half, block],
            send_sem=x_send.at[half, kind, a, b],
            recv_sem=x_recv.at[half, kind, a, b],
            device_id=to,
            device_id_type=MESH,
        )

    def block_of(half, a, b):
        dx, dy = (a, b) if half == 0 else (b, a)
        return (xs[-dx % 4] * 4 + ys[-dy % 4]) * 2

    def to_first(half, k):
        return near(k, 0, False) if half == 0 else near(0, k, False)

    def to_second(half, k):
        return near(0, k, False) if half == 0 else near(k, 0, False)

    def start(copy):
        copy.start()
        started.append(copy)

    def pass_second(half, a):
        for k in range(1, 4):
            start(spread(half, 1, a, k, block_of(half, a, 0) + core, to_second(half, k)))

    def pass_core(half, a, b):
        start(spread(half, 2, a, b, block_of(half, a, b) + core, near(0, 0, True)))

    loads[3].wait()
    for half in (1, 0):
        m, l, total = own_st[half][:, 0:1], own_st[half][:, 1:2], own[half]
        for way in (0, 1):
            m, l, total = combine(m, l, total, *arrived(way, half, 3))
        latent = (total / l).astype(jnp.bfloat16)
        heads = half_rows // fresh.shape[0]
        for h in range(heads):
            full = jnp.dot(latent, value_up[half * heads + h], preferred_element_type=jnp.float32)
            picked = full.reshape(fresh.shape[0], heads, -1)[:, h, :]
            width = picked.shape[1]
            held[half, xfer, :, h * width : (h + 1) * width] = picked.astype(jnp.bfloat16)
        for k in range(1, 4):
            start(spread(half, 0, 0, k, xfer, to_first(half, k)))
        pass_second(half, 0)
        pass_core(half, 0, 0)
    for a in range(1, 4):
        for half in (1, 0):
            spread(half, 0, 0, a, xfer, near(0, 0, True)).wait_recv()
            pass_second(half, a)
            pass_core(half, a, 0)
    for a in range(4):
        for b in range(1, 4):
            for half in (1, 0):
                spread(half, 1, a, b, xfer, near(0, 0, True)).wait_recv()
                pass_core(half, a, b)
    for half in (1, 0):
        for a in range(4):
            for b in range(4):
                spread(half, 2, a, b, xfer, near(0, 0, True)).wait_recv()

    loads[4].wait()
    depth = held.shape[3]
    total = None
    for half in (0, 1):
        left = held[half].reshape(-1, depth)
        right = out_proj[:, half * depth : (half + 1) * depth]
        piece = lax.dot_general(left, right, (((1,), (1,)), ((), ())), preferred_element_type=jnp.float32)
        total = piece if total is None else total + piece
    parts[...] = total.reshape(parts.shape)

    def final(k):
        return pltpu.make_async_remote_copy(
            src_ref=share.at[0, k],
            dst_ref=share.at[1, k],
            send_sem=o_send.at[k],
            recv_sem=o_recv.at[k],
            device_id=along(k),
            device_id_type=MESH,
        )

    for k in (4, 3, 5, 2, 6, 1, 7):
        share[0, k] = parts[zs[k]].astype(jnp.bfloat16)
        start(final(k))
    done = parts[z]
    for k in (1, 7, 2, 6, 3, 5, 4):
        final(k).wait_recv()
        done += share[1, k].astype(jnp.float32)
    out[...] = done.astype(jnp.bfloat16)
    for c in started:
        c.wait_send()


def finish(lengths, starts, pages, q_own, fresh, value_up, out_proj, owners, groups, scale):
    vmem = pl.BlockSpec(memory_space=pltpu.VMEM)
    operands = (pages, q_own, fresh, value_up, out_proj)
    smem = pl.BlockSpec(memory_space=pltpu.SMEM)
    rows = fresh.shape[0]
    half_rows, latent = q_own.shape[1:]
    rank = value_up.shape[1]
    tokens = pages.shape[0] * pages.shape[1] * 128 // latent
    width, depth = out_proj.shape
    piece = owners * rows // groups
    dma = pltpu.SemaphoreType.DMA
    return pl.pallas_call(
        functools.partial(finish_kernel, scale),
        in_specs=[smem, smem] + [pl.BlockSpec(memory_space=pl.ANY)] * 5,
        out_specs=vmem,
        out_shape=jax.ShapeDtypeStruct((piece, width), jnp.bfloat16),
        scratch_shapes=[
            pltpu.VMEM(pages.shape, pages.dtype),
            pltpu.VMEM(pages.shape, pages.dtype),
            pltpu.VMEM((2 * groups, half_rows, latent), q_own.dtype),
            *(pltpu.VMEM(a.shape, a.dtype) for a in operands[2:]),
            dma((5,)),
            pltpu.VMEM((tokens, rank), jnp.bfloat16),
            pltpu.VMEM((tokens, latent - rank), jnp.bfloat16),
            pltpu.VMEM((half_rows, tokens), jnp.float32),
            pltpu.VMEM((2 * half_rows, tokens), jnp.float32),
            pltpu.VMEM((2 * half_rows, tokens), jnp.bfloat16),
            pltpu.VMEM((2 * groups, half_rows, rank), jnp.float32),
            pltpu.VMEM((2 * groups, half_rows, 128), jnp.float32),
            pltpu.VMEM((2, 2, 4, half_rows, rank), jnp.bfloat16),
            pltpu.VMEM((2, 2, 4, 8, 128), jnp.float32),
            pltpu.VMEM((2, 2, 4, half_rows, rank), jnp.bfloat16),
            pltpu.VMEM((2, 2, 4, 8, 128), jnp.float32),
            pltpu.VMEM((2, half_rows, rank), jnp.float32),
            pltpu.VMEM((2, half_rows, 128), jnp.float32),
            pltpu.VMEM((2, owners, rows, depth // 2), jnp.bfloat16),
            pltpu.VMEM((2, groups, piece, width), jnp.bfloat16),
            pltpu.VMEM((groups, piece, width), jnp.float32),
            dma((2, 2, 4, 2)),
            dma((2, 2, 4, 2)),
            dma((2, 3, 4, 4)),
            dma((2, 3, 4, 4)),
            dma((groups,)),
            dma((groups,)),
            dma((owners,)),
            dma((owners,)),
            dma((2, 8)),
            dma((2, 8)),
        ],
        compiler_params=pltpu.CompilerParams(
            collective_id=0, has_side_effects=True, vmem_limit_bytes=56 * MIB
        ),
    )(lengths, starts, *operands)


def body(
    kv_pool, lengths, start_device, page_table, queries, new_latent, key_up, value_up, out_proj
):
    owners = lax.axis_size("xfer")
    groups = lax.axis_size("head")
    latent = kv_pool.shape[2]
    row_count, heads = queries.shape[:2]
    score_scale = queries.shape[2] ** (-0.5)
    device = lax.axis_index("xfer") * groups + lax.axis_index("head")
    nth = (device - start_device) % (owners * groups)
    here = nth * kv_pool.shape[1] < lengths
    column = jnp.arange(page_table.shape[1], dtype=jnp.int32)
    picked = (column[None, :] == nth[:, None]) & here[:, None]
    chosen = jnp.where(picked, page_table, 0).reshape(owners, -1, page_table.shape[1]).sum(axis=(1, 2))
    pages, q_own = prepare(chosen, kv_pool, queries, key_up)
    q_own = q_own.reshape(2, row_count * heads // 2, latent)
    return finish(
        lengths, start_device, pages, q_own, new_latent, value_up, out_proj.T, owners, groups, score_scale
    )


def solution(mesh):
    in_specs = (
        P(("xfer", "head"), None, None),
        P(),
        P(),
        P(),
        P("xfer", "head", None),
        P("xfer", None),
        P("head", None, None),
        P("head", None, None),
        P("head", "xfer"),
    )
    out_specs = P("head", "xfer")
    return jax.shard_map(body, mesh=mesh, in_specs=in_specs, out_specs=out_specs, check_vma=False)
```
